32 devices in a mesh: dp: 8 (over y, x, core), mp: 4 (over z).
Axes of the slice: x: 2, y: 2, z: 4, core: 2. Of those that a mesh axis runs over, the one named last changes fastest.
Arguments:
- tokens: bfloat16 [6272, 768], P('dp', 'mp'), may hold values from -6 to 6
- norm_params: float32 [4, 768], replicated, may hold values from -0.3 to 1.5
- w_qkv: float32 [3, 768, 768], P(None, 'dp', 'mp'), may hold values from -0.21875 to 0.21875
- w_proj: float32 [768, 768], P('mp', 'dp'), may hold values from -2.5 to 2.5
- phi: float32 [768, 16], replicated, may hold values from -0.109375 to 0.109375
- w_in: float32 [16, 768, 3072], P('dp', None, 'mp'), may hold values from -3.5 to 3.5
- w_out: float32 [16, 3072, 768], P('dp', 'mp'), may hold values from -0.4375 to 0.4375
- cotangent: bfloat16 [6272, 768], P('dp', 'mp'), may hold values from -6 to 6
Outputs:
- output: float32 [6272, 768], P('dp', 'mp')
- input_grad: float32 [6272, 768], P('dp', 'mp')
- qkv_grad: float32 [3, 768, 768], P(None, 'dp', 'mp')
- proj_grad: float32 [768, 768], P('mp', 'dp')
- expert_in_grad: float32 [16, 768, 3072], P('dp', None, 'mp')
- expert_out_grad: float32 [16, 3072, 768], P('dp', 'mp')
- phi_grad: float32 [768, 16], replicated
- norm_grad: float32 [4, 768], replicated
The draws below stay inside these ranges and needn't reach their ends.
All inputs are finite; a program needn't handle non-finite values.
Results may differ from the reference program's by a relative error of at most 0.017.
The reference program's roundings to bfloat16 on the way count: a program that leaves them out, or rounds other values in their place, can miss the bound.
Values may be sent and summed in bfloat16 or wider, within the bound.
A program may use at most 128 MiB of HBM per device.

```python
import math
import jax
import jax.numpy as jnp
from jax import lax

D = 768
HEADS = 12
HEAD_DIM = 64
FF = 3072
SEQ = 196
IMAGES = 32
TOKENS = 6272
EXPERTS = 16


def draw_norm_params(key, part):
    gain_key = jax.random.fold_in(key, 11)
    shift_key = jax.random.fold_in(key, 23)
    gain_rows = jax.random.uniform(gain_key, (2, D), jnp.float32, 0.5, 1.5)
    shift_rows = 0.1 * jax.random.truncated_normal(shift_key, -3.0, 3.0, (2, D), jnp.float32)
    return jnp.stack([gain_rows[0], shift_rows[0], gain_rows[1], shift_rows[1]])


def block_levels(key, extent, shards, smallest, high):
    def one(dim, shards_of):
        steps = jax.random.uniform(jax.random.fold_in(jax.random.fold_in(key, 6), dim), (shards_of,), jnp.float32, smallest / len(shards), high / len(shards))
        return jnp.repeat(jnp.exp(steps), extent[dim] // shards_of).reshape((-1,) + (1,) * (len(extent) - dim - 1))

    factor_of = one(*shards[0])
    for cut in shards[1:]:
        factor_of = factor_of * one(*cut)
    return factor_of


def bell_draw(rng, extent, width, bound, pieces=(), held_as=jnp.bfloat16):
    array = width * jax.random.normal(rng, extent, jnp.float32)
    if pieces:
        array = array * block_levels(rng, extent, pieces, -0.22, 0.18)
    return jnp.clip(array, -bound, bound).astype(held_as)


def setup_inputs(seed: int = 0) -> dict:
    arg_keys = jax.random.split(jax.random.key(seed), 9)
    tokens = bell_draw(arg_keys[0], (TOKENS, D), 1.0, 6.0, ((0, 8), (1, 4)))
    norm_params = draw_norm_params(jax.random.fold_in(arg_keys[8], 71), 0)
    w_qkv = bell_draw(arg_keys[2], (3, D, D), D ** -0.5, 0.21875, ((1, 8), (2, 4)), jnp.float32)
    w_proj = bell_draw(arg_keys[3], (D, D), (max(D // 128, 1)) ** -0.5, 2.5, ((0, 4), (1, 8)), jnp.float32)
    phi = bell_draw(arg_keys[4], (D, EXPERTS), (4 * D) ** -0.5, 0.109375, (), jnp.float32)
    w_in = bell_draw(arg_keys[5], (EXPERTS, D, FF), (max(D // SEQ, 1)) ** -0.5, 3.5, ((0, 8), (2, 4)), jnp.float32)
    w_out = bell_draw(arg_keys[6], (EXPERTS, FF, D), (max(FF // EXPERTS, 1)) ** -0.5, 0.4375, ((0, 8), (1, 4)), jnp.float32)
    cotangent = bell_draw(arg_keys[7], (TOKENS, D), 1.0, 6.0, ((0, 8), (1, 4)))
    return dict(tokens=tokens, norm_params=norm_params, w_qkv=w_qkv, w_proj=w_proj, phi=phi, w_in=w_in, w_out=w_out, cotangent=cotangent)


@jax.custom_vjp
def low(v):
    return lax.optimization_barrier(v.astype(jnp.bfloat16)).astype(jnp.float32)

@jax.custom_vjp
def low_back(v):
    return v

def low_keep(v):
    return (low(v), None)

def low_pass(kept, grad):
    return (grad,)

def back_keep(v):
    return (v, None)

def back_low(kept, grad):
    return (low(grad),)
low.defvjp(low_keep, low_pass)
low_back.defvjp(back_keep, back_low)
EPSILON = 1e-06
HIGHEST = lax.Precision.HIGHEST

def layer_norm(values_in, gain_row, shift_row):
    row_mean = lax.optimization_barrier(jnp.mean(values_in, axis=-1, keepdims=True))
    centered = values_in - row_mean
    row_var = lax.optimization_barrier(jnp.mean(centered * centered, axis=-1, keepdims=True))
    return centered * lax.rsqrt(row_var + EPSILON) * gain_row + shift_row

def attend(triple):
    query_rows, key_rows, value_rows = triple
    scale = 1.0 / math.sqrt(HEAD_DIM)
    scores = low_back(jnp.einsum('hqd,hkd->hqk', query_rows, key_rows, precision=HIGHEST) * scale)
    attn_probs = low(jax.nn.softmax(scores, axis=-1))
    return low_back(low(jnp.einsum('hqk,hkd->hqd', attn_probs, value_rows, precision=HIGHEST)))

def forward(inputs_f, norm_params, w_qkv, w_proj, phi, w_in, w_out):
    first = low(layer_norm(inputs_f, norm_params[0], norm_params[1]))
    projected = jnp.einsum('td,cde->cte', first, low(w_qkv), precision=HIGHEST)
    projected = low_back(low(projected))
    projected = projected.reshape(3, IMAGES, SEQ, HEADS, HEAD_DIM).transpose(0, 1, 3, 2, 4)
    attended = lax.map(jax.checkpoint(attend), (projected[0], projected[1], projected[2]))
    attended = attended.transpose(0, 2, 1, 3).reshape(TOKENS, D)
    branch = low_back(jnp.dot(attended, low(w_proj), precision=HIGHEST))
    residual = inputs_f + branch
    second = low(layer_norm(residual, norm_params[2], norm_params[3]))
    logits = low_back(jnp.dot(second, low(phi), precision=HIGHEST)).reshape(IMAGES, SEQ, EXPERTS)
    dispatch = low(jax.nn.softmax(logits, axis=1))
    combine = low(jax.nn.softmax(logits, axis=2))
    second_img = second.reshape(IMAGES, SEQ, D)
    slot_rows = low_back(low(jnp.einsum('bse,bsd->bed', dispatch, second_img, precision=HIGHEST)))
    pre_act = low_back(jnp.einsum('bed,edf->bef', slot_rows, low(w_in), precision=HIGHEST))
    hidden = low(jax.nn.gelu(pre_act, approximate=False))
    results = low_back(low(jnp.einsum('bef,efd->bed', hidden, low(w_out), precision=HIGHEST)))
    moe_mixed = low_back(jnp.einsum('bse,bed->bsd', combine, results, precision=HIGHEST))
    return residual + moe_mixed.reshape(TOKENS, D)

def reference(tokens, norm_params, w_qkv, w_proj, phi, w_in, w_out, cotangent):
    inputs_f = tokens.astype(jnp.float32)
    output, backward = jax.vjp(forward, inputs_f, norm_params, w_qkv, w_proj, phi, w_in, w_out)
    grads = backward(cotangent.astype(jnp.float32))
    return (output, grads[0], grads[2], grads[3], grads[5], grads[6], grads[4], grads[1])
```

```python
import functools
import math

import jax
import jax.numpy as jnp
from jax import lax
from jax.experimental import pallas as pl
from jax.experimental.pallas import tpu as pltpu
from jax.sharding import PartitionSpec as P

HEAD_DIM = 64
SEQ = 196
EPSILON = 1e-06
MESH = pl.DeviceIdType.MESH
BF = jnp.bfloat16
F32 = jnp.float32
NEG = -1e30


def nn(a, b):
    return lax.dot_general(a, b, (((1,), (0,)), ((), ())), preferred_element_type=F32)


def nt(a, b):
    return lax.dot_general(a, b, (((1,), (1,)), ((), ())), preferred_element_type=F32)


def tn(a, b):
    return lax.dot_general(a, b, (((0,), (0,)), ((), ())), preferred_element_type=F32)


def each(low, high, body):
    if high - low <= 8:
        for i in range(low, high):
            body(i)
    else:

        def step(i, carry):
            body(i)
            return carry

        lax.fori_loop(low, high, step, 0)


def select_rows(rows, cols, source):
    row = lax.broadcasted_iota(jnp.int32, (rows, cols), 0)
    col = lax.broadcasted_iota(jnp.int32, (rows, cols), 1)
    return jnp.where(col == source(row), 1.0, 0.0).astype(BF)


def normalize(values):
    mean = jnp.mean(values, axis=-1, keepdims=True)
    centered = values - mean
    var = jnp.mean(centered * centered, axis=-1, keepdims=True)
    inv = lax.rsqrt(var + EPSILON)
    return centered * inv, inv


def norm_backward(grad, gain, normed, inv):
    scaled = grad * gain
    first = jnp.mean(scaled, axis=-1, keepdims=True)
    second = jnp.mean(scaled * normed, axis=-1, keepdims=True)
    return inv * (scaled - first - normed * second)


class Sizes:
    def __init__(self, mesh, tokens, w_qkv, phi, w_in):
        self.DP, self.MP = mesh.shape["dp"], mesh.shape["mp"]
        self.D, self.E = phi.shape
        self.CW = tokens.shape[1]
        self.RB = w_qkv.shape[1]
        self.QW = 3 * self.CW
        self.HL = self.CW // HEAD_DIM
        self.EPD = w_in.shape[0]
        self.F = w_in.shape[2]
        self.IN = 2 if self.DP % 2 == 0 else 1
        self.NX = self.DP // self.IN
        self.SP = (SEQ + 15) // 16 * 16
        self.ROWS = tokens.shape[0]
        self.TR = (2 * self.EPD + 7) // 8 * 8
        self.SUM = self.E + 8
        self.own_weights = self.RB % 16 == 0 and self.DP <= 8


def scratch_of(z):
    dma = pltpu.SemaphoreType.DMA
    v = pltpu.VMEM
    DP, MP, D, CW, RB, QW, SP, NX, IN = z.DP, z.MP, z.D, z.CW, z.RB, z.QW, z.SP, z.NX, z.IN
    items = dict(
        tsend=v((MP, SP, CW), BF), tin=v((MP, SP, CW), BF),
        csend=v((MP, SP, CW), BF), cin=v((MP, SP, CW), BF),
        osend=v((MP, SP, CW), BF), oin=v((MP, SP, CW), BF),
        isend=v((MP, SP, CW), BF), iin=v((MP, SP, CW), BF),
        wf_in=v((z.EPD, D, z.F), F32), wf_out=v((z.EPD, z.F, D), F32),
        wb_in=v((z.EPD, D, z.F), BF), wb_out=v((z.EPD, z.F, D), BF),
        h1=v((SP, D), BF), qkv=v((MP, SP, QW), BF), probs=v((MP, z.HL, SP, SP), F32),
        att=v((MP, SP, CW), BF), dqkv=v((SP, QW), BF), datt=v((MP, SP, CW), BF),
        resid=v((SP, D), F32), dresid=v((SP, D), F32), dh1=v((SP, D), F32),
        slot_out=v((DP * z.TR, D), F32), slot_in=v((DP * z.TR, D), F32),
        slot_all=v((MP, 2 * z.EPD * DP, D), BF),
        part=v((MP, 2 * z.EPD * DP, D), F32), psend=v((MP, 2 * z.EPD * DP, D), BF),
        pin=v((MP, 2 * z.EPD * DP, D), BF),
        back_out=v((DP * z.TR, D), F32), back_in=v((DP * z.TR, D), F32),
    )
    sems = dict(
        tok=(2, MP), cot=(2, MP), outs=(2, MP), ings=(2, MP), hbm=(2,),
        dp1=(2, DP), mp1=(2, MP), mp2=(2, MP), dp2=(2, DP),
    )
    if z.own_weights:
        items.update(
            wall=v((MP, NX, IN, RB, QW), BF), wpall=v((MP, NX, IN, RB, CW), BF),
            gq=v((MP, NX, IN, RB, QW), BF), gp=v((MP, NX, IN, RB, CW), BF),
            cq=v((MP, NX, RB, QW), BF), cp=v((MP, NX, RB, CW), BF),
            xq=v((MP, NX, RB, QW), BF), xp=v((NX, MP, RB, CW), BF),
            yq=v((MP, NX, RB, QW), BF), yp=v((NX, MP, RB, CW), BF),
            zq=v((MP, RB, QW), BF), zp=v((MP, RB, CW), BF),
            rq=v((MP, RB, QW), BF), rp=v((MP, RB, CW), BF),
            sums_p=v((MP, RB, CW), F32),
            sa=v((z.SUM, D), F32), sb=v((IN, z.SUM, D), F32), sc=v((NX, z.SUM, D), F32),
            sd=v((MP, z.SUM, D), F32),
            ta=v((8, D), F32), tb=v((IN, 8, D), F32), tc=v((NX, 8, D), F32), td=v((MP, 8, D), F32),
        )
        sems.update(
            wz=(2, MP), wx=(2, MP, NX), wc=(2, MP), vz=(2, MP), vx=(2, NX), vc=(2,),
            gc=(2, MP), gx=(2, MP, NX), gz=(2, MP), hc=(2,), hx=(2, NX), hz=(2, MP),
            s1=(2,), s2=(2, NX), s3=(2, MP), t1=(2,), t2=(2, NX), t3=(2, MP),
        )
    names, shapes = [], []
    for name, shape in items.items():
        names.append(name)
        shapes.append(shape)
    for name, shape in sems.items():
        names.append("m_" + name)
        shapes.append(dma(shape))
    return names, shapes


class Refs:
    pass


def block_kernel(z, in_names, out_names, names, *refs):
    r = Refs()
    for name, ref in zip(in_names + out_names + names, refs):
        setattr(r, name, ref)
    DP, MP, D, CW, RB, QW, SP = z.DP, z.MP, z.D, z.CW, z.RB, z.QW, z.SP
    NX, IN, E, EPD, TR = z.NX, z.IN, z.E, z.EPD, z.TR
    KE = 2 * EPD
    dp, mp = lax.axis_index("dp"), lax.axis_index("mp")
    xy, co = dp // IN, lax.rem(dp, IN)
    sends = []

    def remote(src, dst, sem, s_at, r_at, device):
        return pltpu.make_async_remote_copy(
            src_ref=src, dst_ref=dst, send_sem=sem.at[(0,) + s_at], recv_sem=sem.at[(1,) + r_at],
            device_id=device, device_id_type=MESH,
        )

    def mp_at(k):
        return lax.rem(mp + k, MP)

    def dp_at(k):
        return lax.rem(dp + k, DP)

    def xy_at(k):
        return lax.rem(xy + k, NX)

    def to_mp(k):
        return (dp, mp_at(k))

    def to_xy(k):
        return (xy_at(k) * IN + co, mp)

    def to_core():
        return (xy * IN + 1 - co, mp)

    barrier = pltpu.get_barrier_semaphore()
    for k in range(1, MP):
        pl.semaphore_signal(barrier, inc=1, device_id=to_mp(k), device_id_type=MESH)
    each(1, DP, lambda k: pl.semaphore_signal(barrier, inc=1, device_id=(dp_at(k), mp), device_id_type=MESH))

    load_in = pltpu.make_async_copy(r.w_in, r.wf_in, r.m_hbm.at[0])
    load_out = pltpu.make_async_copy(r.w_out, r.wf_out, r.m_hbm.at[1])
    load_in.start()
    load_out.start()

    if z.own_weights:
        r.wall[mp, xy, co] = jnp.concatenate([r.w_qkv[c].astype(BF) for c in range(3)], axis=1)
        r.wpall[mp, xy, co] = r.w_proj[...].T.astype(BF)

    def to_images(source, target):
        target[...] = jnp.zeros((MP, SP, CW), BF)
        for i in range(MP):
            target[i, 0:SEQ, :] = source[pl.ds(SEQ * i, SEQ), :]

    to_images(r.tokens, r.tsend)
    pl.semaphore_wait(barrier, MP - 1 + DP - 1)

    def swap(src, dst, sem, k):
        return remote(src.at[mp_at(k)], dst.at[mp], sem, (k,), (MP - k,), to_mp(k))

    def swap_start(src, dst, sem):
        for k in range(1, MP):
            swap(src, dst, sem, k).start()
        dst[mp] = src[mp]
        sends.extend((lambda k=k: swap(src, dst, sem, k).wait_send()) for k in range(1, MP))

    def swap_wait(src, dst, sem):
        for k in range(1, MP):
            remote(src.at[mp_at(k)], dst.at[mp_at(k)], sem, (k,), (k,), to_mp(k)).wait_recv()

    def wz(k):
        block = r.wall.at[mp, xy, co]
        return remote(block, block, r.m_wz, (k,), (MP - k,), to_mp(k))

    def wz_wait(k):
        block = r.wall.at[mp_at(k), xy, co]
        remote(block, block, r.m_wz, (k,), (k,), to_mp(k)).wait_recv()

    def wx(j, k):
        block = r.wall.at[mp_at(j), xy, co]
        return remote(block, block, r.m_wx, (j, k), (j, NX - k), to_xy(k))

    def wx_wait(j, k):
        block = r.wall.at[mp_at(j), xy_at(k), co]
        remote(block, block, r.m_wx, (j, k), (j, k), to_xy(k)).wait_recv()

    def wc(j):
        block = r.wall.at[mp_at(j), :, co]
        return remote(block, block, r.m_wc, (j,), (j,), to_core())

    def wc_wait(j):
        block = r.wall.at[mp_at(j), :, 1 - co]
        remote(block, block, r.m_wc, (j,), (j,), to_core()).wait_recv()

    def vz(k):
        block = r.wpall.at[mp, xy, co]
        return remote(block, block, r.m_vz, (k,), (MP - k,), to_mp(k))

    def vz_wait(k):
        block = r.wpall.at[mp_at(k), xy, co]
        remote(block, block, r.m_vz, (k,), (k,), to_mp(k)).wait_recv()

    def vx(k):
        block = r.wpall.at[:, xy, co]
        return remote(block, block, r.m_vx, (k,), (NX - k,), to_xy(k))

    def vx_wait(k):
        block = r.wpall.at[:, xy_at(k), co]
        remote(block, block, r.m_vx, (k,), (k,), to_xy(k)).wait_recv()

    def vc():
        block = r.wpall.at[:, :, co]
        return remote(block, block, r.m_vc, (), (), to_core())

    def vc_wait():
        block = r.wpall.at[:, :, 1 - co]
        remote(block, block, r.m_vc, (), (), to_core()).wait_recv()

    if z.own_weights:
        for k in range(1, MP):
            wz(k).start()
        for k in range(1, NX):
            wx(0, k).start()
    swap_start(r.tsend, r.tin, r.m_tok)
    if z.own_weights:
        for k in range(1, MP):
            vz(k).start()
    to_images(r.cotangent, r.csend)
    swap_start(r.csend, r.cin, r.m_cot)

    load_in.wait()
    r.wb_in[...] = r.wf_in[...].astype(BF)
    if z.own_weights:
        for j in range(1, MP):
            wz_wait(j)
            for k in range(1, NX):
                wx(j, k).start()
    load_out.wait()
    r.wb_out[...] = r.wf_out[...].astype(BF)

    swap_wait(r.tsend, r.tin, r.m_tok)
    gain1, shift1 = r.norm_params[0:1, :], r.norm_params[1:2, :]
    gain2, shift2 = r.norm_params[2:3, :], r.norm_params[3:4, :]

    def own_image(ref):
        return jnp.concatenate([ref[i] for i in range(MP)], axis=1).astype(F32)

    normed1, _ = normalize(own_image(r.tin))
    r.h1[...] = (normed1 * gain1 + shift1).astype(BF)

    scale = 1.0 / math.sqrt(HEAD_DIM)
    key_ok = lax.broadcasted_iota(jnp.int32, (1, SP), 1) < SEQ

    def weight(m):
        return r.wall[m].reshape(D, QW) if z.own_weights else r.wall[m]

    def proj_weight(m):
        return r.wpall[m].reshape(D, CW) if z.own_weights else r.wpall[m]

    if z.own_weights:
        for k in range(1, NX):
            wx_wait(0, k)
        wc(0).start()
        wc_wait(0)

    def heads_forward(j, carry):
        m = mp_at(j)
        qkv = nn(r.h1[...], weight(m)).astype(BF)
        r.qkv[m] = qkv
        if z.own_weights:

            @pl.when(j < MP - 1)
            def _():
                for k in range(1, NX):
                    wx_wait(j + 1, k)
                wc(j + 1).start()

            @pl.when(j == 0)
            def _():
                for k in range(1, MP):
                    vz_wait(k)
                for k in range(1, NX):
                    vx(k).start()

            @pl.when(j == MP - 1)
            def _():
                for k in range(1, NX):
                    vx_wait(k)
                vc().start()

        attended = []
        for h in range(z.HL):
            query, key, value = (
                qkv[:, c * CW + h * HEAD_DIM : c * CW + (h + 1) * HEAD_DIM] for c in range(3)
            )
            scores = jnp.where(key_ok, nt(query, key) * scale, NEG)
            top = jnp.max(scores, axis=-1, keepdims=True)
            grown = jnp.exp(scores - top)
            probs = grown / jnp.sum(grown, axis=-1, keepdims=True)
            r.probs[m, h] = probs
            attended.append(nn(probs.astype(BF), value))
        r.att[m] = jnp.concatenate(attended, axis=1).astype(BF)
        if z.own_weights:

            @pl.when(j < MP - 1)
            def _():
                wc_wait(j + 1)

        return carry

    lax.fori_loop(0, MP, heads_forward, 0)
    if z.own_weights:
        vc_wait()

    resid = own_image(r.tin)
    for m in range(MP):
        resid = resid + nt(r.att[m], proj_weight(m))
    r.resid[...] = resid
    normed2, inv2 = normalize(resid)
    h2 = (normed2 * gain2 + shift2).astype(BF)
    phi_low = r.phi[...].astype(BF)
    logits = nn(h2, phi_low)
    token_ok = lax.broadcasted_iota(jnp.int32, (SP, 1), 0) < SEQ
    masked = jnp.where(token_ok, logits, NEG)
    grown = jnp.exp(masked - jnp.max(masked, axis=0, keepdims=True))
    dispatch = grown / jnp.sum(grown, axis=0, keepdims=True)
    grown = jnp.exp(logits - jnp.max(logits, axis=1, keepdims=True))
    combine = grown / jnp.sum(grown, axis=1, keepdims=True)
    dispatch_low, combine_low = dispatch.astype(BF), combine.astype(BF)
    swap_wait(r.csend, r.cin, r.m_cot)
    grad = jnp.concatenate([r.cin[i] for i in range(MP)], axis=1)
    slots = tn(dispatch_low, h2).astype(BF)
    dresults = tn(combine_low, grad).astype(BF)

    def out_row(row):
        d, q = row // TR, row % TR
        return jnp.where(q < KE, (q // EPD) * E + d * EPD + q % EPD, -1)

    r.slot_out[...] = nn(select_rows(DP * TR, 2 * E, out_row), jnp.concatenate([slots, dresults], axis=0))

    def rows_of(ref, d):
        return ref.at[pl.ds(pl.multiple_of(d * TR, 8), TR)]

    def dp_swap(src, dst, sem):
        def copy(k):
            return remote(rows_of(src, dp_at(k)), rows_of(dst, dp), sem, (k,), (DP - k,), (dp_at(k), mp))

        each(1, DP, lambda k: copy(k).start())
        here = pl.ds(pl.multiple_of(dp * TR, 8), TR)
        dst[here, :] = src[here, :]
        sends.append(lambda: each(1, DP, lambda k: copy(k).wait_send()))

        def arrive(k):
            remote(rows_of(src, dp_at(k)), rows_of(dst, dp_at(k)), sem, (k,), (k,), (dp_at(k), mp)).wait_recv()

        each(1, DP, arrive)

    dp_swap(r.slot_out, r.slot_in, r.m_dp1)
    gather_rows = select_rows(KE * DP, DP * TR, lambda row: (row % DP) * TR + row // DP)
    r.slot_all[mp] = nn(gather_rows, r.slot_in[...].astype(BF)).astype(BF)

    def slot_copy(k):
        return remote(r.slot_all.at[mp], r.slot_all.at[mp], r.m_mp1, (k,), (MP - k,), to_mp(k))

    for k in range(1, MP):
        slot_copy(k).start()
        sends.append(lambda k=k: slot_copy(k).wait_send())
    for k in range(1, MP):
        block = r.slot_all.at[mp_at(k)]
        remote(block, block, r.m_mp1, (k,), (k,), to_mp(k)).wait_recv()

    everything = [r.slot_all[m].astype(F32) for m in range(MP)]

    def expert_rows(q):
        return jnp.concatenate([one[q * DP : (q + 1) * DP] for one in everything], axis=0).astype(BF)

    for e in range(EPD):
        slots_e, dresults_e = expert_rows(e), expert_rows(EPD + e)
        pre = nn(slots_e, r.wb_in[e])
        cdf = 0.5 * (1.0 + lax.erf(pre * (1.0 / math.sqrt(2.0))))
        hidden = (pre * cdf).astype(BF)
        results_e = nn(hidden, r.wb_out[e])
        slope = cdf + pre * jnp.exp(-0.5 * pre * pre) * (1.0 / math.sqrt(2.0 * math.pi))
        dpre = (nt(dresults_e, r.wb_out[e]) * slope).astype(BF)
        dslots_e = nt(dpre, r.wb_in[e])
        r.slots[e], r.dresults[e], r.hidden[e], r.dpre[e] = slots_e, dresults_e, hidden, dpre
        for m in range(MP):
            r.part[m, e * DP : (e + 1) * DP, :] = results_e[m * DP : (m + 1) * DP]
            r.part[m, (EPD + e) * DP : (EPD + e + 1) * DP, :] = dslots_e[m * DP : (m + 1) * DP]

    r.psend[...] = r.part[...].astype(BF)

    def part_copy(k):
        return remote(r.psend.at[mp_at(k)], r.pin.at[MP - k], r.m_mp2, (k,), (MP - k,), to_mp(k))

    for k in range(1, MP):
        part_copy(k).start()
        sends.append(lambda k=k: part_copy(k).wait_send())
    total = r.part[mp]
    for k in range(1, MP):
        remote(r.psend.at[mp_at(k)], r.pin.at[k], r.m_mp2, (k,), (k,), to_mp(k)).wait_recv()
        total = total + r.pin[k].astype(F32)

    def back_row(row):
        d, q = row // TR, row % TR
        return jnp.where(q < KE, q * DP + d, -1)

    r.back_out[...] = nn(select_rows(DP * TR, KE * DP, back_row), total.astype(BF))
    dp_swap(r.back_out, r.back_in, r.m_dp2)

    def result_row(row):
        kind, e = row // E, row % E
        return (e // EPD) * TR + kind * EPD + e % EPD

    both = nn(select_rows(2 * E, DP * TR, result_row), r.back_in[...].astype(BF)).astype(BF)
    results, dslots = both[:E], both[E:]

    output = r.resid[...] + nn(combine_low, results)
    for m in range(MP):
        r.osend[m] = output[:, m * CW : (m + 1) * CW].astype(BF)
    swap_start(r.osend, r.oin, r.m_outs)
    dcombine, ddispatch = nt(grad, results), nt(h2, dslots)
    dlogits = dispatch * (ddispatch - jnp.sum(dispatch * ddispatch, axis=0, keepdims=True))
    dlogits = dlogits + combine * (dcombine - jnp.sum(combine * dcombine, axis=1, keepdims=True))
    dlogits = dlogits.astype(BF)
    dh2 = nn(dispatch_low, dslots) + nt(dlogits, phi_low)
    gain_part2 = jnp.sum(dh2 * normed2, axis=0, keepdims=True)
    shift_part2 = jnp.sum(dh2, axis=0, keepdims=True)
    dresid = grad.astype(F32) + norm_backward(dh2, gain2, normed2, inv2)
    r.dresid[...] = dresid
    dbranch = dresid.astype(BF)
    for m in range(MP):
        r.datt[m] = nn(dbranch, proj_weight(m)).astype(BF)
        piece = tn(dbranch, r.att[m])
        if z.own_weights:
            r.gp[m] = piece.astype(BF).reshape(NX, IN, RB, CW)
        else:
            r.gp[m] = piece.astype(BF)

    def hc():
        return remote(r.gp.at[:, :, 1 - co], r.cp, r.m_hc, (), (), to_core())

    def hx(k):
        return remote(r.xp.at[xy_at(k)], r.yp.at[NX - k], r.m_hx, (k,), (NX - k,), to_xy(k))

    def hz(k):
        return remote(r.zp.at[k], r.rp.at[MP - k], r.m_hz, (k,), (MP - k,), to_mp(k))

    def gc(j):
        return remote(r.gq.at[mp_at(j), :, 1 - co], r.cq.at[j], r.m_gc, (j,), (j,), to_core())

    def gx(j, k):
        return remote(r.xq.at[j, xy_at(k)], r.yq.at[j, NX - k], r.m_gx, (j, k), (j, NX - k), to_xy(k))

    def gz(k):
        return remote(r.zq.at[k], r.rq.at[MP - k], r.m_gz, (k,), (MP - k,), to_mp(k))

    def hc_finish():
        hc().wait_recv()
        for x in range(NX):
            r.xp[x] = (r.gp[:, x, co].astype(F32) + r.cp[:, x].astype(F32)).astype(BF)
        for k in range(1, NX):
            hx(k).start()

    def gc_finish(j):
        gc(j).wait_recv()
        m = mp_at(j)
        for x in range(NX):
            r.xq[j, x] = (r.gq[m, x, co].astype(F32) + r.cq[j, x].astype(F32)).astype(BF)
        for k in range(1, NX):
            gx(j, k).start()

    def gx_total(j):
        total = r.xq[j, xy].astype(F32)
        for k in range(1, NX):
            remote(r.xq.at[j, xy_at(k)], r.yq.at[j, k], r.m_gx, (j, k), (j, k), to_xy(k)).wait_recv()
            total = total + r.yq[j, k].astype(F32)
        return total

    def gx_finish(j):
        r.zq[j] = gx_total(j).astype(BF)
        gz(j).start()

    def small_core(a, b, sem):
        copy = remote(a, b.at[co], sem, (), (), to_core())
        copy.start()
        b[co] = a[...]
        sends.append(copy.wait_send)

    def small_core_finish(a, b, c, sem1, sem2):
        remote(a, b.at[1 - co], sem1, (), (), to_core()).wait_recv()
        c[xy] = sum_of(b, IN)
        for k in range(1, NX):
            copy = remote(c.at[xy], c.at[xy], sem2, (k,), (NX - k,), to_xy(k))
            copy.start()
            sends.append(copy.wait_send)

    def small_plane_finish(c, d, sem2, sem3):
        for k in range(1, NX):
            block = c.at[xy_at(k)]
            remote(block, block, sem2, (k,), (k,), to_xy(k)).wait_recv()
        d[mp] = sum_of(c, NX)
        for k in range(1, MP):
            copy = remote(d.at[mp], d.at[mp], sem3, (k,), (MP - k,), to_mp(k))
            copy.start()
            sends.append(copy.wait_send)

    def small_finish(d, sem3):
        for k in range(1, MP):
            block = d.at[mp_at(k)]
            remote(block, block, sem3, (k,), (k,), to_mp(k)).wait_recv()
        return sum_of(d, MP)

    def sum_of(ref, count):
        total = ref[0]
        for i in range(1, count):
            total = total + ref[i]
        return total

    pad = jnp.zeros((6, D), F32)
    rows2 = jnp.concatenate([gain_part2, shift_part2, pad], axis=0)
    phi_to = r.sa if z.own_weights else r.phi_grad
    phi_to[0:E, :] = tn(dlogits, h2)
    if z.own_weights:
        hc().start()
        r.sa[E : E + 8, :] = rows2
        small_core(r.sa, r.sb, r.m_s1)
        hc_finish()
        small_core_finish(r.sa, r.sb, r.sc, r.m_s1, r.m_s2)

    r.dh1[...] = jnp.zeros((SP, D), F32)

    def heads_backward(i, carry):
        j = lax.rem(i + 1, MP)
        m = mp_at(j)
        qkv, datt = r.qkv[m], r.datt[m]
        pieces = [[], [], []]
        for h in range(z.HL):
            query, key, value = (
                qkv[:, c * CW + h * HEAD_DIM : c * CW + (h + 1) * HEAD_DIM] for c in range(3)
            )
            grad_h = datt[:, h * HEAD_DIM : (h + 1) * HEAD_DIM]
            probs = r.probs[m, h]
            dprobs = nt(grad_h, value)
            dscores = probs * (dprobs - jnp.sum(probs * dprobs, axis=-1, keepdims=True))
            dscores = dscores.astype(BF)
            pieces[0].append(nn(dscores, key) * scale)
            pieces[1].append(tn(dscores, query) * scale)
            pieces[2].append(tn(probs.astype(BF), grad_h))
        dqkv = jnp.concatenate(pieces[0] + pieces[1] + pieces[2], axis=1).astype(BF)
        piece = tn(r.h1[...], dqkv)
        if z.own_weights:
            r.gq[m] = piece.astype(BF).reshape(NX, IN, RB, QW)
            gc(j).start()
        else:
            r.gq[m] = piece.astype(BF)
        r.dh1[...] += nt(dqkv, weight(m))
        if z.own_weights:

            @pl.when(i >= 1)
            def _():
                gc_finish(i)

            @pl.when(i >= 2)
            def _():
                gx_finish(i - 1)

        return carry

    lax.fori_loop(0, MP, heads_backward, 0)

    normed1, inv1 = normalize(own_image(r.tin))
    dh1 = r.dh1[...]
    gain_part1 = jnp.sum(dh1 * normed1, axis=0, keepdims=True)
    shift_part1 = jnp.sum(dh1, axis=0, keepdims=True)
    late = jnp.concatenate([gain_part1, shift_part1, pad], axis=0)
    if z.own_weights:
        gc_finish(0)
        r.ta[...] = late
        small_core(r.ta, r.tb, r.m_t1)
    input_grad = r.dresid[...] + norm_backward(dh1, gain1, normed1, inv1)
    for m in range(MP):
        r.isend[m] = input_grad[:, m * CW : (m + 1) * CW].astype(BF)
    swap_start(r.isend, r.iin, r.m_ings)

    if z.own_weights:
        gx_finish(MP - 1)
        small_core_finish(r.ta, r.tb, r.tc, r.m_t1, r.m_t2)
        total = r.xp[xy].astype(F32)
        for k in range(1, NX):
            remote(r.xp.at[xy_at(k)], r.yp.at[k], r.m_hx, (k,), (k,), to_xy(k)).wait_recv()
            total = total + r.yp[k].astype(F32)
        r.sums_p[...] = total
        for k in range(1, MP):
            r.zp[k] = r.sums_p[mp_at(k)].astype(BF)
            hz(k).start()
        small_plane_finish(r.sc, r.sd, r.m_s2, r.m_s3)
        own = gx_total(0)
        small_plane_finish(r.tc, r.td, r.m_t2, r.m_t3)

    def from_images(source, target):
        for i in range(MP):
            target[pl.ds(SEQ * i, SEQ), :] = source[i, 0:SEQ, :].astype(F32)

    swap_wait(r.osend, r.oin, r.m_outs)
    from_images(r.oin, r.output)
    if z.own_weights:
        total = r.sums_p[mp]
        for k in range(1, MP):
            remote(r.zp.at[k], r.rp.at[k], r.m_hz, (k,), (k,), to_mp(k)).wait_recv()
            total = total + r.rp[k].astype(F32)
        r.proj_grad[...] = total.T
        for k in range(1, MP):
            remote(r.zq.at[k], r.rq.at[k], r.m_gz, (k,), (k,), to_mp(k)).wait_recv()
            own = own + r.rq[k].astype(F32)
        for c in range(3):
            r.qkv_grad[c] = own[:, c * CW : (c + 1) * CW]
        first = small_finish(r.sd, r.m_s3)
        second = small_finish(r.td, r.m_t3)
        r.phi_grad[...] = first[:E]
        r.norm_grad[...] = jnp.concatenate([second[0:2], first[E : E + 2]], axis=0)
    else:
        r.norm_grad[...] = jnp.concatenate([late[0:2], rows2[0:2]], axis=0)
    swap_wait(r.isend, r.iin, r.m_ings)
    from_images(r.iin, r.input_grad)

    if z.own_weights:
        for k in range(1, MP):
            wz(k).wait_send()
            vz(k).wait_send()
            gz(k).wait_send()
            hz(k).wait_send()
        for k in range(1, NX):
            vx(k).wait_send()
            hx(k).wait_send()
            for j in range(MP):
                wx(j, k).wait_send()
                gx(j, k).wait_send()
        for j in range(MP):
            wc(j).wait_send()
            gc(j).wait_send()
        vc().wait_send()
        hc().wait_send()
    for wait in sends:
        wait()


def expert_grad_kernel(slots, dpre, hidden, dresults, in_grad, out_grad):
    in_grad[0] = tn(slots[0], dpre[0])
    out_grad[0] = tn(hidden[0], dresults[0])


def per_device(mesh, tokens, norm_params, w_qkv, w_proj, phi, w_in, w_out, cotangent):
    z = Sizes(mesh, tokens, w_qkv, phi, w_in)
    vmem, anyspace = pl.BlockSpec(memory_space=pltpu.VMEM), pl.BlockSpec(memory_space=pl.ANY)
    inputs = dict(
        tokens=tokens, norm_params=norm_params, w_qkv=w_qkv, w_proj=w_proj, phi=phi, cotangent=cotangent
    )
    specs = [vmem] * len(inputs)
    inputs.update(w_in=w_in, w_out=w_out)
    specs += [anyspace] * 2
    images = z.MP * z.DP
    outs = dict(
        output=((z.ROWS, z.CW), F32), input_grad=((z.ROWS, z.CW), F32),
        phi_grad=((z.E, z.D), F32), norm_grad=((4, z.D), F32),
        slots=((z.EPD, images, z.D), BF), dresults=((z.EPD, images, z.D), BF),
        hidden=((z.EPD, images, z.F), BF), dpre=((z.EPD, images, z.F), BF),
    )
    if z.own_weights:
        outs.update(qkv_grad=((3, z.RB, z.CW), F32), proj_grad=((z.CW, z.RB), F32))
    else:
        outs.update(gq=((z.MP, z.D, z.QW), BF), gp=((z.MP, z.D, z.CW), BF))
        wall = lax.all_gather(w_qkv.astype(BF), "dp", axis=1, tiled=True)
        wall = jnp.concatenate([wall[c] for c in range(3)], axis=1)
        wpall = lax.all_gather(w_proj.T.astype(BF), "dp", axis=0, tiled=True)
        inputs.update(wall=lax.all_gather(wall, "mp"), wpall=lax.all_gather(wpall, "mp"))
        specs += [vmem] * 2
    names, scratch = scratch_of(z)
    result = pl.pallas_call(
        functools.partial(block_kernel, z, list(inputs), list(outs), names),
        out_shape=[jax.ShapeDtypeStruct(*one) for one in outs.values()],
        in_specs=specs,
        out_specs=[vmem] * len(outs),
        scratch_shapes=scratch,
        compiler_params=pltpu.CompilerParams(
            collective_id=0, has_side_effects=True, vmem_limit_bytes=62 * 2**20
        ),
        name="block",
    )(*inputs.values())
    got = dict(zip(outs, result))

    pieces = 3

    def rows_in(e, i):
        return (e, 0, i)

    in_grad, out_grad = pl.pallas_call(
        expert_grad_kernel,
        grid=(z.EPD, pieces),
        in_specs=[
            pl.BlockSpec((1, images, z.D // pieces), rows_in),
            pl.BlockSpec((1, images, z.F), lambda e, i: (e, 0, 0)),
            pl.BlockSpec((1, images, z.F // pieces), rows_in),
            pl.BlockSpec((1, images, z.D), lambda e, i: (e, 0, 0)),
        ],
        out_specs=[
            pl.BlockSpec((1, z.D // pieces, z.F), lambda e, i: (e, i, 0)),
            pl.BlockSpec((1, z.F // pieces, z.D), lambda e, i: (e, i, 0)),
        ],
        out_shape=[
            jax.ShapeDtypeStruct((z.EPD, z.D, z.F), F32),
            jax.ShapeDtypeStruct((z.EPD, z.F, z.D), F32),
        ],
        name="expert_grads",
    )(got["slots"], got["dpre"], got["hidden"], got["dresults"])

    phi_grad, norm_grad = got["phi_grad"].T, got["norm_grad"]
    if z.own_weights:
        qkv_grad, proj_grad = got["qkv_grad"], got["proj_grad"]
    else:
        phi_grad, norm_grad = lax.psum((phi_grad, norm_grad), ("dp", "mp"))
        gq = lax.psum_scatter(got["gq"].astype(F32), "mp", scatter_dimension=0, tiled=False)
        gp = lax.psum_scatter(got["gp"].astype(F32), "mp", scatter_dimension=0, tiled=False)
        gq = jnp.stack([gq[:, c * z.CW : (c + 1) * z.CW] for c in range(3)])
        qkv_grad = lax.psum_scatter(gq, "dp", scatter_dimension=1, tiled=True)
        proj_grad = lax.psum_scatter(gp, "dp", scatter_dimension=0, tiled=True).T
    return (
        got["output"], got["input_grad"], qkv_grad, proj_grad, in_grad, out_grad, phi_grad, norm_grad
    )


def solution(mesh):
    return jax.shard_map(
        functools.partial(per_device, mesh),
        mesh=mesh,
        in_specs=(
            P("dp", "mp"), P(), P(None, "dp", "mp"), P("mp", "dp"), P(),
            P("dp", None, "mp"), P("dp", "mp", None), P("dp", "mp"),
        ),
        out_specs=(
            P("dp", "mp"), P("dp", "mp"), P(None, "dp", "mp"), P("mp", "dp"),
            P("dp", None, "mp"), P("dp", "mp", None), P(), P(),
        ),
        check_vma=False,
    )
```

```python
import functools
import math

import jax
import jax.numpy as jnp
from jax import lax
from jax.experimental import pallas as pl
from jax.experimental.pallas import tpu as pltpu
from jax.sharding import PartitionSpec as P

HEAD_DIM = 64
SEQ = 196
EPSILON = 1e-06
MESH = pl.DeviceIdType.MESH
BF = jnp.bfloat16
F32 = jnp.float32
NEG = -1e30


def nn(a, b):
    return lax.dot_general(a, b, (((1,), (0,)), ((), ())), preferred_element_type=F32)


def nt(a, b):
    return lax.dot_general(a, b, (((1,), (1,)), ((), ())), preferred_element_type=F32)


def tn(a, b):
    return lax.dot_general(a, b, (((0,), (0,)), ((), ())), preferred_element_type=F32)


def each(low, high, body):
    if high - low <= 8:
        for i in range(low, high):
            body(i)
    else:

        def step(i, carry):
            body(i)
            return carry

        lax.fori_loop(low, high, step, 0)


def select_rows(rows, cols, source):
    row = lax.broadcasted_iota(jnp.int32, (rows, cols), 0)
    col = lax.broadcasted_iota(jnp.int32, (rows, cols), 1)
    return jnp.where(col == source(row), 1.0, 0.0).astype(BF)


def normalize(values):
    mean = jnp.mean(values, axis=-1, keepdims=True)
    centered = values - mean
    var = jnp.mean(centered * centered, axis=-1, keepdims=True)
    inv = lax.rsqrt(var + EPSILON)
    return centered * inv, inv


def norm_backward(grad, gain, normed, inv):
    scaled = grad * gain
    first = jnp.mean(scaled, axis=-1, keepdims=True)
    second = jnp.mean(scaled * normed, axis=-1, keepdims=True)
    return inv * (scaled - first - normed * second)


class Sizes:
    def __init__(self, mesh, tokens, w_qkv, phi, w_in):
        self.DP, self.MP = mesh.shape["dp"], mesh.shape["mp"]
        self.D, self.E = phi.shape
        self.CW = tokens.shape[1]
        self.RB = w_qkv.shape[1]
        self.QW = 3 * self.CW
        self.HL = self.CW // HEAD_DIM
        self.EPD = w_in.shape[0]
        self.F = w_in.shape[2]
        self.IN = 2
        self.NX = self.DP // self.IN
        self.SP = (SEQ + 15) // 16 * 16
        self.ROWS = tokens.shape[0]
        self.KE = 2 * self.EPD
        self.own_weights = self.NX == 4 and self.RB % 32 == 0 and self.E + 2 <= self.KE * self.DP


def scratch_of(z):
    dma = pltpu.SemaphoreType.DMA
    v = pltpu.VMEM
    DP, MP, D, CW, RB, QW, SP, NX, IN, KE = z.DP, z.MP, z.D, z.CW, z.RB, z.QW, z.SP, z.NX, z.IN, z.KE
    half = RB // 2
    items = dict(
        tsend=v((MP, SP, CW), BF), tin=v((MP, SP, CW), BF),
        csend=v((MP, SP, CW), BF), cin=v((MP, SP, CW), BF),
        osend=v((MP, SP, CW), BF), oin=v((MP, SP, CW), BF),
        isend=v((MP, SP, CW), BF),
        wf_in=v((z.EPD, D, z.F), F32), wf_out=v((z.EPD, z.F, D), F32),
        wb_in=v((z.EPD, D, z.F), BF), wb_out=v((z.EPD, z.F, D), BF),
        h1=v((SP, D), BF), qkv=v((MP, SP, QW), BF), probs=v((MP, z.HL, SP, SP), F32),
        att=v((MP, SP, CW), BF), datt=v((MP, SP, CW), BF),
        resid=v((SP, D), F32), dresid=v((SP, D), F32), dh1=v((SP, D), F32),
        slot_out=v((DP, KE, D), F32), slot_in=v((DP, KE, D), F32),
        slot_all=v((MP, KE * DP, D), BF),
        part=v((MP, KE * DP, D), F32), psend=v((MP, KE * DP, D), BF), pin=v((MP, KE * DP, D), BF),
        back_out=v((DP, KE, D), F32), back_in=v((DP, KE, D), F32),
    )
    sems = dict(
        tok=(2, MP), cot=(2, MP), outs=(2, MP), ings=(2, MP), hbm=(2,),
        dp1=(2, DP), mp1=(2, 2, MP), mp2=(2, 2, MP), dp2=(2, DP),
    )
    if z.own_weights:
        items.update(
            wall=v((MP, NX, IN, RB, QW), BF), wpall=v((MP, NX, IN, RB, CW), BF),
            gq=v((MP, NX, IN, RB, QW), BF), gp=v((NX, IN, RB, D), BF),
            cq=v((MP, NX, RB, QW), BF), cp=v((NX, RB, D), BF),
            xq=v((MP, NX, RB, QW), BF), xp=v((NX, RB, D), BF),
            aq=v((MP, 4, half, QW), BF), ap=v((4, half, D), BF),
            bq=v((MP, 2, half, QW), BF), bp=v((2, half, D), BF),
            dq=v((MP, 2, half, QW), BF), dp_=v((2, half, D), BF),
            zq=v((MP, RB, QW), BF), rq=v((MP, RB, QW), BF),
            fp=v((MP, RB, CW), F32), zp=v((MP, RB, CW), BF), rp=v((MP, RB, CW), BF),
            sa=v((DP, KE, D), F32), sb=v((DP, KE, D), F32), sc=v((MP, KE, D), F32), sd=v((DP, KE, D), F32),
            ta=v((2, D), F32), tb=v((DP, 2, D), F32), tc=v((MP, 2, D), F32),
        )
        sems.update(
            wz=(2, MP), wx=(2, MP, 4), wc=(2, MP), vz=(2, MP), vx=(2, 4), vc=(2,),
            gc=(2, MP), gx=(2, MP, 6), gz=(2, MP), hc=(2,), hx=(2, 6), hz=(2, MP),
            s1=(2, DP), s2=(2, MP), s3=(2, DP), t1=(2, DP), t2=(2, MP),
        )
    names, shapes = [], []
    for name, shape in items.items():
        names.append(name)
        shapes.append(shape)
    for name, shape in sems.items():
        names.append("m_" + name)
        shapes.append(dma(shape))
    return names, shapes


class Refs:
    pass


def block_kernel(z, in_names, out_names, names, *refs):
    r = Refs()
    for name, ref in zip(in_names + out_names + names, refs):
        setattr(r, name, ref)
    DP, MP, D, CW, RB, QW, SP = z.DP, z.MP, z.D, z.CW, z.RB, z.QW, z.SP
    NX, IN, E, EPD, KE = z.NX, z.IN, z.E, z.EPD, z.KE
    half = RB // 2
    dp, mp = lax.axis_index("dp"), lax.axis_index("mp")
    xy, co = dp // IN, lax.rem(dp, IN)
    xn = xy + 1 - 2 * lax.rem(xy, 2)
    yn = lax.rem(xy + 2, NX)
    dg = lax.rem(xn + 2, NX)
    to_x, to_y, to_core = (xn * IN + co, mp), (yn * IN + co, mp), (xy * IN + 1 - co, mp)
    sends = []

    def remote(src, dst, sem, s_at, r_at, device):
        return pltpu.make_async_remote_copy(
            src_ref=src, dst_ref=dst, send_sem=sem.at[(0,) + s_at], recv_sem=sem.at[(1,) + r_at],
            device_id=device, device_id_type=MESH,
        )

    def send(*copy):
        remote(*copy).start()
        sends.append(lambda: remote(*copy).wait_send())

    def arrive(ref, sem, at):
        remote(ref, ref, sem, at, at, to_mp(1)).wait_recv()

    def mp_at(k):
        return lax.rem(mp + k, MP)

    def dp_at(k):
        return lax.rem(dp + k, DP)

    def to_mp(k):
        return (dp, mp_at(k))

    def to_dp(k):
        return (dp_at(k), mp)

    barrier = pltpu.get_barrier_semaphore()
    for k in range(1, MP):
        pl.semaphore_signal(barrier, inc=1, device_id=to_mp(k), device_id_type=MESH)
    each(1, DP, lambda k: pl.semaphore_signal(barrier, inc=1, device_id=to_dp(k), device_id_type=MESH))

    load_in = pltpu.make_async_copy(r.w_in, r.wf_in, r.m_hbm.at[0])
    load_out = pltpu.make_async_copy(r.w_out, r.wf_out, r.m_hbm.at[1])
    load_in.start()
    load_out.start()

    if z.own_weights:
        r.wall[mp, xy, co] = jnp.concatenate([r.w_qkv[c].astype(BF) for c in range(3)], axis=1)
        r.wpall[mp, xy, co] = r.w_proj[...].T.astype(BF)
    pl.semaphore_wait(barrier, MP - 1 + DP - 1)

    def to_images(source, target):
        target[...] = jnp.zeros((MP, SP, CW), BF)
        rows = source[...].T
        for i in range(MP):
            target[i, 0:SEQ, :] = rows[SEQ * i : SEQ * (i + 1)]

    def swap(src, dst, sem):
        for k in range(1, MP):
            send(src.at[mp_at(k)], dst.at[mp], sem, (k,), (MP - k,), to_mp(k))
        dst[mp] = src[mp]

    def swap_wait(dst, sem):
        for k in range(1, MP):
            arrive(dst.at[mp_at(k)], sem, (k,))

    def to_column(block, sem):
        for k in range(1, MP):
            send(block, block, sem, (k,), (MP - k,), to_mp(k))

    class Plane:
        def __init__(self, block, sem, at):
            self.block, self.sem, self.at = block, sem, at

        def copy(self, ref, way, device):
            send(ref, ref, self.sem, self.at + (way,), self.at + (way,), device)

        def start(self):
            self.copy(self.block(xy, 0, RB), 0, to_x)
            self.copy(self.block(xy, 0, RB), 1, to_y)

        def forward(self):
            arrive(self.block(xn, 0, RB), self.sem, self.at + (0,))
            self.copy(self.block(xn, 0, half), 2, to_y)
            arrive(self.block(yn, 0, RB), self.sem, self.at + (1,))
            self.copy(self.block(yn, half, half), 3, to_x)

        def wait(self):
            arrive(self.block(dg, 0, half), self.sem, self.at + (2,))
            arrive(self.block(dg, half, half), self.sem, self.at + (3,))

    def qkv_plane(j):
        return Plane(lambda pos, low, rows: r.wall.at[mp_at(j), pos, co, pl.ds(low, rows)], r.m_wx, (j,))

    def other_core(ref, core, sem, at):
        send(ref(core), ref(core), sem, at, at, to_core)

    def qkv_cores(j):
        return lambda core: r.wall.at[mp_at(j), :, core]

    def load_expert(copy, wide, low):
        copy.wait()
        low[...] = wide[...].astype(BF)

    if z.own_weights:
        planes = [qkv_plane(j) for j in range(MP)]
        proj_plane = Plane(lambda pos, low, rows: r.wpall.at[:, pos, co, pl.ds(low, rows)], r.m_vx, ())

        def column_arrived(j):
            arrive(r.wall.at[mp_at(j), xy, co], r.m_wz, (j,))
            planes[j].start()

        def plane_arrived(j):
            planes[j].wait()
            other_core(qkv_cores(j), co, r.m_wc, (j,))

        to_column(r.wall.at[mp, xy, co], r.m_wz)
        planes[0].start()
        to_column(r.wpall.at[mp, xy, co], r.m_vz)
        to_images(r.tokens, r.tsend)
        load_expert(load_in, r.wf_in, r.wb_in)
        column_arrived(1)
        planes[0].forward()
        column_arrived(2)
        planes[1].forward()
        plane_arrived(0)
        column_arrived(3)
        swap(r.tsend, r.tin, r.m_tok)
        planes[2].forward()
        plane_arrived(1)
        for k in range(1, MP):
            arrive(r.wpall.at[mp_at(k), xy, co], r.m_vz, (k,))
        proj_plane.start()
        to_images(r.cotangent, r.csend)
        planes[3].forward()
        plane_arrived(2)
        load_expert(load_out, r.wf_out, r.wb_out)
        swap(r.csend, r.cin, r.m_cot)
        proj_plane.forward()
        plane_arrived(3)
    else:
        to_images(r.tokens, r.tsend)
        swap(r.tsend, r.tin, r.m_tok)
        to_images(r.cotangent, r.csend)
        swap(r.csend, r.cin, r.m_cot)
        load_expert(load_in, r.wf_in, r.wb_in)
        load_expert(load_out, r.wf_out, r.wb_out)

    swap_wait(r.tin, r.m_tok)
    gain1, shift1 = r.norm_params[0:1, :], r.norm_params[1:2, :]
    gain2, shift2 = r.norm_params[2:3, :], r.norm_params[3:4, :]

    def own_image(ref):
        return jnp.concatenate([ref[i] for i in range(MP)], axis=1)

    normed1, _ = normalize(own_image(r.tin).astype(F32))
    r.h1[...] = (normed1 * gain1 + shift1).astype(BF)

    scale = 1.0 / math.sqrt(HEAD_DIM)
    key_ok = lax.broadcasted_iota(jnp.int32, (1, SP), 1) < SEQ

    def weight(m):
        return r.wall[m].reshape(D, QW) if z.own_weights else r.wall[m]

    def proj_weight(m):
        return r.wpall[m].reshape(D, CW) if z.own_weights else r.wpall[m]

    def head_cols(qkv, h):
        return (qkv[:, c * CW + h * HEAD_DIM : c * CW + (h + 1) * HEAD_DIM] for c in range(3))

    def heads_forward(j, carry):
        m = mp_at(j)
        if z.own_weights:
            arrive(r.wall.at[m, :, 1 - co], r.m_wc, (j,))

            @pl.when(j == MP - 1)
            def _():
                proj_plane.wait()
                remote(r.wpall.at[:, :, co], r.wpall.at[:, :, co], r.m_vc, (), (), to_core).start()

        qkv = nn(r.h1[...], weight(m)).astype(BF)
        r.qkv[m] = qkv
        attended = []
        for h in range(z.HL):
            query, key, value = head_cols(qkv, h)
            scores = jnp.where(key_ok, nt(query, key) * scale, NEG)
            top = jnp.max(scores, axis=-1, keepdims=True)
            grown = jnp.exp(scores - top)
            probs = grown / jnp.sum(grown, axis=-1, keepdims=True)
            r.probs[m, h] = probs
            attended.append(nn(probs.astype(BF), value))
        r.att[m] = jnp.concatenate(attended, axis=1).astype(BF)
        return carry

    lax.fori_loop(0, MP, heads_forward, 0)
    if z.own_weights:
        sends.append(lambda: remote(r.wpall.at[:, :, co], r.wpall.at[:, :, co], r.m_vc, (), (), to_core).wait_send())
        arrive(r.wpall.at[:, :, 1 - co], r.m_vc, ())

    resid = own_image(r.tin).astype(F32)
    for m in range(MP):
        resid = resid + nt(r.att[m], proj_weight(m))
    r.resid[...] = resid
    normed2, inv2 = normalize(resid)
    h2 = (normed2 * gain2 + shift2).astype(BF)
    phi_low = r.phi[...].astype(BF)
    logits = nt(h2, phi_low)
    token_ok = lax.broadcasted_iota(jnp.int32, (SP, 1), 0) < SEQ
    masked = jnp.where(token_ok, logits, NEG)
    grown = jnp.exp(masked - jnp.max(masked, axis=0, keepdims=True))
    dispatch = grown / jnp.sum(grown, axis=0, keepdims=True)
    grown = jnp.exp(logits - jnp.max(logits, axis=1, keepdims=True))
    combine = grown / jnp.sum(grown, axis=1, keepdims=True)
    dispatch_low, combine_low = dispatch.astype(BF), combine.astype(BF)
    swap_wait(r.cin, r.m_cot)
    grad = own_image(r.cin)
    slots = tn(dispatch_low, h2).astype(BF)
    dresults = tn(combine_low, grad).astype(BF)

    def spread(target, rows):
        for d in range(DP):
            target[d] = rows[d * KE : (d + 1) * KE]

    def collect(source):
        return jnp.concatenate([source[d] for d in range(DP)], axis=0)

    def dp_swap(src, dst, sem):
        def copy(k):
            return remote(src.at[dp_at(k)], dst.at[dp], sem, (k,), (DP - k,), to_dp(k))

        each(1, DP, lambda k: copy(k).start())
        sends.append(lambda: each(1, DP, lambda k: copy(k).wait_send()))
        dst[dp] = src[dp]

    def dp_wait(dst, sem):
        each(1, DP, lambda k: arrive(dst.at[dp_at(k)], sem, (k,)))

    def out_row(row):
        d, q = row // KE, row % KE
        return (q // EPD) * E + d * EPD + q % EPD

    spread(r.slot_out, nn(select_rows(DP * KE, 2 * E, out_row), jnp.concatenate([slots, dresults], axis=0)))
    dp_swap(r.slot_out, r.slot_in, r.m_dp1)
    dp_wait(r.slot_in, r.m_dp1)
    gather_rows = select_rows(KE * DP, DP * KE, lambda row: (row % DP) * KE + row // DP)
    r.slot_all[mp] = nn(gather_rows, collect(r.slot_in).astype(BF)).astype(BF)
    rows = EPD * DP

    def kind_rows(ref, kind):
        return ref.at[pl.ds(kind * rows, rows)]

    for kind in range(2):
        for k in range(1, MP):
            block = kind_rows(r.slot_all.at[mp], kind)
            send(block, block, r.m_mp1, (kind, k), (kind, MP - k), to_mp(k))

    def expert_rows(kind):
        for k in range(1, MP):
            arrive(kind_rows(r.slot_all.at[mp_at(k)], kind), r.m_mp1, (kind, k))
        parts = [r.slot_all[m, kind * rows : (kind + 1) * rows, :].astype(F32) for m in range(MP)]
        return [
            jnp.concatenate([one[e * DP : (e + 1) * DP] for one in parts], axis=0).astype(BF) for e in range(EPD)
        ]

    def send_parts(kind, per_expert):
        for e in range(EPD):
            at = kind * rows + e * DP
            for m in range(MP):
                r.part[m, at : at + DP, :] = per_expert[e][m * DP : (m + 1) * DP]
        here = slice(kind * rows, (kind + 1) * rows)
        r.psend[:, here, :] = r.part[:, here, :].astype(BF)
        for k in range(1, MP):
            send(
                kind_rows(r.psend.at[mp_at(k)], kind), kind_rows(r.pin.at[MP - k], kind),
                r.m_mp2, (kind, k), (kind, MP - k), to_mp(k),
            )

    slopes, results_part = [], []
    for e, slots_e in enumerate(expert_rows(0)):
        pre = nn(slots_e, r.wb_in[e])
        cdf = 0.5 * (1.0 + lax.erf(pre * (1.0 / math.sqrt(2.0))))
        hidden = (pre * cdf).astype(BF)
        results_part.append(nn(hidden, r.wb_out[e]))
        slopes.append(cdf + pre * jnp.exp(-0.5 * pre * pre) * (1.0 / math.sqrt(2.0 * math.pi)))
        r.slots[e], r.hidden[e] = slots_e, hidden
    send_parts(0, results_part)
    dslots_part = []
    for e, dresults_e in enumerate(expert_rows(1)):
        dpre = (nt(dresults_e, r.wb_out[e]) * slopes[e]).astype(BF)
        dslots_part.append(nt(dpre, r.wb_in[e]))
        r.dresults[e], r.dpre[e] = dresults_e, dpre
    send_parts(1, dslots_part)
    total = r.part[mp]
    for k in range(1, MP):
        for kind in range(2):
            arrive(kind_rows(r.pin.at[k], kind), r.m_mp2, (kind, k))
        total = total + r.pin[k].astype(F32)
    back_rows = select_rows(DP * KE, KE * DP, lambda row: (row % KE) * DP + row // KE)
    spread(r.back_out, nn(back_rows, total.astype(BF)))
    dp_swap(r.back_out, r.back_in, r.m_dp2)
    dp_wait(r.back_in, r.m_dp2)

    def result_row(row):
        kind, e = row // E, row % E
        return (e // EPD) * KE + kind * EPD + e % EPD

    both = nn(select_rows(2 * E, DP * KE, result_row), collect(r.back_in).astype(BF)).astype(BF)
    results, dslots = both[:E], both[E:]

    output = r.resid[...] + nn(combine_low, results)
    for m in range(MP):
        r.osend[m] = output[:, m * CW : (m + 1) * CW].astype(BF)
    swap(r.osend, r.oin, r.m_outs)
    dcombine, ddispatch = nt(grad, results), nt(h2, dslots)
    dlogits = dispatch * (ddispatch - jnp.sum(dispatch * ddispatch, axis=0, keepdims=True))
    dlogits = dlogits + combine * (dcombine - jnp.sum(combine * dcombine, axis=1, keepdims=True))
    dlogits = dlogits.astype(BF)
    dh2 = nn(dispatch_low, dslots) + nn(dlogits, phi_low)
    dresid = grad.astype(F32) + norm_backward(dh2, gain2, normed2, inv2)
    r.dresid[...] = dresid
    dbranch = dresid.astype(BF)
    proj_part = tn(dbranch, own_image(r.att)).astype(BF)

    class Unit:
        def __init__(self, part, got, mine, first, out, second, core_sem, sem, at):
            self.part, self.got, self.mine, self.first = part, got, mine, first
            self.out, self.second, self.core_sem, self.sem, self.at = out, second, core_sem, sem, at

        def start(self):
            send(self.part.at[:, 1 - co], self.got, self.core_sem, self.at, self.at, to_core)

        def copy(self, src, dst, way, device):
            send(src, dst, self.sem, self.at + (way,), self.at + (way,), device)

        def plane(self):
            arrive(self.got, self.core_sem, self.at)
            for x in range(NX):
                self.mine[x] = (self.part[x, co].astype(F32) + self.got[x].astype(F32)).astype(BF)
            low, high = pl.ds(0, half), pl.ds(half, half)
            self.copy(self.mine.at[dg, low], self.first.at[1], 1, to_x)
            self.copy(self.mine.at[dg, high], self.first.at[3], 3, to_y)
            self.copy(self.mine.at[xn, low], self.first.at[0], 0, to_x)
            self.copy(self.mine.at[yn, high], self.first.at[2], 2, to_y)

        def added(self, x, low, index):
            arrive(self.first.at[index], self.sem, self.at + (index,))
            return self.mine[x, low : low + half, :].astype(F32) + self.first[index].astype(F32)

        def forward(self):
            self.out[0] = self.added(yn, 0, 1).astype(BF)
            self.copy(self.out.at[0], self.second.at[0], 4, to_y)
            self.out[1] = self.added(xn, half, 3).astype(BF)
            self.copy(self.out.at[1], self.second.at[1], 5, to_x)

        def total(self):
            pieces = []
            for i in range(2):
                piece = self.added(xy, i * half, 2 * i)
                arrive(self.second.at[i], self.sem, self.at + (4 + i,))
                pieces.append(piece + self.second[i].astype(F32))
            return jnp.concatenate(pieces, axis=0)

    def qkv_unit(j):
        return Unit(
            r.gq.at[mp_at(j)], r.cq.at[j], r.xq.at[j], r.aq.at[j], r.bq.at[j], r.dq.at[j], r.m_gc, r.m_gx, (j,)
        )

    def qkv_column(j):
        r.zq[j] = units[j].total().astype(BF)
        send(r.zq.at[j], r.rq.at[MP - j], r.m_gz, (j,), (MP - j,), to_mp(j))

    def proj_column():
        total = proj_unit.total()
        for m in range(MP):
            piece = total[:, m * CW : (m + 1) * CW]
            r.fp[m] = piece
            r.zp[m] = piece.astype(BF)
        for k in range(1, MP):
            send(r.zp.at[mp_at(k)], r.rp.at[MP - k], r.m_hz, (k,), (MP - k,), to_mp(k))

    def sum_of(ref, count):
        total = ref[0]
        for i in range(1, count):
            total = total + ref[i]
        return total

    def small_column():
        dp_wait(r.sb, r.m_s1)
        r.sc[mp] = sum_of(r.sb, DP)
        to_column(r.sc.at[mp], r.m_s2)

    def small_back():
        for k in range(1, MP):
            arrive(r.sc.at[mp_at(k)], r.m_s2, (k,))
        r.sd[dp] = sum_of(r.sc, MP)
        for k in range(1, DP):
            send(r.sd.at[dp], r.sd.at[dp], r.m_s3, (k,), (DP - k,), to_dp(k))

    def gains(grad_out, normed):
        return jnp.concatenate(
            [jnp.sum(grad_out * normed, axis=0, keepdims=True), jnp.sum(grad_out, axis=0, keepdims=True)], axis=0
        )

    if z.own_weights:
        units = [qkv_unit(j) for j in range(MP)]
        proj_unit = Unit(r.gp, r.cp, r.xp, r.ap, r.bp, r.dp_, r.m_hc, r.m_hx, ())
        r.gp[...] = proj_part.reshape(NX, IN, RB, D)
        proj_unit.start()
    else:
        r.gp[...] = proj_part
    for m in range(MP):
        r.datt[m] = nn(dbranch, proj_weight(m)).astype(BF)
    rows2 = gains(dh2, normed2)
    if z.own_weights:
        phi_part = tn(dlogits, h2)
        r.sa[...] = jnp.zeros((DP, KE, D), F32)
        for i in range(E // KE):
            r.sa[i] = phi_part[i * KE : (i + 1) * KE]
        r.sa[E // KE, 0:2, :] = rows2
        dp_swap(r.sa, r.sb, r.m_s1)
    else:
        r.phi_grad[...] = tn(dlogits, h2)

    def heads_backward(j):
        m = mp_at(j)
        qkv, datt = r.qkv[m], r.datt[m]
        pieces = [[], [], []]
        for h in range(z.HL):
            query, key, value = head_cols(qkv, h)
            grad_h = datt[:, h * HEAD_DIM : (h + 1) * HEAD_DIM]
            probs = r.probs[m, h]
            dprobs = nt(grad_h, value)
            dscores = probs * (dprobs - jnp.sum(probs * dprobs, axis=-1, keepdims=True))
            dscores = dscores.astype(BF)
            pieces[0].append(nn(dscores, key) * scale)
            pieces[1].append(tn(dscores, query) * scale)
            pieces[2].append(tn(probs.astype(BF), grad_h))
        dqkv = jnp.concatenate(pieces[0] + pieces[1] + pieces[2], axis=1).astype(BF)
        piece = tn(r.h1[...], dqkv).astype(BF)
        if z.own_weights:
            r.gq[m] = piece.reshape(NX, IN, RB, QW)
        else:
            r.gq[m] = piece
        return dqkv

    order = list(range(1, MP)) + [0]
    between = {0: [], 1: [], 2: [], 3: []}
    if z.own_weights:
        between = {
            0: [proj_unit.plane],
            1: [units[1].plane, proj_unit.forward],
            2: [units[2].plane, units[1].forward, small_column],
            3: [units[3].plane, units[2].forward, proj_column],
        }
    dh1 = None
    for i, j in enumerate(order):
        dqkv = heads_backward(j)
        if z.own_weights:
            units[j].start()
        part = nt(dqkv, weight(mp_at(j)))
        if i == 0:
            r.dh1[...] = part
        else:
            r.dh1[...] += part
        for step in between.get(i, []):
            step()

    if z.own_weights:
        units[0].plane()
    normed1, inv1 = normalize(own_image(r.tin).astype(F32))
    dh1 = r.dh1[...]
    rows1 = gains(dh1, normed1)
    if z.own_weights:
        r.ta[...] = rows1
        for k in range(1, DP):
            send(r.ta, r.tb.at[dp], r.m_t1, (k,), (DP - k,), to_dp(k))
        r.tb[dp] = rows1
    input_grad = r.dresid[...] + norm_backward(dh1, gain1, normed1, inv1)
    for m in range(MP):
        r.isend[m] = input_grad[:, m * CW : (m + 1) * CW].astype(BF)
    swap(r.isend, r.iin, r.m_ings)

    if z.own_weights:
        qkv_column(1)
        units[3].forward()
        small_back()
        qkv_column(2)
        units[0].forward()
        dp_wait(r.tb, r.m_t1)
        r.tc[mp] = sum_of(r.tb, DP)
        to_column(r.tc.at[mp], r.m_t2)
    swap_wait(r.oin, r.m_outs)
    r.output[...] = from_images(r.oin)
    if z.own_weights:
        qkv_column(3)
        total = r.fp[mp]
        for k in range(1, MP):
            arrive(r.rp.at[k], r.m_hz, (k,))
            total = total + r.rp[k].astype(F32)
        r.proj_grad[...] = total.T
        dp_wait(r.sd, r.m_s3)
        for i in range(E // KE):
            r.phi_grad[i * KE : (i + 1) * KE, :] = r.sd[i]
        total = units[0].total()
        for k in range(1, MP):
            arrive(r.rq.at[k], r.m_gz, (k,))
            total = total + r.rq[k].astype(F32)
        for c in range(3):
            r.qkv_grad[c] = total[:, c * CW : (c + 1) * CW]
        for k in range(1, MP):
            arrive(r.tc.at[mp_at(k)], r.m_t2, (k,))
        r.norm_grad[...] = jnp.concatenate([sum_of(r.tc, MP), r.sd[E // KE, 0:2, :]], axis=0)
    else:
        r.norm_grad[...] = jnp.concatenate([rows1, rows2], axis=0)
    swap_wait(r.iin, r.m_ings)

    for wait in sends:
        wait()


def from_images(source):
    images = [source[i, 0:SEQ, :].astype(F32) for i in range(source.shape[0])]
    return jnp.concatenate(images, axis=0).T


def finish_kernel(passed, slots, dpre, hidden, dresults, iin, *refs):
    sources, (in_grad, out_grad, input_grad), rest = refs[:passed], refs[passed : passed + 3], refs[passed + 3 :]
    targets, (grads_in, grads_out, grad_t, sem, tile_sem) = rest[:passed], rest[passed:]
    copies = [pltpu.make_async_copy(a, b, sem.at[i]) for i, (a, b) in enumerate(zip(sources, targets))]
    for copy in copies:
        copy.start()
    experts, _, width = slots.shape
    tile = 256 if width % 256 == 0 else width
    count = 0
    for e in range(experts):
        for left, right, held, target in ((slots, dpre, grads_in, in_grad), (hidden, dresults, grads_out, out_grad)):
            for t in range(width // tile):
                here = pl.ds(t * tile, tile)
                held[e, here, :] = tn(left[e, :, t * tile : (t + 1) * tile], right[e])
                copy = pltpu.make_async_copy(held.at[e, here], target.at[e, here], tile_sem.at[count])
                copy.start()
                copies.append(copy)
                count += 1
    grad_t[...] = from_images(iin)
    last = pltpu.make_async_copy(grad_t, input_grad, sem.at[passed])
    last.start()
    for copy in copies + [last]:
        copy.wait()


def per_device(mesh, tokens, norm_params, w_qkv, w_proj, phi, w_in, w_out, cotangent):
    z = Sizes(mesh, tokens, w_qkv, phi, w_in)
    vmem, anyspace = pl.BlockSpec(memory_space=pltpu.VMEM), pl.BlockSpec(memory_space=pl.ANY)
    inputs = dict(
        tokens=tokens.T, norm_params=norm_params, w_qkv=w_qkv, w_proj=w_proj, phi=phi.T, cotangent=cotangent.T
    )
    specs = [vmem] * len(inputs)
    inputs.update(w_in=w_in, w_out=w_out)
    specs += [anyspace] * 2
    images = z.MP * z.DP
    outs = dict(
        output=((z.CW, z.ROWS), F32), iin=((z.MP, z.SP, z.CW), BF),
        phi_grad=((z.E, z.D), F32), norm_grad=((4, z.D), F32),
        slots=((z.EPD, images, z.D), BF), dresults=((z.EPD, images, z.D), BF),
        hidden=((z.EPD, images, z.F), BF), dpre=((z.EPD, images, z.F), BF),
    )
    if z.own_weights:
        outs.update(qkv_grad=((3, z.RB, z.CW), F32), proj_grad=((z.CW, z.RB), F32))
    else:
        outs.update(gq=((z.MP, z.D, z.QW), BF), gp=((z.D, z.D), BF))
        wall = lax.all_gather(w_qkv.astype(BF), "dp", axis=1, tiled=True)
        wall = jnp.concatenate([wall[c] for c in range(3)], axis=1)
        wpall = lax.all_gather(w_proj.T.astype(BF), "dp", axis=0, tiled=True)
        inputs.update(wall=lax.all_gather(wall, "mp"), wpall=lax.all_gather(wpall, "mp"))
        specs += [vmem] * 2
    names, scratch = scratch_of(z)
    result = pl.pallas_call(
        functools.partial(block_kernel, z, list(inputs), list(outs), names),
        out_shape=[jax.ShapeDtypeStruct(*one) for one in outs.values()],
        in_specs=specs,
        out_specs=[vmem] * len(outs),
        scratch_shapes=scratch,
        compiler_params=pltpu.CompilerParams(
            collective_id=0, has_side_effects=True, vmem_limit_bytes=62 * 2**20
        ),
        name="block",
    )(*inputs.values())
    got = dict(zip(outs, result))

    passed = ["output", "norm_grad", "phi_grad"] + (["qkv_grad", "proj_grad"] if z.own_weights else [])
    tile = 256 if z.F % 256 == 0 and z.D == z.F else z.F
    tiles = 2 * z.EPD * (z.F // tile)
    results = pl.pallas_call(
        functools.partial(finish_kernel, len(passed)),
        in_specs=[vmem] * (5 + len(passed)),
        out_specs=[anyspace] * (3 + len(passed)),
        out_shape=[
            jax.ShapeDtypeStruct((z.EPD, z.D, z.F), F32),
            jax.ShapeDtypeStruct((z.EPD, z.F, z.D), F32),
            jax.ShapeDtypeStruct((z.CW, z.ROWS), F32),
        ]
        + [jax.ShapeDtypeStruct(*outs[name]) for name in passed],
        scratch_shapes=[
            pltpu.VMEM((z.EPD, z.D, z.F), F32),
            pltpu.VMEM((z.EPD, z.F, z.D), F32),
            pltpu.VMEM((z.CW, z.ROWS), F32),
            pltpu.SemaphoreType.DMA((len(passed) + 1,)),
            pltpu.SemaphoreType.DMA((tiles,)),
        ],
        compiler_params=pltpu.CompilerParams(vmem_limit_bytes=60 * 2**20),
        name="finish",
    )(got["slots"], got["dpre"], got["hidden"], got["dresults"], got["iin"], *(got[name] for name in passed))
    in_grad, out_grad, input_grad = results[:3]
    got.update(zip(passed, results[3:]))
    output, input_grad = got["output"].T, input_grad.T
    phi_grad, norm_grad = got["phi_grad"].T, got["norm_grad"]
    if z.own_weights:
        qkv_grad, proj_grad = got["qkv_grad"], got["proj_grad"]
    else:
        phi_grad, norm_grad = lax.psum((phi_grad, norm_grad), ("dp", "mp"))
        gq = lax.psum_scatter(got["gq"].astype(F32), "mp", scatter_dimension=0, tiled=False)
        gp = lax.psum_scatter(got["gp"].astype(F32), "mp", scatter_dimension=1, tiled=True)
        gq = jnp.stack([gq[:, c * z.CW : (c + 1) * z.CW] for c in range(3)])
        qkv_grad = lax.psum_scatter(gq, "dp", scatter_dimension=1, tiled=True)
        proj_grad = lax.psum_scatter(gp, "dp", scatter_dimension=0, tiled=True).T
    return (
        output, input_grad, qkv_grad, proj_grad, in_grad, out_grad, phi_grad, norm_grad
    )


def solution(mesh):
    return jax.shard_map(
        functools.partial(per_device, mesh),
        mesh=mesh,
        in_specs=(
            P("dp", "mp"), P(), P(None, "dp", "mp"), P("mp", "dp"), P(),
            P("dp", None, "mp"), P("dp", "mp", None), P("dp", "mp"),
        ),
        out_specs=(
            P("dp", "mp"), P("dp", "mp"), P(None, "dp", "mp"), P("mp", "dp"),
            P("dp", None, "mp"), P("dp", "mp", None), P(), P(),
        ),
        check_vma=False,
    )
```

```python
import functools
import math

import jax
import jax.numpy as jnp
from jax import lax
from jax.experimental import pallas as pl
from jax.experimental.pallas import tpu as pltpu
from jax.sharding import PartitionSpec as P

HEAD_DIM = 64
SEQ = 196
EPSILON = 1e-06
MESH = pl.DeviceIdType.MESH
BF = jnp.bfloat16
F32 = jnp.float32
NEG = -1e30


def nn(a, b):
    return lax.dot_general(a, b, (((1,), (0,)), ((), ())), preferred_element_type=F32)


def nt(a, b):
    return lax.dot_general(a, b, (((1,), (1,)), ((), ())), preferred_element_type=F32)


def tn(a, b):
    return lax.dot_general(a, b, (((0,), (0,)), ((), ())), preferred_element_type=F32)


def each(low, high, body):
    if high - low <= 8:
        for i in range(low, high):
            body(i)
    else:

        def step(i, carry):
            body(i)
            return carry

        lax.fori_loop(low, high, step, 0)


def select_rows(rows, cols, source):
    row = lax.broadcasted_iota(jnp.int32, (rows, cols), 0)
    col = lax.broadcasted_iota(jnp.int32, (rows, cols), 1)
    return jnp.where(col == source(row), 1.0, 0.0).astype(BF)


def normalize(values):
    mean = jnp.mean(values, axis=-1, keepdims=True)
    centered = values - mean
    var = jnp.mean(centered * centered, axis=-1, keepdims=True)
    inv = lax.rsqrt(var + EPSILON)
    return centered * inv, inv


def norm_backward(grad, gain, normed, inv):
    scaled = grad * gain
    first = jnp.mean(scaled, axis=-1, keepdims=True)
    second = jnp.mean(scaled * normed, axis=-1, keepdims=True)
    return inv * (scaled - first - normed * second)


class Sizes:
    def __init__(self, mesh, tokens, w_qkv, phi, w_in):
        self.DP, self.MP = mesh.shape["dp"], mesh.shape["mp"]
        self.D, self.E = phi.shape
        self.CW = tokens.shape[1]
        self.RB = w_qkv.shape[1]
        self.QW = 3 * self.CW
        self.HL = self.CW // HEAD_DIM
        self.EPD = w_in.shape[0]
        self.F = w_in.shape[2]
        self.IN = 2
        self.NX = self.DP // self.IN
        self.SP = (SEQ + 15) // 16 * 16
        self.ROWS = tokens.shape[0]
        self.KE = 2 * self.EPD
        self.own_weights = self.MP == 4 and self.NX == 4 and self.RB % 32 == 0 and self.E + 2 <= self.KE * self.DP


def scratch_of(z):
    dma = pltpu.SemaphoreType.DMA
    v = pltpu.VMEM
    DP, MP, D, CW, RB, QW, SP, NX, IN, KE = z.DP, z.MP, z.D, z.CW, z.RB, z.QW, z.SP, z.NX, z.IN, z.KE
    half = RB // 2
    items = dict(
        tsend=v((MP, SP, CW), BF), tin=v((MP, SP, CW), BF),
        csend=v((MP, SP, CW), BF), cin=v((MP, SP, CW), BF),
        osend=v((MP, SP, CW), BF), oin=v((MP, SP, CW), BF),
        isend=v((MP, SP, CW), BF),
        wf_in=v((z.EPD, D, z.F), F32), wf_out=v((z.EPD, z.F, D), F32),
        wb_in=v((z.EPD, D, z.F), BF), wb_out=v((z.EPD, z.F, D), BF),
        h1=v((SP, D), BF), qkv=v((MP, SP, QW), BF), probs=v((MP, z.HL, SP, SP), F32),
        att=v((MP, SP, CW), BF), datt=v((MP, SP, CW), BF),
        resid=v((SP, D), F32), dresid=v((SP, D), F32), dh1=v((SP, D), F32),
        slot_out=v((DP, KE, D), F32), slot_in=v((DP, KE, D), F32),
        slot_all=v((MP, KE * DP, D), BF),
        part=v((MP, KE * DP, D), F32), psend=v((MP, KE * DP, D), BF), pin=v((MP, KE * DP, D), BF),
        back_out=v((DP, KE, D), F32), back_in=v((DP, KE, D), F32),
    )
    sems = dict(
        tok=(2, MP), cot=(2, MP), outs=(2, MP), ings=(2, MP), hbm=(2,),
        dp1=(2, DP), mp1=(2, 2, MP), mp2=(2, 2, MP), dp2=(2, DP),
    )
    if z.own_weights:
        items.update(
            wall=v((MP, NX, IN, RB, D), BF),
            gq=v((MP, NX, IN, RB, QW), BF), gp=v((NX, IN, RB, D), BF),
            cq=v((MP, NX, RB, QW), BF), cp=v((NX, RB, D), BF),
            xq=v((MP, NX, RB, QW), BF), xp=v((NX, RB, D), BF),
            aq=v((MP, 4, half, QW), BF), ap=v((4, half, D), BF),
            bq=v((MP, 2, half, QW), BF), bp=v((2, half, D), BF),
            dq=v((MP, 2, half, QW), BF), dp_=v((2, half, D), BF),
            zf=v((RB, D), F32), zs=v((MP, RB, D), BF), zr=v((5, RB, D), BF), fp=v((MP, RB, CW), F32),
            sa=v((DP, KE, D), F32), sb=v((DP, KE, D), F32), sc=v((MP, KE, D), F32), sd=v((DP, KE, D), F32),
            ta=v((2, D), F32), tb=v((DP, 2, D), F32), tc=v((MP, 2, D), F32),
        )
        sems.update(
            wz=(2, 5), wx=(2, MP, 4), wc=(2, MP),
            gc=(2, MP), gx=(2, MP, 6), gz=(2, 5), hc=(2,), hx=(2, 6),
            s1=(2, DP), s2=(2, MP), s3=(2, DP), t1=(2, DP), t2=(2, MP),
        )
    names, shapes = [], []
    for name, shape in items.items():
        names.append(name)
        shapes.append(shape)
    for name, shape in sems.items():
        names.append("m_" + name)
        shapes.append(dma(shape))
    return names, shapes


class Refs:
    pass


def block_kernel(z, in_names, out_names, names, *refs):
    r = Refs()
    for name, ref in zip(in_names + out_names + names, refs):
        setattr(r, name, ref)
    DP, MP, D, CW, RB, QW, SP = z.DP, z.MP, z.D, z.CW, z.RB, z.QW, z.SP
    NX, IN, E, EPD, KE = z.NX, z.IN, z.E, z.EPD, z.KE
    half = RB // 2
    dp, mp = lax.axis_index("dp"), lax.axis_index("mp")
    xy, co = dp // IN, lax.rem(dp, IN)
    xn = xy + 1 - 2 * lax.rem(xy, 2)
    yn = lax.rem(xy + 2, NX)
    dg = lax.rem(xn + 2, NX)
    to_x, to_y, to_core = (xn * IN + co, mp), (yn * IN + co, mp), (xy * IN + 1 - co, mp)
    sends = []

    def remote(src, dst, sem, s_at, r_at, device):
        return pltpu.make_async_remote_copy(
            src_ref=src, dst_ref=dst, send_sem=sem.at[(0,) + s_at], recv_sem=sem.at[(1,) + r_at],
            device_id=device, device_id_type=MESH,
        )

    def send(*copy):
        remote(*copy).start()
        sends.append(lambda: remote(*copy).wait_send())

    def arrive(ref, sem, at):
        remote(ref, ref, sem, at, at, to_mp(1)).wait_recv()

    def mp_at(k):
        if MP != 4:
            return lax.rem(mp + k, MP)
        return 2 * lax.rem(mp // 2 + k // 2, 2) + lax.rem(mp + k, 2)

    def mp_back(k):
        return k if MP == 4 else MP - k

    def dp_at(k):
        return lax.rem(dp + k, DP)

    def to_mp(k):
        return (dp, mp_at(k))

    def to_dp(k):
        return (dp_at(k), mp)

    barrier = pltpu.get_barrier_semaphore()
    for k in range(1, MP):
        pl.semaphore_signal(barrier, inc=1, device_id=to_mp(k), device_id_type=MESH)
    each(1, DP, lambda k: pl.semaphore_signal(barrier, inc=1, device_id=to_dp(k), device_id_type=MESH))

    load_in = pltpu.make_async_copy(r.w_in, r.wf_in, r.m_hbm.at[0])
    load_out = pltpu.make_async_copy(r.w_out, r.wf_out, r.m_hbm.at[1])
    load_in.start()
    load_out.start()

    if z.own_weights:
        r.wall[mp, xy, co] = jnp.concatenate(
            [r.w_qkv[c].astype(BF) for c in range(3)] + [r.w_proj[...].T.astype(BF)], axis=1
        )
    pl.semaphore_wait(barrier, MP - 1 + DP - 1)

    def to_images(source, target):
        target[...] = jnp.zeros((MP, SP, CW), BF)
        rows = source[...].T
        for i in range(MP):
            target[i, 0:SEQ, :] = rows[SEQ * i : SEQ * (i + 1)]

    def swap(src, dst, sem):
        for k in range(1, MP):
            send(src.at[mp_at(k)], dst.at[mp], sem, (k,), (mp_back(k),), to_mp(k))
        dst[mp] = src[mp]

    def swap_wait(dst, sem):
        for k in range(1, MP):
            arrive(dst.at[mp_at(k)], sem, (k,))

    def to_column(block, sem):
        for k in range(1, MP):
            send(block, block, sem, (k,), (mp_back(k),), to_mp(k))

    class Plane:
        def __init__(self, block, sem, at):
            self.block, self.sem, self.at = block, sem, at

        def copy(self, ref, way, device):
            send(ref, ref, self.sem, self.at + (way,), self.at + (way,), device)

        def start(self):
            self.copy(self.block(xy, 0, RB), 0, to_x)
            self.copy(self.block(xy, 0, RB), 1, to_y)

        def forward(self):
            arrive(self.block(xn, 0, RB), self.sem, self.at + (0,))
            self.copy(self.block(xn, 0, half), 2, to_y)
            arrive(self.block(yn, 0, RB), self.sem, self.at + (1,))
            self.copy(self.block(yn, half, half), 3, to_x)

        def wait(self):
            arrive(self.block(dg, 0, half), self.sem, self.at + (2,))
            arrive(self.block(dg, half, half), self.sem, self.at + (3,))

    middle = lax.rem((mp + 1) // 2, 2)
    slots_at = [0, 1, 2 + middle, 3 - middle]

    def column_copy(k, way, slot, target):
        block = r.wall.at[mp_at(k), xy, co]
        return remote(block, block, r.m_wz, (way,), (slot,), to_mp(target))

    def column_send(*copy):
        column_copy(*copy).start()
        sends.append(lambda: column_copy(*copy).wait_send())

    def column_pass(*copy):
        pl.when(middle == 1)(lambda: column_copy(*copy).start())
        sends.append(lambda: pl.when(middle == 1)(lambda: column_copy(*copy).wait_send()))

    def weight_plane(s):
        return Plane(lambda pos, low, rows: r.wall.at[mp_at(slots_at[s]), pos, co, pl.ds(low, rows)], r.m_wx, (s,))

    def load_expert(copy, wide, low):
        copy.wait()
        low[...] = wide[...].astype(BF)

    if z.own_weights:
        planes = [weight_plane(s) for s in range(MP)]

        def column_arrived(s, k, way, slot, target):
            arrive(r.wall.at[mp_at(slots_at[s]), xy, co], r.m_wz, (slots_at[s],))
            column_pass(k, way, slot, target)
            planes[s].start()

        def plane_arrived(s):
            planes[s].wait()
            block = r.wall.at[mp_at(slots_at[s]), :, co]
            send(block, block, r.m_wc, (s,), (s,), to_core)

        column_send(0, 0, 1, 1)
        column_pass(0, 1, 3, 3)
        planes[0].start()
        to_images(r.tokens, r.tsend)
        load_expert(load_in, r.wf_in, r.wb_in)
        column_arrived(1, 1, 2, 2, 3)
        planes[0].forward()
        to_images(r.cotangent, r.csend)
        column_arrived(2, 3, 3, 2, 1)
        planes[1].forward()
        plane_arrived(0)
        load_expert(load_out, r.wf_out, r.wb_out)
        column_arrived(3, 2, 4, 3, 1)
        swap(r.tsend, r.tin, r.m_tok)
        planes[2].forward()
        plane_arrived(1)
        planes[3].forward()
        swap(r.csend, r.cin, r.m_cot)
        plane_arrived(2)
    else:
        to_images(r.tokens, r.tsend)
        swap(r.tsend, r.tin, r.m_tok)
        to_images(r.cotangent, r.csend)
        swap(r.csend, r.cin, r.m_cot)
        load_expert(load_in, r.wf_in, r.wb_in)
        load_expert(load_out, r.wf_out, r.wb_out)

    swap_wait(r.tin, r.m_tok)
    gain1, shift1 = r.norm_params[0:1, :], r.norm_params[1:2, :]
    gain2, shift2 = r.norm_params[2:3, :], r.norm_params[3:4, :]

    def own_image(ref):
        return jnp.concatenate([ref[i] for i in range(MP)], axis=1)

    normed1, _ = normalize(own_image(r.tin).astype(F32))
    r.h1[...] = (normed1 * gain1 + shift1).astype(BF)

    scale = 1.0 / math.sqrt(HEAD_DIM)
    key_ok = lax.broadcasted_iota(jnp.int32, (1, SP), 1) < SEQ

    def weight(m):
        return r.wall[m].reshape(D, D)[:, :QW] if z.own_weights else r.wall[m]

    def proj_weight(m):
        return r.wall[m].reshape(D, D)[:, QW:] if z.own_weights else r.wpall[m]

    def head_cols(qkv, h):
        return (qkv[:, c * CW + h * HEAD_DIM : c * CW + (h + 1) * HEAD_DIM] for c in range(3))

    def heads_forward(s):
        m = mp_at(slots_at[s])
        if z.own_weights:
            arrive(r.wall.at[m, :, 1 - co], r.m_wc, (s,))
        qkv = nn(r.h1[...], weight(m)).astype(BF)
        r.qkv[m] = qkv
        if z.own_weights and s == MP - 2:
            plane_arrived(s + 1)
        attended = []
        for h in range(z.HL):
            query, key, value = head_cols(qkv, h)
            scores = jnp.where(key_ok, nt(query, key) * scale, NEG)
            top = jnp.max(scores, axis=-1, keepdims=True)
            grown = jnp.exp(scores - top)
            probs = grown / jnp.sum(grown, axis=-1, keepdims=True)
            r.probs[m, h] = probs
            attended.append(nn(probs.astype(BF), value))
        r.att[m] = jnp.concatenate(attended, axis=1).astype(BF)

    for s in range(MP):
        heads_forward(s)

    resid = own_image(r.tin).astype(F32)
    for m in range(MP):
        resid = resid + nt(r.att[m], proj_weight(m))
    r.resid[...] = resid
    normed2, inv2 = normalize(resid)
    h2 = (normed2 * gain2 + shift2).astype(BF)
    phi_low = r.phi[...].astype(BF)
    logits = nt(h2, phi_low)
    token_ok = lax.broadcasted_iota(jnp.int32, (SP, 1), 0) < SEQ
    masked = jnp.where(token_ok, logits, NEG)
    grown = jnp.exp(masked - jnp.max(masked, axis=0, keepdims=True))
    dispatch = grown / jnp.sum(grown, axis=0, keepdims=True)
    grown = jnp.exp(logits - jnp.max(logits, axis=1, keepdims=True))
    combine = grown / jnp.sum(grown, axis=1, keepdims=True)
    dispatch_low, combine_low = dispatch.astype(BF), combine.astype(BF)
    swap_wait(r.cin, r.m_cot)
    grad = own_image(r.cin)
    slots = tn(dispatch_low, h2).astype(BF)
    dresults = tn(combine_low, grad).astype(BF)

    def spread(target, rows):
        for d in range(DP):
            target[d] = rows[d * KE : (d + 1) * KE]

    def collect(source):
        return jnp.concatenate([source[d] for d in range(DP)], axis=0)

    def dp_swap(src, dst, sem):
        def copy(k):
            return remote(src.at[dp_at(k)], dst.at[dp], sem, (k,), (DP - k,), to_dp(k))

        each(1, DP, lambda k: copy(k).start())
        sends.append(lambda: each(1, DP, lambda k: copy(k).wait_send()))
        dst[dp] = src[dp]

    def dp_wait(dst, sem):
        each(1, DP, lambda k: arrive(dst.at[dp_at(k)], sem, (k,)))

    def out_row(row):
        d, q = row // KE, row % KE
        return (q // EPD) * E + d * EPD + q % EPD

    spread(r.slot_out, nn(select_rows(DP * KE, 2 * E, out_row), jnp.concatenate([slots, dresults], axis=0)))
    dp_swap(r.slot_out, r.slot_in, r.m_dp1)
    dp_wait(r.slot_in, r.m_dp1)
    gather_rows = select_rows(KE * DP, DP * KE, lambda row: (row % DP) * KE + row // DP)
    r.slot_all[mp] = nn(gather_rows, collect(r.slot_in).astype(BF)).astype(BF)
    rows = EPD * DP

    def kind_rows(ref, kind):
        return ref.at[pl.ds(kind * rows, rows)]

    for kind in range(2):
        for k in range(1, MP):
            block = kind_rows(r.slot_all.at[mp], kind)
            send(block, block, r.m_mp1, (kind, k), (kind, mp_back(k)), to_mp(k))

    def expert_rows(kind):
        for k in range(1, MP):
            arrive(kind_rows(r.slot_all.at[mp_at(k)], kind), r.m_mp1, (kind, k))
        parts = [r.slot_all[m, kind * rows : (kind + 1) * rows, :].astype(F32) for m in range(MP)]
        return [
            jnp.concatenate([one[e * DP : (e + 1) * DP] for one in parts], axis=0).astype(BF) for e in range(EPD)
        ]

    def send_parts(kind, per_expert):
        for e in range(EPD):
            at = kind * rows + e * DP
            for m in range(MP):
                r.part[m, at : at + DP, :] = per_expert[e][m * DP : (m + 1) * DP]
        here = slice(kind * rows, (kind + 1) * rows)
        r.psend[:, here, :] = r.part[:, here, :].astype(BF)
        for k in range(1, MP):
            send(
                kind_rows(r.psend.at[mp_at(k)], kind), kind_rows(r.pin.at[mp_back(k)], kind),
                r.m_mp2, (kind, k), (kind, mp_back(k)), to_mp(k),
            )

    slopes, results_part = [], []
    for e, slots_e in enumerate(expert_rows(0)):
        pre = nn(slots_e, r.wb_in[e])
        cdf = 0.5 * (1.0 + lax.erf(pre * (1.0 / math.sqrt(2.0))))
        hidden = (pre * cdf).astype(BF)
        results_part.append(nn(hidden, r.wb_out[e]))
        slopes.append(cdf + pre * jnp.exp(-0.5 * pre * pre) * (1.0 / math.sqrt(2.0 * math.pi)))
        r.slots[e], r.hidden[e] = slots_e, hidden
    send_parts(0, results_part)
    dslots_part = []
    for e, dresults_e in enumerate(expert_rows(1)):
        dpre = (nt(dresults_e, r.wb_out[e]) * slopes[e]).astype(BF)
        dslots_part.append(nt(dpre, r.wb_in[e]))
        r.dresults[e], r.dpre[e] = dresults_e, dpre
    send_parts(1, dslots_part)
    total = r.part[mp]
    for k in range(1, MP):
        for kind in range(2):
            arrive(kind_rows(r.pin.at[k], kind), r.m_mp2, (kind, k))
        total = total + r.pin[k].astype(F32)
    back_rows = select_rows(DP * KE, KE * DP, lambda row: (row % KE) * DP + row // KE)
    spread(r.back_out, nn(back_rows, total.astype(BF)))
    dp_swap(r.back_out, r.back_in, r.m_dp2)
    dp_wait(r.back_in, r.m_dp2)

    def result_row(row):
        kind, e = row // E, row % E
        return (e // EPD) * KE + kind * EPD + e % EPD

    both = nn(select_rows(2 * E, DP * KE, result_row), collect(r.back_in).astype(BF)).astype(BF)
    results, dslots = both[:E], both[E:]

    output = r.resid[...] + nn(combine_low, results)
    for m in range(MP):
        r.osend[m] = output[:, m * CW : (m + 1) * CW].astype(BF)
    swap(r.osend, r.oin, r.m_outs)
    dcombine, ddispatch = nt(grad, results), nt(h2, dslots)
    dlogits = dispatch * (ddispatch - jnp.sum(dispatch * ddispatch, axis=0, keepdims=True))
    dlogits = dlogits + combine * (dcombine - jnp.sum(combine * dcombine, axis=1, keepdims=True))
    dlogits = dlogits.astype(BF)
    dh2 = nn(dispatch_low, dslots) + nn(dlogits, phi_low)
    dresid = grad.astype(F32) + norm_backward(dh2, gain2, normed2, inv2)
    r.dresid[...] = dresid
    dbranch = dresid.astype(BF)
    proj_part = tn(dbranch, own_image(r.att)).astype(BF)

    class Unit:
        def __init__(self, part, got, mine, first, out, second, core_sem, sem, at):
            self.part, self.got, self.mine, self.first = part, got, mine, first
            self.out, self.second, self.core_sem, self.sem, self.at = out, second, core_sem, sem, at

        def start(self):
            send(self.part.at[:, 1 - co], self.got, self.core_sem, self.at, self.at, to_core)

        def copy(self, src, dst, way, device):
            send(src, dst, self.sem, self.at + (way,), self.at + (way,), device)

        def plane(self):
            arrive(self.got, self.core_sem, self.at)
            for x in range(NX):
                self.mine[x] = (self.part[x, co].astype(F32) + self.got[x].astype(F32)).astype(BF)
            low, high = pl.ds(0, half), pl.ds(half, half)
            self.copy(self.mine.at[dg, low], self.first.at[1], 1, to_x)
            self.copy(self.mine.at[dg, high], self.first.at[3], 3, to_y)
            self.copy(self.mine.at[xn, low], self.first.at[0], 0, to_x)
            self.copy(self.mine.at[yn, high], self.first.at[2], 2, to_y)

        def added(self, x, low, index):
            arrive(self.first.at[index], self.sem, self.at + (index,))
            return self.mine[x, low : low + half, :].astype(F32) + self.first[index].astype(F32)

        def forward(self):
            self.out[0] = self.added(yn, 0, 1).astype(BF)
            self.copy(self.out.at[0], self.second.at[0], 4, to_y)
            self.out[1] = self.added(xn, half, 3).astype(BF)
            self.copy(self.out.at[1], self.second.at[1], 5, to_x)

        def total(self):
            pieces = []
            for i in range(2):
                piece = self.added(xy, i * half, 2 * i)
                arrive(self.second.at[i], self.sem, self.at + (4 + i,))
                pieces.append(piece + self.second[i].astype(F32))
            return jnp.concatenate(pieces, axis=0)

    orders = [2 + middle, 3 - middle, 1, 0]

    def qkv_unit(i):
        m = mp_at(orders[i])
        return Unit(r.gq.at[m], r.cq.at[i], r.xq.at[i], r.aq.at[i], r.bq.at[i], r.dq.at[i], r.m_gc, r.m_gx, (i,))

    def column_slot(i):
        return (i + 3 * middle,) if i < 2 else (2,)

    def from_line(index):
        arrive(r.zr.at[index], r.m_gz, (index,))
        return r.zr[index].astype(F32)

    def unit_total(i):
        return jnp.concatenate([units[i].total(), r.fp[mp_at(orders[i])]], axis=1)

    def column(i):
        r.zf[...] = unit_total(i)

        @pl.when(middle == 1)
        def _():
            r.zf[...] += from_line([0, 1, 4][i])

        r.zs[i] = r.zf[...].astype(BF)
        target = 1 if i == 2 else 1 + 2 * middle
        at = column_slot(i)

        def copy():
            return pltpu.make_async_remote_copy(
                src_ref=r.zs.at[i], dst_ref=r.zr.at[at[0]], send_sem=r.m_gz.at[0, i], recv_sem=r.m_gz.at[1, at[0]],
                device_id=to_mp(target), device_id_type=MESH,
            )

        copy().start()
        sends.append(lambda: copy().wait_send())

    def column_own():
        r.zf[...] = unit_total(MP - 1) + from_line(2)

        @pl.when(middle == 1)
        def _():
            r.zf[...] += from_line(3)

        for c in range(3):
            r.qkv_grad[c] = r.zf[:, c * CW : (c + 1) * CW]
        r.proj_grad[...] = r.zf[:, QW:].T

    def proj_total():
        total = proj_unit.total()
        for m in range(MP):
            r.fp[m] = total[:, m * CW : (m + 1) * CW]

    def sum_of(ref, count):
        total = ref[0]
        for i in range(1, count):
            total = total + ref[i]
        return total

    def small_column():
        dp_wait(r.sb, r.m_s1)
        r.sc[mp] = sum_of(r.sb, DP)
        to_column(r.sc.at[mp], r.m_s2)

    def small_back():
        for k in range(1, MP):
            arrive(r.sc.at[mp_at(k)], r.m_s2, (k,))
        r.sd[dp] = sum_of(r.sc, MP)
        for k in range(1, DP):
            send(r.sd.at[dp], r.sd.at[dp], r.m_s3, (k,), (DP - k,), to_dp(k))

    def gains(grad_out, normed):
        return jnp.concatenate(
            [jnp.sum(grad_out * normed, axis=0, keepdims=True), jnp.sum(grad_out, axis=0, keepdims=True)], axis=0
        )

    if z.own_weights:
        units = [qkv_unit(i) for i in range(MP)]
        proj_unit = Unit(r.gp, r.cp, r.xp, r.ap, r.bp, r.dp_, r.m_hc, r.m_hx, ())
        r.gp[...] = proj_part.reshape(NX, IN, RB, D)
        proj_unit.start()
    else:
        r.gp[...] = proj_part
    for m in range(MP):
        r.datt[m] = nn(dbranch, proj_weight(m)).astype(BF)
    rows2 = gains(dh2, normed2)
    if z.own_weights:
        phi_part = tn(dlogits, h2)
        r.sa[...] = jnp.zeros((DP, KE, D), F32)
        for i in range(E // KE):
            r.sa[i] = phi_part[i * KE : (i + 1) * KE]
        r.sa[E // KE, 0:2, :] = rows2
        dp_swap(r.sa, r.sb, r.m_s1)
    else:
        r.phi_grad[...] = tn(dlogits, h2)

    def heads_backward(m):
        qkv, datt = r.qkv[m], r.datt[m]
        pieces = [[], [], []]
        for h in range(z.HL):
            query, key, value = head_cols(qkv, h)
            grad_h = datt[:, h * HEAD_DIM : (h + 1) * HEAD_DIM]
            probs = r.probs[m, h]
            dprobs = nt(grad_h, value)
            dscores = probs * (dprobs - jnp.sum(probs * dprobs, axis=-1, keepdims=True))
            dscores = dscores.astype(BF)
            pieces[0].append(nn(dscores, key) * scale)
            pieces[1].append(tn(dscores, query) * scale)
            pieces[2].append(tn(probs.astype(BF), grad_h))
        dqkv = jnp.concatenate(pieces[0] + pieces[1] + pieces[2], axis=1).astype(BF)
        piece = tn(r.h1[...], dqkv).astype(BF)
        if z.own_weights:
            r.gq[m] = piece.reshape(NX, IN, RB, QW)
        else:
            r.gq[m] = piece
        return dqkv

    between = {}
    if z.own_weights:
        first, second, third, last = units
        between = {0: [proj_unit.plane], 1: [first.plane], 2: [second.plane, proj_unit.forward], 3: [third.plane]}
    for i in range(MP):
        m = mp_at(orders[i] if MP == 4 else i)
        dqkv = heads_backward(m)
        if z.own_weights:
            units[i].start()
        part = nt(dqkv, weight(m))
        if i == 0:
            r.dh1[...] = part
        else:
            r.dh1[...] += part
        for step in between.get(i, []):
            step()

    normed1, inv1 = normalize(own_image(r.tin).astype(F32))
    dh1 = r.dh1[...]
    input_grad = r.dresid[...] + norm_backward(dh1, gain1, normed1, inv1)
    for m in range(MP):
        r.isend[m] = input_grad[:, m * CW : (m + 1) * CW].astype(BF)
    swap(r.isend, r.iin, r.m_ings)
    rows1 = gains(dh1, normed1)
    if z.own_weights:
        r.ta[...] = rows1
        for k in range(1, DP):
            send(r.ta, r.tb.at[dp], r.m_t1, (k,), (DP - k,), to_dp(k))
        r.tb[dp] = rows1

    if z.own_weights:
        first.forward()
        last.plane()
        second.forward()
        third.forward()
        proj_total()
        column(0)
        last.forward()
        small_column()
        column(1)
        small_back()
        dp_wait(r.tb, r.m_t1)
        r.tc[mp] = sum_of(r.tb, DP)
        to_column(r.tc.at[mp], r.m_t2)
    swap_wait(r.oin, r.m_outs)
    r.output[...] = from_images(r.oin)
    if z.own_weights:
        column(2)
        dp_wait(r.sd, r.m_s3)
        for i in range(E // KE):
            r.phi_grad[i * KE : (i + 1) * KE, :] = r.sd[i]
        column_own()
        for k in range(1, MP):
            arrive(r.tc.at[mp_at(k)], r.m_t2, (k,))
        r.norm_grad[...] = jnp.concatenate([sum_of(r.tc, MP), r.sd[E // KE, 0:2, :]], axis=0)
    else:
        r.norm_grad[...] = jnp.concatenate([rows1, rows2], axis=0)
    swap_wait(r.iin, r.m_ings)

    for wait in sends:
        wait()


def from_images(source):
    images = [source[i, 0:SEQ, :].astype(F32) for i in range(source.shape[0])]
    return jnp.concatenate(images, axis=0).T


def finish_kernel(passed, slots, dpre, hidden, dresults, iin, *refs):
    sources, (in_grad, out_grad, input_grad), rest = refs[:passed], refs[passed : passed + 3], refs[passed + 3 :]
    targets, (grads_in, grads_out, grad_t, sem, tile_sem) = rest[:passed], rest[passed:]
    copies = [pltpu.make_async_copy(a, b, sem.at[i]) for i, (a, b) in enumerate(zip(sources, targets))]
    for copy in copies:
        copy.start()
    experts, _, width = slots.shape
    tile = 256 if width % 256 == 0 else width
    count = 0
    for e in range(experts):
        for left, right, held, target in ((slots, dpre, grads_in, in_grad), (hidden, dresults, grads_out, out_grad)):
            for t in range(width // tile):
                here = pl.ds(t * tile, tile)
                held[e, here, :] = tn(left[e, :, t * tile : (t + 1) * tile], right[e])
                copy = pltpu.make_async_copy(held.at[e, here], target.at[e, here], tile_sem.at[count])
                copy.start()
                copies.append(copy)
                count += 1
    grad_t[...] = from_images(iin)
    last = pltpu.make_async_copy(grad_t, input_grad, sem.at[passed])
    last.start()
    for copy in copies + [last]:
        copy.wait()


def per_device(mesh, tokens, norm_params, w_qkv, w_proj, phi, w_in, w_out, cotangent):
    z = Sizes(mesh, tokens, w_qkv, phi, w_in)
    vmem, anyspace = pl.BlockSpec(memory_space=pltpu.VMEM), pl.BlockSpec(memory_space=pl.ANY)
    inputs = dict(
        tokens=tokens.T, norm_params=norm_params, w_qkv=w_qkv, w_proj=w_proj, phi=phi.T, cotangent=cotangent.T
    )
    specs = [vmem] * len(inputs)
    inputs.update(w_in=w_in, w_out=w_out)
    specs += [anyspace] * 2
    images = z.MP * z.DP
    outs = dict(
        output=((z.CW, z.ROWS), F32), iin=((z.MP, z.SP, z.CW), BF),
        phi_grad=((z.E, z.D), F32), norm_grad=((4, z.D), F32),
        slots=((z.EPD, images, z.D), BF), dresults=((z.EPD, images, z.D), BF),
        hidden=((z.EPD, images, z.F), BF), dpre=((z.EPD, images, z.F), BF),
    )
    if z.own_weights:
        outs.update(qkv_grad=((3, z.RB, z.CW), F32), proj_grad=((z.CW, z.RB), F32))
    else:
        outs.update(gq=((z.MP, z.D, z.QW), BF), gp=((z.D, z.D), BF))
        wall = lax.all_gather(w_qkv.astype(BF), "dp", axis=1, tiled=True)
        wall = jnp.concatenate([wall[c] for c in range(3)], axis=1)
        wpall = lax.all_gather(w_proj.T.astype(BF), "dp", axis=0, tiled=True)
        inputs.update(wall=lax.all_gather(wall, "mp"), wpall=lax.all_gather(wpall, "mp"))
        specs += [vmem] * 2
    names, scratch = scratch_of(z)
    result = pl.pallas_call(
        functools.partial(block_kernel, z, list(inputs), list(outs), names),
        out_shape=[jax.ShapeDtypeStruct(*one) for one in outs.values()],
        in_specs=specs,
        out_specs=[vmem] * len(outs),
        scratch_shapes=scratch,
        compiler_params=pltpu.CompilerParams(
            collective_id=0, has_side_effects=True, vmem_limit_bytes=62 * 2**20
        ),
        name="block",
    )(*inputs.values())
    got = dict(zip(outs, result))

    passed = ["output", "norm_grad", "phi_grad"] + (["qkv_grad", "proj_grad"] if z.own_weights else [])
    tile = 256 if z.F % 256 == 0 and z.D == z.F else z.F
    tiles = 2 * z.EPD * (z.F // tile)
    results = pl.pallas_call(
        functools.partial(finish_kernel, len(passed)),
        in_specs=[vmem] * (5 + len(passed)),
        out_specs=[anyspace] * (3 + len(passed)),
        out_shape=[
            jax.ShapeDtypeStruct((z.EPD, z.D, z.F), F32),
            jax.ShapeDtypeStruct((z.EPD, z.F, z.D), F32),
            jax.ShapeDtypeStruct((z.CW, z.ROWS), F32),
        ]
        + [jax.ShapeDtypeStruct(*outs[name]) for name in passed],
        scratch_shapes=[
            pltpu.VMEM((z.EPD, z.D, z.F), F32),
            pltpu.VMEM((z.EPD, z.F, z.D), F32),
            pltpu.VMEM((z.CW, z.ROWS), F32),
            pltpu.SemaphoreType.DMA((len(passed) + 1,)),
            pltpu.SemaphoreType.DMA((tiles,)),
        ],
        compiler_params=pltpu.CompilerParams(vmem_limit_bytes=60 * 2**20),
        name="finish",
    )(got["slots"], got["dpre"], got["hidden"], got["dresults"], got["iin"], *(got[name] for name in passed))
    in_grad, out_grad, input_grad = results[:3]
    got.update(zip(passed, results[3:]))
    output, input_grad = got["output"].T, input_grad.T
    phi_grad, norm_grad = got["phi_grad"].T, got["norm_grad"]
    if z.own_weights:
        qkv_grad, proj_grad = got["qkv_grad"], got["proj_grad"]
    else:
        phi_grad, norm_grad = lax.psum((phi_grad, norm_grad), ("dp", "mp"))
        gq = lax.psum_scatter(got["gq"].astype(F32), "mp", scatter_dimension=0, tiled=False)
        gp = lax.psum_scatter(got["gp"].astype(F32), "mp", scatter_dimension=1, tiled=True)
        gq = jnp.stack([gq[:, c * z.CW : (c + 1) * z.CW] for c in range(3)])
        qkv_grad = lax.psum_scatter(gq, "dp", scatter_dimension=1, tiled=True)
        proj_grad = lax.psum_scatter(gp, "dp", scatter_dimension=0, tiled=True).T
    return (
        output, input_grad, qkv_grad, proj_grad, in_grad, out_grad, phi_grad, norm_grad
    )


def solution(mesh):
    return jax.shard_map(
        functools.partial(per_device, mesh),
        mesh=mesh,
        in_specs=(
            P("dp", "mp"), P(), P(None, "dp", "mp"), P("mp", "dp"), P(),
            P("dp", None, "mp"), P("dp", "mp", None), P("dp", "mp"),
        ),
        out_specs=(
            P("dp", "mp"), P("dp", "mp"), P(None, "dp", "mp"), P("mp", "dp"),
            P("dp", None, "mp"), P("dp", "mp", None), P(), P(),
        ),
        check_vma=False,
    )
```

```python
import functools
import math

import jax
import jax.numpy as jnp
from jax import lax
from jax.experimental import pallas as pl
from jax.experimental.pallas import tpu as pltpu
from jax.sharding import PartitionSpec as P

HEAD_DIM = 64
SEQ = 196
EPSILON = 1e-06
MESH = pl.DeviceIdType.MESH
BF = jnp.bfloat16
F32 = jnp.float32
NEG = -1e30


def nn(a, b):
    return lax.dot_general(a, b, (((1,), (0,)), ((), ())), preferred_element_type=F32)


def nt(a, b):
    return lax.dot_general(a, b, (((1,), (1,)), ((), ())), preferred_element_type=F32)


def tn(a, b):
    return lax.dot_general(a, b, (((0,), (0,)), ((), ())), preferred_element_type=F32)


def each(low, high, body):
    if high - low <= 32:
        for i in range(low, high):
            body(i)
    else:

        def step(i, carry):
            body(i)
            return carry

        lax.fori_loop(low, high, step, 0)


def select_rows(rows, cols, source):
    row = lax.broadcasted_iota(jnp.int32, (rows, cols), 0)
    col = lax.broadcasted_iota(jnp.int32, (rows, cols), 1)
    return jnp.where(col == source(row), 1.0, 0.0).astype(BF)


def normalize(values):
    mean = jnp.mean(values, axis=-1, keepdims=True)
    centered = values - mean
    var = jnp.mean(centered * centered, axis=-1, keepdims=True)
    inv = lax.rsqrt(var + EPSILON)
    return centered * inv, inv


def norm_backward(grad, gain, normed, inv):
    scaled = grad * gain
    first = jnp.mean(scaled, axis=-1, keepdims=True)
    second = jnp.mean(scaled * normed, axis=-1, keepdims=True)
    return inv * (scaled - first - normed * second)


class Sizes:
    def __init__(self, mesh, tokens, w_qkv, phi, w_in):
        self.DP, self.MP = mesh.shape["dp"], mesh.shape["mp"]
        self.D, self.E = phi.shape
        self.CW = tokens.shape[1]
        self.RB = w_qkv.shape[1]
        self.QW = 3 * self.CW
        self.HL = self.CW // HEAD_DIM
        self.EPD = w_in.shape[0]
        self.F = w_in.shape[2]
        self.IN = 2
        self.NX = self.DP // self.IN
        self.SP = (SEQ + 15) // 16 * 16
        self.ROWS = tokens.shape[0]
        self.KE = 2 * self.EPD
        self.NS = self.DP * self.MP
        self.LC = self.D // 128
        self.Q = self.EPD * self.LC
        self.QP = (self.Q + 15) // 16 * 16
        self.GD = 8 if self.DP % 8 == 0 else self.DP
        self.GS = self.GD * self.MP
        self.own_weights = self.MP == 4 and self.NX == 4 and self.RB % 32 == 0 and self.E + 2 <= self.KE * self.DP


def scratch_of(z):
    dma = pltpu.SemaphoreType.DMA
    v = pltpu.VMEM
    DP, MP, D, CW, RB, QW, SP, NX, IN, KE = z.DP, z.MP, z.D, z.CW, z.RB, z.QW, z.SP, z.NX, z.IN, z.KE
    half = RB // 2
    items = dict(
        tsend=v((MP, SP, CW), BF), tin=v((MP, SP, CW), BF),
        csend=v((MP, SP, CW), BF), cin=v((MP, SP, CW), BF),
        osend=v((MP, SP, CW), BF), oin=v((MP, SP, CW), BF),
        isend=v((MP, SP, CW), BF),
        wf_in=v((z.EPD, D, z.F), F32), wf_out=v((z.EPD, z.F, D), F32),
        wb_in=v((z.EPD, D, z.F), BF), wb_out=v((z.EPD, z.F, D), BF),
        h1=v((SP, D), BF), qkv=v((MP, SP, QW), BF), probs=v((MP, z.HL, SP, SP), F32),
        att=v((MP, SP, CW), BF), datt=v((MP, SP, CW), BF),
        resid=v((SP, D), F32), dresid=v((SP, D), F32), dh1=v((SP, D), F32),
        slot_out=v((2, DP, z.QP, 128), BF), slot_in=v((2, z.NS, z.QP, 128), BF),
        back_out=v((2, z.NS, z.QP, 128), BF), back_in=v((2, z.NS, z.QP, 128), BF),
        pick_in=v((z.Q * z.GS, z.GS * z.QP), BF), pick_back=v((z.GS * z.QP, z.Q * z.GS), BF),
        pick_sum=v((z.LC * z.GD * z.EPD, z.GS * z.QP), BF),
    )
    sems = dict(
        tok=(2, MP), cot=(2, MP), outs=(2, MP), ings=(2, MP), hbm=(2,),
        slot=(2, 2), back=(2, 2),
    )
    if z.own_weights:
        items.update(
            wall=v((MP, NX, IN, RB, D), BF),
            gq=v((MP, NX, IN, RB, QW), BF), gp=v((NX, IN, RB, D), BF),
            cq=v((MP, NX, RB, QW), BF), cp=v((NX, RB, D), BF),
            xq=v((MP, NX, RB, QW), BF), xp=v((NX, RB, D), BF),
            aq=v((MP, 4, half, QW), BF), ap=v((4, half, D), BF),
            bq=v((MP, 2, half, QW), BF), bp=v((2, half, D), BF),
            dq=v((MP, 2, half, QW), BF), dp_=v((2, half, D), BF),
            zf=v((RB, D), F32), zs=v((MP, RB, D), BF), zr=v((5, RB, D), BF), fp=v((MP, RB, CW), F32),
            sa=v((DP, KE, D), F32), sb=v((DP, KE, D), F32), sc=v((MP, KE, D), F32), sd=v((DP, KE, D), F32),
            ta=v((2, D), F32), tb=v((DP, 2, D), F32), tc=v((MP, 2, D), F32),
        )
        sems.update(
            wz=(2, 5), wx=(2, MP, 4), wc=(2, MP),
            gc=(2, MP), gx=(2, MP, 6), gz=(2, 5), hc=(2,), hx=(2, 6),
            s1=(2, DP), s2=(2, MP), s3=(2, DP), t1=(2, DP), t2=(2, MP),
        )
    names, shapes = [], []
    for name, shape in items.items():
        names.append(name)
        shapes.append(shape)
    for name, shape in sems.items():
        names.append("m_" + name)
        shapes.append(dma(shape))
    names.append("entered")
    shapes.append(pltpu.SemaphoreType.REGULAR)
    return names, shapes


class Refs:
    pass


def block_kernel(z, in_names, out_names, names, *refs):
    r = Refs()
    for name, ref in zip(in_names + out_names + names, refs):
        setattr(r, name, ref)
    DP, MP, D, CW, RB, QW, SP = z.DP, z.MP, z.D, z.CW, z.RB, z.QW, z.SP
    NX, IN, E, EPD, KE = z.NX, z.IN, z.E, z.EPD, z.KE
    half = RB // 2
    dp, mp = lax.axis_index("dp"), lax.axis_index("mp")
    xy, co = dp // IN, lax.rem(dp, IN)
    xn = xy + 1 - 2 * lax.rem(xy, 2)
    yn = lax.rem(xy + 2, NX)
    dg = lax.rem(xn + 2, NX)
    to_x, to_y, to_core = (xn * IN + co, mp), (yn * IN + co, mp), (xy * IN + 1 - co, mp)
    sends = []

    def remote(src, dst, sem, s_at, r_at, device):
        return pltpu.make_async_remote_copy(
            src_ref=src, dst_ref=dst, send_sem=sem.at[(0,) + s_at], recv_sem=sem.at[(1,) + r_at],
            device_id=device, device_id_type=MESH,
        )

    def send(*copy):
        remote(*copy).start()
        sends.append(lambda: remote(*copy).wait_send())

    def arrive(ref, sem, at):
        remote(ref, ref, sem, at, at, to_mp(1)).wait_recv()

    def mp_at(k):
        if MP != 4:
            return lax.rem(mp + k, MP)
        return 2 * lax.rem(mp // 2 + k // 2, 2) + lax.rem(mp + k, 2)

    def mp_back(k):
        return k if MP == 4 else MP - k

    def dp_at(k):
        return lax.rem(dp + k, DP)

    def to_mp(k):
        return (dp, mp_at(k))

    def to_dp(k):
        return (dp_at(k), mp)

    def to_any(k):
        if isinstance(k, int):
            return (dp_at(k // MP), lax.rem(mp + k % MP, MP))
        return (dp_at(k // MP), lax.rem(mp + lax.rem(k, MP), MP))

    barrier = pltpu.get_barrier_semaphore()
    if z.own_weights:
        for k in range(1, MP):
            pl.semaphore_signal(barrier, inc=1, device_id=to_mp(k), device_id_type=MESH)
        each(1, DP, lambda k: pl.semaphore_signal(barrier, inc=1, device_id=to_dp(k), device_id_type=MESH))
    else:
        each(1, z.NS, lambda k: pl.semaphore_signal(barrier, inc=1, device_id=to_any(k), device_id_type=MESH))

    load_in = pltpu.make_async_copy(r.w_in, r.wf_in, r.m_hbm.at[0])
    load_out = pltpu.make_async_copy(r.w_out, r.wf_out, r.m_hbm.at[1])
    load_in.start()
    load_out.start()

    if z.own_weights:
        r.wall[mp, xy, co] = jnp.concatenate(
            [r.w_qkv[c].astype(BF) for c in range(3)] + [r.w_proj[...].T.astype(BF)], axis=1
        )
    pl.semaphore_wait(barrier, MP - 1 + DP - 1 if z.own_weights else z.NS - 1)
    if z.own_weights:
        for k in range(1, MP):
            pl.semaphore_signal(r.entered, inc=1, device_id=to_mp(k), device_id_type=MESH)

    def to_images(source, target):
        target[...] = jnp.zeros((MP, SP, CW), BF)
        rows = source[...].T
        for i in range(MP):
            target[i, 0:SEQ, :] = rows[SEQ * i : SEQ * (i + 1)]

    def swap(src, dst, sem):
        for k in range(1, MP):
            send(src.at[mp_at(k)], dst.at[mp], sem, (k,), (mp_back(k),), to_mp(k))
        dst[mp] = src[mp]

    def swap_wait(dst, sem):
        for k in range(1, MP):
            arrive(dst.at[mp_at(k)], sem, (k,))

    def to_column(block, sem):
        for k in range(1, MP):
            send(block, block, sem, (k,), (mp_back(k),), to_mp(k))

    class Plane:
        def __init__(self, block, sem, at):
            self.block, self.sem, self.at = block, sem, at

        def copy(self, ref, way, device):
            send(ref, ref, self.sem, self.at + (way,), self.at + (way,), device)

        def start(self):
            self.copy(self.block(xy, 0, RB), 0, to_x)
            self.copy(self.block(xy, 0, RB), 1, to_y)

        def forward(self):
            arrive(self.block(xn, 0, RB), self.sem, self.at + (0,))
            self.copy(self.block(xn, 0, half), 2, to_y)
            arrive(self.block(yn, 0, RB), self.sem, self.at + (1,))
            self.copy(self.block(yn, half, half), 3, to_x)

        def wait(self):
            arrive(self.block(dg, 0, half), self.sem, self.at + (2,))
            arrive(self.block(dg, half, half), self.sem, self.at + (3,))

    middle = lax.rem((mp + 1) // 2, 2)
    slots_at = [0, 1, 2 + middle, 3 - middle]

    def column_copy(k, way, slot, target):
        block = r.wall.at[mp_at(k), xy, co]
        return remote(block, block, r.m_wz, (way,), (slot,), to_mp(target))

    def column_send(*copy):
        column_copy(*copy).start()
        sends.append(lambda: column_copy(*copy).wait_send())

    def column_pass(*copy):
        pl.when(middle == 1)(lambda: column_copy(*copy).start())
        sends.append(lambda: pl.when(middle == 1)(lambda: column_copy(*copy).wait_send()))

    def weight_plane(s):
        return Plane(lambda pos, low, rows: r.wall.at[mp_at(slots_at[s]), pos, co, pl.ds(low, rows)], r.m_wx, (s,))

    def load_expert(copy, wide, low):
        copy.wait()
        low[...] = wide[...].astype(BF)


    def make_picks():
        GS, Q, QP, LC = z.GS, z.Q, z.QP, z.LC
        r.pick_in[...] = select_rows(Q * GS, GS * QP, lambda row: (row % GS) * QP + row // GS)
        r.pick_back[...] = select_rows(
            GS * QP, Q * GS, lambda row: jnp.where(row % QP < Q, (row % QP) * GS + row // QP, -1)
        )
        shape = (LC * z.GD * EPD, GS * QP)
        row, col = (lax.broadcasted_iota(jnp.int32, shape, i) for i in range(2))
        expert, chunk = row % (z.GD * EPD), row // (z.GD * EPD)
        wanted = (col // (QP * MP) == expert // EPD) & (col % QP == (expert % EPD) * LC + chunk)
        r.pick_sum[...] = jnp.where(wanted, 1.0, 0.0).astype(BF)

    if z.own_weights:
        planes = [weight_plane(s) for s in range(MP)]

        def column_arrived(s, k, way, slot, target):
            arrive(r.wall.at[mp_at(slots_at[s]), xy, co], r.m_wz, (slots_at[s],))
            column_pass(k, way, slot, target)
            planes[s].start()

        def plane_arrived(s):
            planes[s].wait()
            block = r.wall.at[mp_at(slots_at[s]), :, co]
            send(block, block, r.m_wc, (s,), (s,), to_core)

        column_send(0, 0, 1, 1)
        column_pass(0, 1, 3, 3)
        planes[0].start()
        to_images(r.tokens, r.tsend)
        load_expert(load_in, r.wf_in, r.wb_in)
        column_arrived(1, 1, 2, 2, 3)
        planes[0].forward()
        to_images(r.cotangent, r.csend)
        column_arrived(2, 3, 3, 2, 1)
        planes[1].forward()
        plane_arrived(0)
        load_expert(load_out, r.wf_out, r.wb_out)
        make_picks()
        column_arrived(3, 2, 4, 3, 1)
        swap(r.tsend, r.tin, r.m_tok)
        planes[2].forward()
        plane_arrived(1)
        planes[3].forward()
        swap(r.csend, r.cin, r.m_cot)
        plane_arrived(2)
    else:
        to_images(r.tokens, r.tsend)
        swap(r.tsend, r.tin, r.m_tok)
        to_images(r.cotangent, r.csend)
        swap(r.csend, r.cin, r.m_cot)
        load_expert(load_in, r.wf_in, r.wb_in)
        load_expert(load_out, r.wf_out, r.wb_out)
        make_picks()

    swap_wait(r.tin, r.m_tok)
    gain1, shift1 = r.norm_params[0:1, :], r.norm_params[1:2, :]
    gain2, shift2 = r.norm_params[2:3, :], r.norm_params[3:4, :]

    def own_image(ref):
        return jnp.concatenate([ref[i] for i in range(MP)], axis=1)

    normed1, _ = normalize(own_image(r.tin).astype(F32))
    r.h1[...] = (normed1 * gain1 + shift1).astype(BF)

    scale = 1.0 / math.sqrt(HEAD_DIM)
    key_ok = lax.broadcasted_iota(jnp.int32, (1, SP), 1) < SEQ

    def weight(m):
        return r.wall[m].reshape(D, D)[:, :QW] if z.own_weights else r.wall[m]

    def proj_weight(m):
        return r.wall[m].reshape(D, D)[:, QW:] if z.own_weights else r.wpall[m]

    def head_cols(qkv, h):
        return (qkv[:, c * CW + h * HEAD_DIM : c * CW + (h + 1) * HEAD_DIM] for c in range(3))

    def heads_forward(s):
        m = mp_at(slots_at[s])
        if z.own_weights:
            arrive(r.wall.at[m, :, 1 - co], r.m_wc, (s,))
        qkv = nn(r.h1[...], weight(m)).astype(BF)
        r.qkv[m] = qkv
        if z.own_weights and s == MP - 2:
            plane_arrived(s + 1)
        attended = []
        for h in range(z.HL):
            query, key, value = head_cols(qkv, h)
            scores = jnp.where(key_ok, nt(query, key) * scale, NEG)
            top = jnp.max(scores, axis=-1, keepdims=True)
            grown = jnp.exp(scores - top)
            probs = grown / jnp.sum(grown, axis=-1, keepdims=True)
            r.probs[m, h] = probs
            attended.append(nn(probs.astype(BF), value))
        r.att[m] = jnp.concatenate(attended, axis=1).astype(BF)

    for s in range(MP):
        heads_forward(s)

    resid = own_image(r.tin).astype(F32)
    for m in range(MP):
        resid = resid + nt(r.att[m], proj_weight(m))
    r.resid[...] = resid
    normed2, inv2 = normalize(resid)
    h2 = (normed2 * gain2 + shift2).astype(BF)
    phi_low = r.phi[...].astype(BF)
    logits = nt(h2, phi_low)
    token_ok = lax.broadcasted_iota(jnp.int32, (SP, 1), 0) < SEQ
    masked = jnp.where(token_ok, logits, NEG)
    grown = jnp.exp(masked - jnp.max(masked, axis=0, keepdims=True))
    dispatch = grown / jnp.sum(grown, axis=0, keepdims=True)
    grown = jnp.exp(logits - jnp.max(logits, axis=1, keepdims=True))
    combine = grown / jnp.sum(grown, axis=1, keepdims=True)
    dispatch_low, combine_low = dispatch.astype(BF), combine.astype(BF)
    slots = tn(dispatch_low, h2).astype(BF)

    GD, GS, Q, QP, LC = z.GD, z.GS, z.Q, z.QP, z.LC
    groups = DP // GD
    here = dp * MP + mp

    def stack(rows):
        return jnp.concatenate([rows[:, c * 128 : (c + 1) * 128] for c in range(LC)], axis=0)

    def unstack(chunks):
        count = chunks.shape[0] // LC
        return jnp.concatenate([chunks[c * count : (c + 1) * count] for c in range(LC)], axis=1)

    def exchange(source, dst, kind, sem):
        def copy(k):
            device = to_any(k)
            return pltpu.make_async_remote_copy(
                src_ref=source(*device), dst_ref=dst.at[kind, here], send_sem=sem.at[0, kind],
                recv_sem=sem.at[1, kind], device_id=device, device_id_type=MESH,
            )

        each(1, z.NS, lambda k: copy(k).start())
        all_of_them = dst.at[kind, pl.ds(0, z.NS - 1)]
        sends.append(
            lambda: pltpu.make_async_remote_copy(
                src_ref=all_of_them, dst_ref=all_of_them, send_sem=sem.at[0, kind], recv_sem=sem.at[1, kind],
                device_id=to_mp(1), device_id_type=MESH,
            ).wait_send()
        )

    def exchange_wait(dst, kind, sem):
        all_of_them = dst.at[kind, pl.ds(0, z.NS - 1)]
        pltpu.make_async_remote_copy(
            src_ref=all_of_them, dst_ref=all_of_them, send_sem=sem.at[0, kind], recv_sem=sem.at[1, kind],
            device_id=to_mp(1), device_id_type=MESH,
        ).wait_recv()

    def out_row(row):
        d, q = row // QP, row % QP
        return jnp.where(q < Q, (q % LC) * (GD * EPD) + d * EPD + q // LC, -1)

    pick_out = select_rows(GD * QP, LC * GD * EPD, out_row)

    def send_slots(kind, rows):
        for g in range(groups):
            part = nn(pick_out, stack(rows[g * GD * EPD : (g + 1) * GD * EPD]))
            r.slot_out[kind, g * GD : (g + 1) * GD] = part.astype(BF).reshape(GD, QP, 128)
        exchange(lambda d, m: r.slot_out.at[kind, d], r.slot_in, kind, r.m_slot)
        r.slot_in[kind, here] = r.slot_out[kind, dp]

    if z.own_weights:
        pl.semaphore_wait(r.entered, MP - 1)
    send_slots(0, slots)
    swap_wait(r.cin, r.m_cot)
    grad = own_image(r.cin)
    send_slots(1, tn(combine_low, grad).astype(BF))

    def expert_rows(kind):
        exchange_wait(r.slot_in, kind, r.m_slot)
        found = [[] for _ in range(EPD)]
        for g in range(groups):
            got = r.slot_in[kind, g * GS : (g + 1) * GS].reshape(GS * QP, 128)
            chunks = nn(r.pick_in[...], got)
            for e in range(EPD):
                found[e].append(unstack(chunks[e * LC * GS : (e + 1) * LC * GS]).astype(BF))
        return [jnp.concatenate(one, axis=0) for one in found]

    def send_parts(kind, per_expert):
        for g in range(groups):
            rows = [stack(one[g * GS : (g + 1) * GS]).astype(BF) for one in per_expert]
            part = nn(r.pick_back[...], jnp.concatenate(rows, axis=0))
            r.back_out[kind, g * GS : (g + 1) * GS] = part.astype(BF).reshape(GS, QP, 128)
        exchange(lambda d, m: r.back_out.at[kind, d * MP + m], r.back_in, kind, r.m_back)
        r.back_in[kind, here] = r.back_out[kind, here]

    def back_rows(kind):
        exchange_wait(r.back_in, kind, r.m_back)
        found = []
        for g in range(groups):
            got = r.back_in[kind, g * GS : (g + 1) * GS].reshape(GS * QP, 128)
            found.append(unstack(nn(r.pick_sum[...], got)).astype(BF))
        return jnp.concatenate(found, axis=0)

    slopes, results_part = [], []
    for e, slots_e in enumerate(expert_rows(0)):
        pre = nn(slots_e, r.wb_in[e])
        cdf = 0.5 * (1.0 + lax.erf(pre * (1.0 / math.sqrt(2.0))))
        hidden = (pre * cdf).astype(BF)
        results_part.append(nn(hidden, r.wb_out[e]))
        slopes.append(cdf + pre * jnp.exp(-0.5 * pre * pre) * (1.0 / math.sqrt(2.0 * math.pi)))
        r.slots[e], r.hidden[e] = slots_e, hidden
    send_parts(0, results_part)
    dslots_part = []
    for e, dresults_e in enumerate(expert_rows(1)):
        dpre = (nt(dresults_e, r.wb_out[e]) * slopes[e]).astype(BF)
        dslots_part.append(nt(dpre, r.wb_in[e]))
        r.dresults[e], r.dpre[e] = dresults_e, dpre
    send_parts(1, dslots_part)
    results = back_rows(0)

    output = r.resid[...] + nn(combine_low, results)
    for m in range(MP):
        r.osend[m] = output[:, m * CW : (m + 1) * CW].astype(BF)
    swap(r.osend, r.oin, r.m_outs)
    dslots = back_rows(1)
    dcombine, ddispatch = nt(grad, results), nt(h2, dslots)
    dlogits = dispatch * (ddispatch - jnp.sum(dispatch * ddispatch, axis=0, keepdims=True))
    dlogits = dlogits + combine * (dcombine - jnp.sum(combine * dcombine, axis=1, keepdims=True))
    dlogits = dlogits.astype(BF)
    dh2 = nn(dispatch_low, dslots) + nn(dlogits, phi_low)
    dresid = grad.astype(F32) + norm_backward(dh2, gain2, normed2, inv2)
    r.dresid[...] = dresid
    dbranch = dresid.astype(BF)
    proj_part = tn(dbranch, own_image(r.att)).astype(BF)

    class Unit:
        def __init__(self, part, got, mine, first, out, second, core_sem, sem, at):
            self.part, self.got, self.mine, self.first = part, got, mine, first
            self.out, self.second, self.core_sem, self.sem, self.at = out, second, core_sem, sem, at

        def start(self):
            send(self.part.at[:, 1 - co], self.got, self.core_sem, self.at, self.at, to_core)

        def copy(self, src, dst, way, device):
            send(src, dst, self.sem, self.at + (way,), self.at + (way,), device)

        def plane(self):
            arrive(self.got, self.core_sem, self.at)
            for x in range(NX):
                self.mine[x] = (self.part[x, co].astype(F32) + self.got[x].astype(F32)).astype(BF)
            low, high = pl.ds(0, half), pl.ds(half, half)
            self.copy(self.mine.at[dg, low], self.first.at[1], 1, to_x)
            self.copy(self.mine.at[dg, high], self.first.at[3], 3, to_y)
            self.copy(self.mine.at[xn, low], self.first.at[0], 0, to_x)
            self.copy(self.mine.at[yn, high], self.first.at[2], 2, to_y)

        def added(self, x, low, index):
            arrive(self.first.at[index], self.sem, self.at + (index,))
            return self.mine[x, low : low + half, :].astype(F32) + self.first[index].astype(F32)

        def forward(self):
            self.out[0] = self.added(yn, 0, 1).astype(BF)
            self.copy(self.out.at[0], self.second.at[0], 4, to_y)
            self.out[1] = self.added(xn, half, 3).astype(BF)
            self.copy(self.out.at[1], self.second.at[1], 5, to_x)

        def total(self):
            pieces = []
            for i in range(2):
                piece = self.added(xy, i * half, 2 * i)
                arrive(self.second.at[i], self.sem, self.at + (4 + i,))
                pieces.append(piece + self.second[i].astype(F32))
            return jnp.concatenate(pieces, axis=0)

    orders = [2 + middle, 3 - middle, 1, 0]

    def qkv_unit(i):
        m = mp_at(orders[i])
        return Unit(r.gq.at[m], r.cq.at[i], r.xq.at[i], r.aq.at[i], r.bq.at[i], r.dq.at[i], r.m_gc, r.m_gx, (i,))

    def column_slot(i):
        return (i + 3 * middle,) if i < 2 else (2,)

    def from_line(index):
        arrive(r.zr.at[index], r.m_gz, (index,))
        return r.zr[index].astype(F32)

    def unit_total(i):
        return jnp.concatenate([units[i].total(), r.fp[mp_at(orders[i])]], axis=1)

    def column(i):
        r.zf[...] = unit_total(i)

        @pl.when(middle == 1)
        def _():
            r.zf[...] += from_line([0, 1, 4][i])

        r.zs[i] = r.zf[...].astype(BF)
        target = 1 if i == 2 else 1 + 2 * middle
        at = column_slot(i)

        def copy():
            return pltpu.make_async_remote_copy(
                src_ref=r.zs.at[i], dst_ref=r.zr.at[at[0]], send_sem=r.m_gz.at[0, i], recv_sem=r.m_gz.at[1, at[0]],
                device_id=to_mp(target), device_id_type=MESH,
            )

        copy().start()
        sends.append(lambda: copy().wait_send())

    def column_own():
        r.zf[...] = unit_total(MP - 1) + from_line(2)

        @pl.when(middle == 1)
        def _():
            r.zf[...] += from_line(3)

        for c in range(3):
            r.qkv_grad[c] = r.zf[:, c * CW : (c + 1) * CW]
        r.proj_grad[...] = r.zf[:, QW:].T

    def proj_total():
        total = proj_unit.total()
        for m in range(MP):
            r.fp[m] = total[:, m * CW : (m + 1) * CW]

    def dp_swap(src, dst, sem):
        def copy(k):
            return remote(src.at[dp_at(k)], dst.at[dp], sem, (k,), (DP - k,), to_dp(k))

        each(1, DP, lambda k: copy(k).start())
        sends.append(lambda: each(1, DP, lambda k: copy(k).wait_send()))
        dst[dp] = src[dp]

    def dp_wait(dst, sem):
        each(1, DP, lambda k: arrive(dst.at[dp_at(k)], sem, (k,)))

    def sum_of(ref, count):
        total = ref[0]
        for i in range(1, count):
            total = total + ref[i]
        return total

    def small_column():
        dp_wait(r.sb, r.m_s1)
        r.sc[mp] = sum_of(r.sb, DP)
        to_column(r.sc.at[mp], r.m_s2)

    def small_back():
        for k in range(1, MP):
            arrive(r.sc.at[mp_at(k)], r.m_s2, (k,))
        r.sd[dp] = sum_of(r.sc, MP)
        for k in range(1, DP):
            send(r.sd.at[dp], r.sd.at[dp], r.m_s3, (k,), (DP - k,), to_dp(k))

    def gains(grad_out, normed):
        return jnp.concatenate(
            [jnp.sum(grad_out * normed, axis=0, keepdims=True), jnp.sum(grad_out, axis=0, keepdims=True)], axis=0
        )

    if z.own_weights:
        units = [qkv_unit(i) for i in range(MP)]
        proj_unit = Unit(r.gp, r.cp, r.xp, r.ap, r.bp, r.dp_, r.m_hc, r.m_hx, ())
        r.gp[...] = proj_part.reshape(NX, IN, RB, D)
        proj_unit.start()
    else:
        r.gp[...] = proj_part
    for m in range(MP):
        r.datt[m] = nn(dbranch, proj_weight(m)).astype(BF)
    rows2 = gains(dh2, normed2)
    if z.own_weights:
        phi_part = tn(dlogits, h2)
        r.sa[...] = jnp.zeros((DP, KE, D), F32)
        for i in range(E // KE):
            r.sa[i] = phi_part[i * KE : (i + 1) * KE]
        r.sa[E // KE, 0:2, :] = rows2
        dp_swap(r.sa, r.sb, r.m_s1)
    else:
        r.phi_grad[...] = tn(dlogits, h2)

    def heads_backward(m):
        qkv, datt = r.qkv[m], r.datt[m]
        pieces = [[], [], []]
        for h in range(z.HL):
            query, key, value = head_cols(qkv, h)
            grad_h = datt[:, h * HEAD_DIM : (h + 1) * HEAD_DIM]
            probs = r.probs[m, h]
            dprobs = nt(grad_h, value)
            dscores = probs * (dprobs - jnp.sum(probs * dprobs, axis=-1, keepdims=True))
            dscores = dscores.astype(BF)
            pieces[0].append(nn(dscores, key) * scale)
            pieces[1].append(tn(dscores, query) * scale)
            pieces[2].append(tn(probs.astype(BF), grad_h))
        dqkv = jnp.concatenate(pieces[0] + pieces[1] + pieces[2], axis=1).astype(BF)
        piece = tn(r.h1[...], dqkv).astype(BF)
        if z.own_weights:
            r.gq[m] = piece.reshape(NX, IN, RB, QW)
        else:
            r.gq[m] = piece
        return dqkv

    between = {}
    if z.own_weights:
        first, second, third, last = units
        between = {0: [proj_unit.plane], 1: [first.plane], 2: [second.plane, proj_unit.forward], 3: [third.plane]}
    for i in range(MP):
        m = mp_at(orders[i] if MP == 4 else i)
        dqkv = heads_backward(m)
        if z.own_weights:
            units[i].start()
        part = nt(dqkv, weight(m))
        if i == 0:
            r.dh1[...] = part
        else:
            r.dh1[...] += part
        for step in between.get(i, []):
            step()

    normed1, inv1 = normalize(own_image(r.tin).astype(F32))
    dh1 = r.dh1[...]
    input_grad = r.dresid[...] + norm_backward(dh1, gain1, normed1, inv1)
    for m in range(MP):
        r.isend[m] = input_grad[:, m * CW : (m + 1) * CW].astype(BF)
    swap(r.isend, r.iin, r.m_ings)
    rows1 = gains(dh1, normed1)
    if z.own_weights:
        r.ta[...] = rows1
        for k in range(1, DP):
            send(r.ta, r.tb.at[dp], r.m_t1, (k,), (DP - k,), to_dp(k))
        r.tb[dp] = rows1

    if z.own_weights:
        first.forward()
        last.plane()
        second.forward()
        third.forward()
        proj_total()
        column(0)
        last.forward()
        small_column()
        column(1)
        small_back()
        dp_wait(r.tb, r.m_t1)
        r.tc[mp] = sum_of(r.tb, DP)
        to_column(r.tc.at[mp], r.m_t2)
    swap_wait(r.oin, r.m_outs)
    r.output[...] = from_images(r.oin)
    if z.own_weights:
        column(2)
        dp_wait(r.sd, r.m_s3)
        for i in range(E // KE):
            r.phi_grad[i * KE : (i + 1) * KE, :] = r.sd[i]
        column_own()
        for k in range(1, MP):
            arrive(r.tc.at[mp_at(k)], r.m_t2, (k,))
        r.norm_grad[...] = jnp.concatenate([sum_of(r.tc, MP), r.sd[E // KE, 0:2, :]], axis=0)
    else:
        r.norm_grad[...] = jnp.concatenate([rows1, rows2], axis=0)
    swap_wait(r.iin, r.m_ings)

    for wait in sends:
        wait()


def from_images(source):
    images = [source[i, 0:SEQ, :].astype(F32) for i in range(source.shape[0])]
    return jnp.concatenate(images, axis=0).T


def finish_kernel(passed, slots, dpre, hidden, dresults, iin, *refs):
    sources, (in_grad, out_grad, input_grad), rest = refs[:passed], refs[passed : passed + 3], refs[passed + 3 :]
    targets, (grads_in, grads_out, grad_t, sem, tile_sem) = rest[:passed], rest[passed:]
    copies = [pltpu.make_async_copy(a, b, sem.at[i]) for i, (a, b) in enumerate(zip(sources, targets))]
    for copy in copies:
        copy.start()
    experts, _, width = slots.shape
    tile = 256 if width % 256 == 0 else width
    count = 0
    for e in range(experts):
        for left, right, held, target in ((slots, dpre, grads_in, in_grad), (hidden, dresults, grads_out, out_grad)):
            for t in range(width // tile):
                here = pl.ds(t * tile, tile)
                held[e, here, :] = tn(left[e, :, t * tile : (t + 1) * tile], right[e])
                copy = pltpu.make_async_copy(held.at[e, here], target.at[e, here], tile_sem.at[count])
                copy.start()
                copies.append(copy)
                count += 1
    grad_t[...] = from_images(iin)
    last = pltpu.make_async_copy(grad_t, input_grad, sem.at[passed])
    last.start()
    for copy in copies + [last]:
        copy.wait()


def per_device(mesh, tokens, norm_params, w_qkv, w_proj, phi, w_in, w_out, cotangent):
    z = Sizes(mesh, tokens, w_qkv, phi, w_in)
    vmem, anyspace = pl.BlockSpec(memory_space=pltpu.VMEM), pl.BlockSpec(memory_space=pl.ANY)
    inputs = dict(
        tokens=tokens.T, norm_params=norm_params, w_qkv=w_qkv, w_proj=w_proj, phi=phi.T, cotangent=cotangent.T
    )
    specs = [vmem] * len(inputs)
    inputs.update(w_in=w_in, w_out=w_out)
    specs += [anyspace] * 2
    images = z.MP * z.DP
    outs = dict(
        output=((z.CW, z.ROWS), F32), iin=((z.MP, z.SP, z.CW), BF),
        phi_grad=((z.E, z.D), F32), norm_grad=((4, z.D), F32),
        slots=((z.EPD, images, z.D), BF), dresults=((z.EPD, images, z.D), BF),
        hidden=((z.EPD, images, z.F), BF), dpre=((z.EPD, images, z.F), BF),
    )
    if z.own_weights:
        outs.update(qkv_grad=((3, z.RB, z.CW), F32), proj_grad=((z.CW, z.RB), F32))
    else:
        outs.update(gq=((z.MP, z.D, z.QW), BF), gp=((z.D, z.D), BF))
        wall = lax.all_gather(w_qkv.astype(BF), "dp", axis=1, tiled=True)
        wall = jnp.concatenate([wall[c] for c in range(3)], axis=1)
        wpall = lax.all_gather(w_proj.T.astype(BF), "dp", axis=0, tiled=True)
        inputs.update(wall=lax.all_gather(wall, "mp"), wpall=lax.all_gather(wpall, "mp"))
        specs += [vmem] * 2
    names, scratch = scratch_of(z)
    result = pl.pallas_call(
        functools.partial(block_kernel, z, list(inputs), list(outs), names),
        out_shape=[jax.ShapeDtypeStruct(*one) for one in outs.values()],
        in_specs=specs,
        out_specs=[vmem] * len(outs),
        scratch_shapes=scratch,
        compiler_params=pltpu.CompilerParams(
            collective_id=0, has_side_effects=True, vmem_limit_bytes=62 * 2**20
        ),
        name="block",
    )(*inputs.values())
    got = dict(zip(outs, result))

    passed = ["output", "norm_grad", "phi_grad"] + (["qkv_grad", "proj_grad"] if z.own_weights else [])
    tile = 256 if z.F % 256 == 0 and z.D == z.F else z.F
    tiles = 2 * z.EPD * (z.F // tile)
    results = pl.pallas_call(
        functools.partial(finish_kernel, len(passed)),
        in_specs=[vmem] * (5 + len(passed)),
        out_specs=[anyspace] * (3 + len(passed)),
        out_shape=[
            jax.ShapeDtypeStruct((z.EPD, z.D, z.F), F32),
            jax.ShapeDtypeStruct((z.EPD, z.F, z.D), F32),
            jax.ShapeDtypeStruct((z.CW, z.ROWS), F32),
        ]
        + [jax.ShapeDtypeStruct(*outs[name]) for name in passed],
        scratch_shapes=[
            pltpu.VMEM((z.EPD, z.D, z.F), F32),
            pltpu.VMEM((z.EPD, z.F, z.D), F32),
            pltpu.VMEM((z.CW, z.ROWS), F32),
            pltpu.SemaphoreType.DMA((len(passed) + 1,)),
            pltpu.SemaphoreType.DMA((tiles,)),
        ],
        compiler_params=pltpu.CompilerParams(vmem_limit_bytes=60 * 2**20),
        name="finish",
    )(got["slots"], got["dpre"], got["hidden"], got["dresults"], got["iin"], *(got[name] for name in passed))
    in_grad, out_grad, input_grad = results[:3]
    got.update(zip(passed, results[3:]))
    output, input_grad = got["output"].T, input_grad.T
    phi_grad, norm_grad = got["phi_grad"].T, got["norm_grad"]
    if z.own_weights:
        qkv_grad, proj_grad = got["qkv_grad"], got["proj_grad"]
    else:
        phi_grad, norm_grad = lax.psum((phi_grad, norm_grad), ("dp", "mp"))
        gq = lax.psum_scatter(got["gq"].astype(F32), "mp", scatter_dimension=0, tiled=False)
        gp = lax.psum_scatter(got["gp"].astype(F32), "mp", scatter_dimension=1, tiled=True)
        gq = jnp.stack([gq[:, c * z.CW : (c + 1) * z.CW] for c in range(3)])
        qkv_grad = lax.psum_scatter(gq, "dp", scatter_dimension=1, tiled=True)
        proj_grad = lax.psum_scatter(gp, "dp", scatter_dimension=0, tiled=True).T
    return (
        output, input_grad, qkv_grad, proj_grad, in_grad, out_grad, phi_grad, norm_grad
    )


def solution(mesh):
    return jax.shard_map(
        functools.partial(per_device, mesh),
        mesh=mesh,
        in_specs=(
            P("dp", "mp"), P(), P(None, "dp", "mp"), P("mp", "dp"), P(),
            P("dp", None, "mp"), P("dp", "mp", None), P("dp", "mp"),
        ),
        out_specs=(
            P("dp", "mp"), P("dp", "mp"), P(None, "dp", "mp"), P("mp", "dp"),
            P("dp", None, "mp"), P("dp", "mp", None), P(), P(),
        ),
        check_vma=False,
    )
```

```python
import functools
import math

import jax
import jax.numpy as jnp
from jax import lax
from jax.experimental import pallas as pl
from jax.experimental.pallas import tpu as pltpu
from jax.sharding import PartitionSpec as P

HEAD_DIM = 64
SEQ = 196
EPSILON = 1e-06
MESH = pl.DeviceIdType.MESH
BF = jnp.bfloat16
F32 = jnp.float32
NEG = -1e30


def nn(a, b):
    return lax.dot_general(a, b, (((1,), (0,)), ((), ())), preferred_element_type=F32)


def nt(a, b):
    return lax.dot_general(a, b, (((1,), (1,)), ((), ())), preferred_element_type=F32)


def tn(a, b):
    return lax.dot_general(a, b, (((0,), (0,)), ((), ())), preferred_element_type=F32)


def each(low, high, body):
    if high - low <= 32:
        for i in range(low, high):
            body(i)
    else:

        def step(i, carry):
            body(i)
            return carry

        lax.fori_loop(low, high, step, 0)


def select_rows(rows, cols, source):
    row = lax.broadcasted_iota(jnp.int32, (rows, cols), 0)
    col = lax.broadcasted_iota(jnp.int32, (rows, cols), 1)
    return jnp.where(col == source(row), 1.0, 0.0).astype(BF)


def normalize(values):
    mean = jnp.mean(values, axis=-1, keepdims=True)
    centered = values - mean
    var = jnp.mean(centered * centered, axis=-1, keepdims=True)
    inv = lax.rsqrt(var + EPSILON)
    return centered * inv, inv


def norm_backward(grad, gain, normed, inv):
    scaled = grad * gain
    first = jnp.mean(scaled, axis=-1, keepdims=True)
    second = jnp.mean(scaled * normed, axis=-1, keepdims=True)
    return inv * (scaled - first - normed * second)


class Sizes:
    def __init__(self, mesh, tokens, w_qkv, phi, w_in):
        self.DP, self.MP = mesh.shape["dp"], mesh.shape["mp"]
        self.D, self.E = phi.shape
        self.CW = tokens.shape[1]
        self.RB = w_qkv.shape[1]
        self.QW = 3 * self.CW
        self.HL = self.CW // HEAD_DIM
        self.EPD = w_in.shape[0]
        self.F = w_in.shape[2]
        self.IN = 2
        self.NX = self.DP // self.IN
        self.SP = (SEQ + 15) // 16 * 16
        self.ROWS = tokens.shape[0]
        self.KE = 2 * self.EPD
        self.NS = self.DP * self.MP
        self.LC = self.D // 128
        self.Q = self.EPD * self.LC
        self.QP = (self.Q + 15) // 16 * 16
        self.GD = 8 if self.DP % 8 == 0 else self.DP
        self.GS = self.GD * self.MP
        self.own_weights = self.MP == 4 and self.NX == 4 and self.RB % 32 == 0 and self.E + 2 <= self.KE * self.DP


def scratch_of(z):
    dma = pltpu.SemaphoreType.DMA
    v = pltpu.VMEM
    DP, MP, D, CW, RB, QW, SP, NX, IN, KE = z.DP, z.MP, z.D, z.CW, z.RB, z.QW, z.SP, z.NX, z.IN, z.KE
    half = RB // 2
    items = dict(
        tsend=v((MP, SP, CW), BF), tin=v((MP, SP, CW), BF),
        csend=v((MP, SP, CW), BF), cin=v((MP, SP, CW), BF),
        osend=v((MP, SP, CW), BF), oin=v((MP, SP, CW), BF),
        isend=v((MP, SP, CW), BF),
        wf_in=v((z.EPD, D, z.F), F32), wf_out=v((z.EPD, z.F, D), F32),
        wb_in=v((z.EPD, D, z.F), BF), wb_out=v((z.EPD, z.F, D), BF),
        h1=v((SP, D), BF), qkv=v((MP, SP, QW), BF), probs=v((MP, z.HL, SP, SP), F32),
        att=v((MP, SP, CW), BF), datt=v((MP, SP, CW), BF),
        resid=v((SP, D), F32), dresid=v((SP, D), F32), dh1=v((SP, D), F32),
        slot_out=v((2, DP, z.QP, 128), BF), slot_in=v((2, z.NS, z.QP, 128), BF),
        back_out=v((2, z.NS, z.QP, 128), BF), back_in=v((2, z.NS, z.QP, 128), BF),
        pick_in=v((z.Q * z.GS, z.GS * z.QP), BF), pick_back=v((z.GS * z.QP, z.Q * z.GS), BF),
        pick_sum=v((z.LC * z.GD * z.EPD, z.GS * z.QP), BF),
    )
    sems = dict(
        tok=(2, MP), cot=(2, MP), outs=(2, MP), ings=(2, MP), hbm=(2,),
        slot=(2, 2), back=(2, 2),
    )
    if z.own_weights:
        items.update(
            wall=v((MP, NX, IN, RB, D), BF),
            gq=v((MP, NX, IN, RB, QW), BF), gp=v((NX, IN, RB, D), BF),
            cq=v((MP, NX, RB, QW), BF), cp=v((NX, RB, D), BF),
            xq=v((MP, NX, RB, QW), BF), xp=v((NX, RB, D), BF),
            aq=v((MP, 4, half, QW), BF), ap=v((4, half, D), BF),
            bq=v((MP, 2, half, QW), BF), bp=v((2, half, D), BF),
            dq=v((MP, 2, half, QW), BF), dp_=v((2, half, D), BF),
            zf=v((RB, D), F32), zs=v((MP, RB, D), BF), zr=v((5, RB, D), BF), fp=v((MP, RB, CW), F32),
            sa=v((DP, KE, D), F32), sb=v((DP, KE, D), F32), sc=v((MP, KE, D), F32), sd=v((DP, KE, D), F32),
            ta=v((2, D), F32), tb=v((DP, 2, D), F32), tc=v((MP, 2, D), F32),
        )
        sems.update(
            wz=(2, 5), wx=(2, MP, 4), wc=(2, MP),
            gc=(2, MP), gx=(2, MP, 6), gz=(2, 5), hc=(2,), hx=(2, 6),
            s1=(2, DP), s2=(2, MP), s3=(2, DP), t1=(2, DP), t2=(2, MP),
        )
    names, shapes = [], []
    for name, shape in items.items():
        names.append(name)
        shapes.append(shape)
    for name, shape in sems.items():
        names.append("m_" + name)
        shapes.append(dma(shape))
    names.append("entered")
    shapes.append(pltpu.SemaphoreType.REGULAR)
    return names, shapes


class Refs:
    pass


def block_kernel(z, in_names, out_names, names, *refs):
    r = Refs()
    for name, ref in zip(in_names + out_names + names, refs):
        setattr(r, name, ref)
    DP, MP, D, CW, RB, QW, SP = z.DP, z.MP, z.D, z.CW, z.RB, z.QW, z.SP
    NX, IN, E, EPD, KE = z.NX, z.IN, z.E, z.EPD, z.KE
    half = RB // 2
    dp, mp = lax.axis_index("dp"), lax.axis_index("mp")
    xy, co = dp // IN, lax.rem(dp, IN)
    xn = xy + 1 - 2 * lax.rem(xy, 2)
    yn = lax.rem(xy + 2, NX)
    dg = lax.rem(xn + 2, NX)
    to_x, to_y, to_core = (xn * IN + co, mp), (yn * IN + co, mp), (xy * IN + 1 - co, mp)
    sends = []

    def remote(src, dst, sem, s_at, r_at, device):
        return pltpu.make_async_remote_copy(
            src_ref=src, dst_ref=dst, send_sem=sem.at[(0,) + s_at], recv_sem=sem.at[(1,) + r_at],
            device_id=device, device_id_type=MESH,
        )

    def send(*copy):
        remote(*copy).start()
        sends.append(lambda: remote(*copy).wait_send())

    def arrive(ref, sem, at):
        remote(ref, ref, sem, at, at, to_mp(1)).wait_recv()

    def mp_at(k):
        if MP != 4:
            return lax.rem(mp + k, MP)
        return 2 * lax.rem(mp // 2 + k // 2, 2) + lax.rem(mp + k, 2)

    def mp_back(k):
        return k if MP == 4 else MP - k

    def dp_at(k):
        return lax.rem(dp + k, DP)

    def to_mp(k):
        return (dp, mp_at(k))

    def to_dp(k):
        return (dp_at(k), mp)

    def to_any(k):
        if isinstance(k, int):
            return (dp_at(k // MP), lax.rem(mp + k % MP, MP))
        return (dp_at(k // MP), lax.rem(mp + lax.rem(k, MP), MP))

    barrier = pltpu.get_barrier_semaphore()
    if z.own_weights:
        for k in range(1, MP):
            pl.semaphore_signal(barrier, inc=1, device_id=to_mp(k), device_id_type=MESH)
        each(1, DP, lambda k: pl.semaphore_signal(barrier, inc=1, device_id=to_dp(k), device_id_type=MESH))
    else:
        each(1, z.NS, lambda k: pl.semaphore_signal(barrier, inc=1, device_id=to_any(k), device_id_type=MESH))

    load_in = pltpu.make_async_copy(r.w_in, r.wf_in, r.m_hbm.at[0])
    load_out = pltpu.make_async_copy(r.w_out, r.wf_out, r.m_hbm.at[1])
    load_in.start()
    load_out.start()

    if z.own_weights:
        r.wall[mp, xy, co] = jnp.concatenate(
            [r.w_qkv[c].astype(BF) for c in range(3)] + [r.w_proj[...].T.astype(BF)], axis=1
        )
    pl.semaphore_wait(barrier, MP - 1 + DP - 1 if z.own_weights else z.NS - 1)
    if z.own_weights:
        for k in range(1, MP):
            pl.semaphore_signal(r.entered, inc=1, device_id=to_mp(k), device_id_type=MESH)

    def to_images(source, target):
        target[...] = jnp.zeros((MP, SP, CW), BF)
        rows = source[...].T
        for i in range(MP):
            target[i, 0:SEQ, :] = rows[SEQ * i : SEQ * (i + 1)]

    def swap(src, dst, sem):
        for k in range(1, MP):
            send(src.at[mp_at(k)], dst.at[mp], sem, (k,), (mp_back(k),), to_mp(k))
        dst[mp] = src[mp]

    def swap_wait(dst, sem):
        for k in range(1, MP):
            arrive(dst.at[mp_at(k)], sem, (k,))

    def to_column(block, sem):
        for k in range(1, MP):
            send(block, block, sem, (k,), (mp_back(k),), to_mp(k))

    class Plane:
        def __init__(self, block, sem, at):
            self.block, self.sem, self.at = block, sem, at

        def copy(self, ref, way, device):
            send(ref, ref, self.sem, self.at + (way,), self.at + (way,), device)

        def start(self):
            self.copy(self.block(xy, 0, RB), 0, to_x)
            self.copy(self.block(xy, 0, RB), 1, to_y)

        def forward(self):
            arrive(self.block(xn, 0, RB), self.sem, self.at + (0,))
            self.copy(self.block(xn, 0, half), 2, to_y)
            arrive(self.block(yn, 0, RB), self.sem, self.at + (1,))
            self.copy(self.block(yn, half, half), 3, to_x)

        def wait(self):
            arrive(self.block(dg, 0, half), self.sem, self.at + (2,))
            arrive(self.block(dg, half, half), self.sem, self.at + (3,))

    middle = lax.rem((mp + 1) // 2, 2)
    slots_at = [0, 1, 2 + middle, 3 - middle]

    def column_copy(k, way, slot, target):
        block = r.wall.at[mp_at(k), xy, co]
        return remote(block, block, r.m_wz, (way,), (slot,), to_mp(target))

    def column_send(*copy):
        column_copy(*copy).start()
        sends.append(lambda: column_copy(*copy).wait_send())

    def column_pass(*copy):
        pl.when(middle == 1)(lambda: column_copy(*copy).start())
        sends.append(lambda: pl.when(middle == 1)(lambda: column_copy(*copy).wait_send()))

    def weight_plane(s):
        return Plane(lambda pos, low, rows: r.wall.at[mp_at(slots_at[s]), pos, co, pl.ds(low, rows)], r.m_wx, (s,))

    def load_expert(copy, wide, low):
        copy.wait()
        low[...] = wide[...].astype(BF)


    def make_picks():
        GS, Q, QP, LC = z.GS, z.Q, z.QP, z.LC
        r.pick_in[...] = select_rows(Q * GS, GS * QP, lambda row: (row % GS) * QP + row // GS)
        r.pick_back[...] = select_rows(
            GS * QP, Q * GS, lambda row: jnp.where(row % QP < Q, (row % QP) * GS + row // QP, -1)
        )
        shape = (LC * z.GD * EPD, GS * QP)
        row, col = (lax.broadcasted_iota(jnp.int32, shape, i) for i in range(2))
        expert, chunk = row % (z.GD * EPD), row // (z.GD * EPD)
        wanted = (col // (QP * MP) == expert // EPD) & (col % QP == (expert % EPD) * LC + chunk)
        r.pick_sum[...] = jnp.where(wanted, 1.0, 0.0).astype(BF)

    if z.own_weights:
        planes = [weight_plane(s) for s in range(MP)]

        def column_arrived(s, k, way, slot, target):
            arrive(r.wall.at[mp_at(slots_at[s]), xy, co], r.m_wz, (slots_at[s],))
            if k:
                column_pass(k, way, slot, target)
            planes[s].start()

        def plane_arrived(s):
            planes[s].wait()
            block = r.wall.at[mp_at(slots_at[s]), :, co]
            send(block, block, r.m_wc, (s,), (s,), to_core)

        column_send(0, 0, 1, 1)
        column_send(0, 1, 3, 3)
        planes[0].start()
        to_images(r.tokens, r.tsend)
        load_expert(load_in, r.wf_in, r.wb_in)
        column_arrived(1, 1, 2, 2, 3)
        planes[0].forward()
        to_images(r.cotangent, r.csend)
        column_arrived(2, 3, 3, 2, 1)
        planes[1].forward()
        swap(r.tsend, r.tin, r.m_tok)
        plane_arrived(0)
        load_expert(load_out, r.wf_out, r.wb_out)
        make_picks()
        column_arrived(3, 0, 0, 0, 0)
        planes[2].forward()
        plane_arrived(1)
        planes[3].forward()
        swap(r.csend, r.cin, r.m_cot)
        plane_arrived(2)
    else:
        to_images(r.tokens, r.tsend)
        swap(r.tsend, r.tin, r.m_tok)
        to_images(r.cotangent, r.csend)
        swap(r.csend, r.cin, r.m_cot)
        load_expert(load_in, r.wf_in, r.wb_in)
        load_expert(load_out, r.wf_out, r.wb_out)
        make_picks()

    swap_wait(r.tin, r.m_tok)
    gain1, shift1 = r.norm_params[0:1, :], r.norm_params[1:2, :]
    gain2, shift2 = r.norm_params[2:3, :], r.norm_params[3:4, :]

    def own_image(ref):
        return jnp.concatenate([ref[i] for i in range(MP)], axis=1)

    normed1, _ = normalize(own_image(r.tin).astype(F32))
    r.h1[...] = (normed1 * gain1 + shift1).astype(BF)

    scale = 1.0 / math.sqrt(HEAD_DIM)
    key_ok = lax.broadcasted_iota(jnp.int32, (1, SP), 1) < SEQ

    def weight(m):
        return r.wall[m].reshape(D, D)[:, :QW] if z.own_weights else r.wall[m]

    def proj_weight(m):
        return r.wall[m].reshape(D, D)[:, QW:] if z.own_weights else r.wpall[m]

    def head_cols(qkv, h):
        return (qkv[:, c * CW + h * HEAD_DIM : c * CW + (h + 1) * HEAD_DIM] for c in range(3))

    def heads_forward(s):
        m = mp_at(slots_at[s])
        if z.own_weights:
            arrive(r.wall.at[m, :, 1 - co], r.m_wc, (s,))
        qkv = nn(r.h1[...], weight(m)).astype(BF)
        r.qkv[m] = qkv
        if z.own_weights and s == MP - 2:
            plane_arrived(s + 1)
        attended = []
        for h in range(z.HL):
            query, key, value = head_cols(qkv, h)
            scores = jnp.where(key_ok, nt(query, key) * scale, NEG)
            top = jnp.max(scores, axis=-1, keepdims=True)
            grown = jnp.exp(scores - top)
            probs = grown / jnp.sum(grown, axis=-1, keepdims=True)
            r.probs[m, h] = probs
            attended.append(nn(probs.astype(BF), value))
        r.att[m] = jnp.concatenate(attended, axis=1).astype(BF)

    for s in range(MP):
        heads_forward(s)

    resid = own_image(r.tin).astype(F32)
    for m in range(MP):
        resid = resid + nt(r.att[m], proj_weight(m))
    r.resid[...] = resid
    normed2, inv2 = normalize(resid)
    h2 = (normed2 * gain2 + shift2).astype(BF)
    phi_low = r.phi[...].astype(BF)
    logits = nt(h2, phi_low)
    token_ok = lax.broadcasted_iota(jnp.int32, (SP, 1), 0) < SEQ
    masked = jnp.where(token_ok, logits, NEG)
    grown = jnp.exp(masked - jnp.max(masked, axis=0, keepdims=True))
    dispatch = grown / jnp.sum(grown, axis=0, keepdims=True)
    grown = jnp.exp(logits - jnp.max(logits, axis=1, keepdims=True))
    combine = grown / jnp.sum(grown, axis=1, keepdims=True)
    dispatch_low, combine_low = dispatch.astype(BF), combine.astype(BF)
    slots = tn(dispatch_low, h2).astype(BF)

    GD, GS, Q, QP, LC = z.GD, z.GS, z.Q, z.QP, z.LC
    groups = DP // GD
    here = dp * MP + mp

    def stack(rows):
        return jnp.concatenate([rows[:, c * 128 : (c + 1) * 128] for c in range(LC)], axis=0)

    def unstack(chunks):
        count = chunks.shape[0] // LC
        return jnp.concatenate([chunks[c * count : (c + 1) * count] for c in range(LC)], axis=1)

    def exchange(source, dst, kind, sem):
        def copy(k):
            device = to_any(k)
            return pltpu.make_async_remote_copy(
                src_ref=source(*device), dst_ref=dst.at[kind, here], send_sem=sem.at[0, kind],
                recv_sem=sem.at[1, kind], device_id=device, device_id_type=MESH,
            )

        each(1, z.NS, lambda k: copy(k).start())
        all_of_them = dst.at[kind, pl.ds(0, z.NS - 1)]
        sends.append(
            lambda: pltpu.make_async_remote_copy(
                src_ref=all_of_them, dst_ref=all_of_them, send_sem=sem.at[0, kind], recv_sem=sem.at[1, kind],
                device_id=to_mp(1), device_id_type=MESH,
            ).wait_send()
        )

    def exchange_wait(dst, kind, sem):
        all_of_them = dst.at[kind, pl.ds(0, z.NS - 1)]
        pltpu.make_async_remote_copy(
            src_ref=all_of_them, dst_ref=all_of_them, send_sem=sem.at[0, kind], recv_sem=sem.at[1, kind],
            device_id=to_mp(1), device_id_type=MESH,
        ).wait_recv()

    def out_row(row):
        d, q = row // QP, row % QP
        return jnp.where(q < Q, (q % LC) * (GD * EPD) + d * EPD + q // LC, -1)

    pick_out = select_rows(GD * QP, LC * GD * EPD, out_row)

    def send_slots(kind, rows):
        for g in range(groups):
            part = nn(pick_out, stack(rows[g * GD * EPD : (g + 1) * GD * EPD]))
            r.slot_out[kind, g * GD : (g + 1) * GD] = part.astype(BF).reshape(GD, QP, 128)
        exchange(lambda d, m: r.slot_out.at[kind, d], r.slot_in, kind, r.m_slot)
        r.slot_in[kind, here] = r.slot_out[kind, dp]

    if z.own_weights:
        pl.semaphore_wait(r.entered, MP - 1)
    send_slots(0, slots)
    swap_wait(r.cin, r.m_cot)
    grad = own_image(r.cin)
    send_slots(1, tn(combine_low, grad).astype(BF))

    def expert_rows(kind):
        exchange_wait(r.slot_in, kind, r.m_slot)
        found = [[] for _ in range(EPD)]
        for g in range(groups):
            got = r.slot_in[kind, g * GS : (g + 1) * GS].reshape(GS * QP, 128)
            chunks = nn(r.pick_in[...], got)
            for e in range(EPD):
                found[e].append(unstack(chunks[e * LC * GS : (e + 1) * LC * GS]).astype(BF))
        return [jnp.concatenate(one, axis=0) for one in found]

    def send_parts(kind, per_expert):
        for g in range(groups):
            rows = [stack(one[g * GS : (g + 1) * GS]).astype(BF) for one in per_expert]
            part = nn(r.pick_back[...], jnp.concatenate(rows, axis=0))
            r.back_out[kind, g * GS : (g + 1) * GS] = part.astype(BF).reshape(GS, QP, 128)
        exchange(lambda d, m: r.back_out.at[kind, d * MP + m], r.back_in, kind, r.m_back)
        r.back_in[kind, here] = r.back_out[kind, here]

    def back_rows(kind):
        exchange_wait(r.back_in, kind, r.m_back)
        found = []
        for g in range(groups):
            got = r.back_in[kind, g * GS : (g + 1) * GS].reshape(GS * QP, 128)
            found.append(unstack(nn(r.pick_sum[...], got)).astype(BF))
        return jnp.concatenate(found, axis=0)

    slopes, results_part = [], []
    for e, slots_e in enumerate(expert_rows(0)):
        pre = nn(slots_e, r.wb_in[e])
        cdf = 0.5 * (1.0 + lax.erf(pre * (1.0 / math.sqrt(2.0))))
        hidden = (pre * cdf).astype(BF)
        results_part.append(nn(hidden, r.wb_out[e]))
        slopes.append(cdf + pre * jnp.exp(-0.5 * pre * pre) * (1.0 / math.sqrt(2.0 * math.pi)))
        r.slots[e], r.hidden[e] = slots_e, hidden
    send_parts(0, results_part)
    dslots_part = []
    for e, dresults_e in enumerate(expert_rows(1)):
        dpre = (nt(dresults_e, r.wb_out[e]) * slopes[e]).astype(BF)
        dslots_part.append(nt(dpre, r.wb_in[e]))
        r.dresults[e], r.dpre[e] = dresults_e, dpre
    send_parts(1, dslots_part)
    results = back_rows(0)

    output = r.resid[...] + nn(combine_low, results)
    for m in range(MP):
        r.osend[m] = output[:, m * CW : (m + 1) * CW].astype(BF)
    swap(r.osend, r.oin, r.m_outs)
    dslots = back_rows(1)
    dcombine, ddispatch = nt(grad, results), nt(h2, dslots)
    dlogits = dispatch * (ddispatch - jnp.sum(dispatch * ddispatch, axis=0, keepdims=True))
    dlogits = dlogits + combine * (dcombine - jnp.sum(combine * dcombine, axis=1, keepdims=True))
    dlogits = dlogits.astype(BF)
    dh2 = nn(dispatch_low, dslots) + nn(dlogits, phi_low)
    dresid = grad.astype(F32) + norm_backward(dh2, gain2, normed2, inv2)
    r.dresid[...] = dresid
    dbranch = dresid.astype(BF)
    proj_part = tn(dbranch, own_image(r.att)).astype(BF)

    class Unit:
        def __init__(self, part, got, mine, first, out, second, core_sem, sem, at):
            self.part, self.got, self.mine, self.first = part, got, mine, first
            self.out, self.second, self.core_sem, self.sem, self.at = out, second, core_sem, sem, at

        def start(self):
            send(self.part.at[:, 1 - co], self.got, self.core_sem, self.at, self.at, to_core)

        def copy(self, src, dst, way, device):
            send(src, dst, self.sem, self.at + (way,), self.at + (way,), device)

        def plane(self):
            arrive(self.got, self.core_sem, self.at)
            for x in range(NX):
                self.mine[x] = (self.part[x, co].astype(F32) + self.got[x].astype(F32)).astype(BF)
            low, high = pl.ds(0, half), pl.ds(half, half)
            self.copy(self.mine.at[dg, low], self.first.at[1], 1, to_x)
            self.copy(self.mine.at[dg, high], self.first.at[3], 3, to_y)
            self.copy(self.mine.at[xn, low], self.first.at[0], 0, to_x)
            self.copy(self.mine.at[yn, high], self.first.at[2], 2, to_y)

        def added(self, x, low, index):
            arrive(self.first.at[index], self.sem, self.at + (index,))
            return self.mine[x, low : low + half, :].astype(F32) + self.first[index].astype(F32)

        def forward(self):
            self.out[0] = self.added(yn, 0, 1).astype(BF)
            self.copy(self.out.at[0], self.second.at[0], 4, to_y)
            self.out[1] = self.added(xn, half, 3).astype(BF)
            self.copy(self.out.at[1], self.second.at[1], 5, to_x)

        def total(self):
            pieces = []
            for i in range(2):
                piece = self.added(xy, i * half, 2 * i)
                arrive(self.second.at[i], self.sem, self.at + (4 + i,))
                pieces.append(piece + self.second[i].astype(F32))
            return jnp.concatenate(pieces, axis=0)

    orders = [2 + middle, 3 - middle, 1, 0]

    def qkv_unit(i):
        m = mp_at(orders[i])
        return Unit(r.gq.at[m], r.cq.at[i], r.xq.at[i], r.aq.at[i], r.bq.at[i], r.dq.at[i], r.m_gc, r.m_gx, (i,))

    def column_slot(i):
        return (i + 3 * middle,) if i < 2 else (2,)

    def from_line(index):
        arrive(r.zr.at[index], r.m_gz, (index,))
        return r.zr[index].astype(F32)

    def unit_total(i):
        return jnp.concatenate([units[i].total(), r.fp[mp_at(orders[i])]], axis=1)

    def column(i):
        r.zf[...] = unit_total(i)

        @pl.when(middle == 1)
        def _():
            r.zf[...] += from_line([0, 1, 4][i])

        r.zs[i] = r.zf[...].astype(BF)
        target = 1 if i == 2 else 1 + 2 * middle
        at = column_slot(i)

        def copy():
            return pltpu.make_async_remote_copy(
                src_ref=r.zs.at[i], dst_ref=r.zr.at[at[0]], send_sem=r.m_gz.at[0, i], recv_sem=r.m_gz.at[1, at[0]],
                device_id=to_mp(target), device_id_type=MESH,
            )

        copy().start()
        sends.append(lambda: copy().wait_send())

    def column_own():
        r.zf[...] = unit_total(MP - 1) + from_line(2)

        @pl.when(middle == 1)
        def _():
            r.zf[...] += from_line(3)

        for c in range(3):
            r.qkv_grad[c] = r.zf[:, c * CW : (c + 1) * CW]
        r.proj_grad[...] = r.zf[:, QW:].T

    def proj_total():
        total = proj_unit.total()
        for m in range(MP):
            r.fp[m] = total[:, m * CW : (m + 1) * CW]

    def dp_swap(src, dst, sem):
        def copy(k):
            return remote(src.at[dp_at(k)], dst.at[dp], sem, (k,), (DP - k,), to_dp(k))

        each(1, DP, lambda k: copy(k).start())
        sends.append(lambda: each(1, DP, lambda k: copy(k).wait_send()))
        dst[dp] = src[dp]

    def dp_wait(dst, sem):
        each(1, DP, lambda k: arrive(dst.at[dp_at(k)], sem, (k,)))

    def sum_of(ref, count):
        total = ref[0]
        for i in range(1, count):
            total = total + ref[i]
        return total

    def small_column():
        dp_wait(r.sb, r.m_s1)
        r.sc[mp] = sum_of(r.sb, DP)
        to_column(r.sc.at[mp], r.m_s2)

    def small_back():
        for k in range(1, MP):
            arrive(r.sc.at[mp_at(k)], r.m_s2, (k,))
        r.sd[dp] = sum_of(r.sc, MP)
        for k in range(1, DP):
            send(r.sd.at[dp], r.sd.at[dp], r.m_s3, (k,), (DP - k,), to_dp(k))

    def gains(grad_out, normed):
        return jnp.concatenate(
            [jnp.sum(grad_out * normed, axis=0, keepdims=True), jnp.sum(grad_out, axis=0, keepdims=True)], axis=0
        )

    if z.own_weights:
        units = [qkv_unit(i) for i in range(MP)]
        proj_unit = Unit(r.gp, r.cp, r.xp, r.ap, r.bp, r.dp_, r.m_hc, r.m_hx, ())
        r.gp[...] = proj_part.reshape(NX, IN, RB, D)
        proj_unit.start()
    else:
        r.gp[...] = proj_part
    for m in range(MP):
        r.datt[m] = nn(dbranch, proj_weight(m)).astype(BF)
    rows2 = gains(dh2, normed2)
    if z.own_weights:
        phi_part = tn(dlogits, h2)
        r.sa[...] = jnp.zeros((DP, KE, D), F32)
        for i in range(E // KE):
            r.sa[i] = phi_part[i * KE : (i + 1) * KE]
        r.sa[E // KE, 0:2, :] = rows2
        dp_swap(r.sa, r.sb, r.m_s1)
    else:
        r.phi_grad[...] = tn(dlogits, h2)

    def heads_backward(m):
        qkv, datt = r.qkv[m], r.datt[m]
        pieces = [[], [], []]
        for h in range(z.HL):
            query, key, value = head_cols(qkv, h)
            grad_h = datt[:, h * HEAD_DIM : (h + 1) * HEAD_DIM]
            probs = r.probs[m, h]
            dprobs = nt(grad_h, value)
            dscores = probs * (dprobs - jnp.sum(probs * dprobs, axis=-1, keepdims=True))
            dscores = dscores.astype(BF)
            pieces[0].append(nn(dscores, key) * scale)
            pieces[1].append(tn(dscores, query) * scale)
            pieces[2].append(tn(probs.astype(BF), grad_h))
        dqkv = jnp.concatenate(pieces[0] + pieces[1] + pieces[2], axis=1).astype(BF)
        piece = tn(r.h1[...], dqkv).astype(BF)
        if z.own_weights:
            r.gq[m] = piece.reshape(NX, IN, RB, QW)
        else:
            r.gq[m] = piece
        return dqkv

    between = {}
    if z.own_weights:
        first, second, third, last = units
        between = {0: [proj_unit.plane], 1: [first.plane], 2: [second.plane, proj_unit.forward], 3: [third.plane]}
    for i in range(MP):
        m = mp_at(orders[i] if MP == 4 else i)
        dqkv = heads_backward(m)
        if z.own_weights:
            units[i].start()
        part = nt(dqkv, weight(m))
        if i == 0:
            r.dh1[...] = part
        else:
            r.dh1[...] += part
        for step in between.get(i, []):
            step()

    normed1, inv1 = normalize(own_image(r.tin).astype(F32))
    dh1 = r.dh1[...]
    input_grad = r.dresid[...] + norm_backward(dh1, gain1, normed1, inv1)
    for m in range(MP):
        r.isend[m] = input_grad[:, m * CW : (m + 1) * CW].astype(BF)
    swap(r.isend, r.iin, r.m_ings)
    rows1 = gains(dh1, normed1)
    if z.own_weights:
        r.ta[...] = rows1
        for k in range(1, DP):
            send(r.ta, r.tb.at[dp], r.m_t1, (k,), (DP - k,), to_dp(k))
        r.tb[dp] = rows1

    if z.own_weights:
        first.forward()
        last.plane()
        second.forward()
        third.forward()
        proj_total()
        column(0)
        last.forward()
        small_column()
        column(1)
        small_back()
        dp_wait(r.tb, r.m_t1)
        r.tc[mp] = sum_of(r.tb, DP)
        to_column(r.tc.at[mp], r.m_t2)
    swap_wait(r.oin, r.m_outs)
    r.output[...] = from_images(r.oin)
    if z.own_weights:
        column(2)
        dp_wait(r.sd, r.m_s3)
        for i in range(E // KE):
            r.phi_grad[i * KE : (i + 1) * KE, :] = r.sd[i]
        column_own()
        for k in range(1, MP):
            arrive(r.tc.at[mp_at(k)], r.m_t2, (k,))
        r.norm_grad[...] = jnp.concatenate([sum_of(r.tc, MP), r.sd[E // KE, 0:2, :]], axis=0)
    else:
        r.norm_grad[...] = jnp.concatenate([rows1, rows2], axis=0)
    swap_wait(r.iin, r.m_ings)

    for wait in sends:
        wait()


def from_images(source):
    images = [source[i, 0:SEQ, :].astype(F32) for i in range(source.shape[0])]
    return jnp.concatenate(images, axis=0).T


def finish_kernel(passed, slots, dpre, hidden, dresults, iin, *refs):
    sources, (in_grad, out_grad, input_grad), rest = refs[:passed], refs[passed : passed + 3], refs[passed + 3 :]
    targets, (grads_in, grads_out, grad_t, sem, tile_sem) = rest[:passed], rest[passed:]
    copies = [pltpu.make_async_copy(a, b, sem.at[i]) for i, (a, b) in enumerate(zip(sources, targets))]
    for copy in copies:
        copy.start()
    experts, _, width = slots.shape
    tile = 256 if width % 256 == 0 else width
    count = 0
    for e in range(experts):
        for left, right, held, target in ((slots, dpre, grads_in, in_grad), (hidden, dresults, grads_out, out_grad)):
            for t in range(width // tile):
                here = pl.ds(t * tile, tile)
                held[e, here, :] = tn(left[e, :, t * tile : (t + 1) * tile], right[e])
                copy = pltpu.make_async_copy(held.at[e, here], target.at[e, here], tile_sem.at[count])
                copy.start()
                copies.append(copy)
                count += 1
    grad_t[...] = from_images(iin)
    last = pltpu.make_async_copy(grad_t, input_grad, sem.at[passed])
    last.start()
    for copy in copies + [last]:
        copy.wait()


def per_device(mesh, tokens, norm_params, w_qkv, w_proj, phi, w_in, w_out, cotangent):
    z = Sizes(mesh, tokens, w_qkv, phi, w_in)
    vmem, anyspace = pl.BlockSpec(memory_space=pltpu.VMEM), pl.BlockSpec(memory_space=pl.ANY)
    inputs = dict(
        tokens=tokens.T, norm_params=norm_params, w_qkv=w_qkv, w_proj=w_proj, phi=phi.T, cotangent=cotangent.T
    )
    specs = [vmem] * len(inputs)
    inputs.update(w_in=w_in, w_out=w_out)
    specs += [anyspace] * 2
    images = z.MP * z.DP
    outs = dict(
        output=((z.CW, z.ROWS), F32), iin=((z.MP, z.SP, z.CW), BF),
        phi_grad=((z.E, z.D), F32), norm_grad=((4, z.D), F32),
        slots=((z.EPD, images, z.D), BF), dresults=((z.EPD, images, z.D), BF),
        hidden=((z.EPD, images, z.F), BF), dpre=((z.EPD, images, z.F), BF),
    )
    if z.own_weights:
        outs.update(qkv_grad=((3, z.RB, z.CW), F32), proj_grad=((z.CW, z.RB), F32))
    else:
        outs.update(gq=((z.MP, z.D, z.QW), BF), gp=((z.D, z.D), BF))
        wall = lax.all_gather(w_qkv.astype(BF), "dp", axis=1, tiled=True)
        wall = jnp.concatenate([wall[c] for c in range(3)], axis=1)
        wpall = lax.all_gather(w_proj.T.astype(BF), "dp", axis=0, tiled=True)
        inputs.update(wall=lax.all_gather(wall, "mp"), wpall=lax.all_gather(wpall, "mp"))
        specs += [vmem] * 2
    names, scratch = scratch_of(z)
    result = pl.pallas_call(
        functools.partial(block_kernel, z, list(inputs), list(outs), names),
        out_shape=[jax.ShapeDtypeStruct(*one) for one in outs.values()],
        in_specs=specs,
        out_specs=[vmem] * len(outs),
        scratch_shapes=scratch,
        compiler_params=pltpu.CompilerParams(
            collective_id=0, has_side_effects=True, vmem_limit_bytes=62 * 2**20
        ),
        name="block",
    )(*inputs.values())
    got = dict(zip(outs, result))

    passed = ["output", "norm_grad", "phi_grad"] + (["qkv_grad", "proj_grad"] if z.own_weights else [])
    tile = 256 if z.F % 256 == 0 and z.D == z.F else z.F
    tiles = 2 * z.EPD * (z.F // tile)
    results = pl.pallas_call(
        functools.partial(finish_kernel, len(passed)),
        in_specs=[vmem] * (5 + len(passed)),
        out_specs=[anyspace] * (3 + len(passed)),
        out_shape=[
            jax.ShapeDtypeStruct((z.EPD, z.D, z.F), F32),
            jax.ShapeDtypeStruct((z.EPD, z.F, z.D), F32),
            jax.ShapeDtypeStruct((z.CW, z.ROWS), F32),
        ]
        + [jax.ShapeDtypeStruct(*outs[name]) for name in passed],
        scratch_shapes=[
            pltpu.VMEM((z.EPD, z.D, z.F), F32),
            pltpu.VMEM((z.EPD, z.F, z.D), F32),
            pltpu.VMEM((z.CW, z.ROWS), F32),
            pltpu.SemaphoreType.DMA((len(passed) + 1,)),
            pltpu.SemaphoreType.DMA((tiles,)),
        ],
        compiler_params=pltpu.CompilerParams(vmem_limit_bytes=60 * 2**20),
        name="finish",
    )(got["slots"], got["dpre"], got["hidden"], got["dresults"], got["iin"], *(got[name] for name in passed))
    in_grad, out_grad, input_grad = results[:3]
    got.update(zip(passed, results[3:]))
    output, input_grad = got["output"].T, input_grad.T
    phi_grad, norm_grad = got["phi_grad"].T, got["norm_grad"]
    if z.own_weights:
        qkv_grad, proj_grad = got["qkv_grad"], got["proj_grad"]
    else:
        phi_grad, norm_grad = lax.psum((phi_grad, norm_grad), ("dp", "mp"))
        gq = lax.psum_scatter(got["gq"].astype(F32), "mp", scatter_dimension=0, tiled=False)
        gp = lax.psum_scatter(got["gp"].astype(F32), "mp", scatter_dimension=1, tiled=True)
        gq = jnp.stack([gq[:, c * z.CW : (c + 1) * z.CW] for c in range(3)])
        qkv_grad = lax.psum_scatter(gq, "dp", scatter_dimension=1, tiled=True)
        proj_grad = lax.psum_scatter(gp, "dp", scatter_dimension=0, tiled=True).T
    return (
        output, input_grad, qkv_grad, proj_grad, in_grad, out_grad, phi_grad, norm_grad
    )


def solution(mesh):
    return jax.shard_map(
        functools.partial(per_device, mesh),
        mesh=mesh,
        in_specs=(
            P("dp", "mp"), P(), P(None, "dp", "mp"), P("mp", "dp"), P(),
            P("dp", None, "mp"), P("dp", "mp", None), P("dp", "mp"),
        ),
        out_specs=(
            P("dp", "mp"), P("dp", "mp"), P(None, "dp", "mp"), P("mp", "dp"),
            P("dp", None, "mp"), P("dp", "mp", None), P(), P(),
        ),
        check_vma=False,
    )
```

```python
import functools
import math

import jax
import jax.numpy as jnp
from jax import lax
from jax.experimental import pallas as pl
from jax.experimental.pallas import tpu as pltpu
from jax.sharding import PartitionSpec as P

HEAD_DIM = 64
SEQ = 196
EPSILON = 1e-06
MESH = pl.DeviceIdType.MESH
BF = jnp.bfloat16
F32 = jnp.float32
NEG = -1e30


def nn(a, b):
    return lax.dot_general(a, b, (((1,), (0,)), ((), ())), preferred_element_type=F32)


def nt(a, b):
    return lax.dot_general(a, b, (((1,), (1,)), ((), ())), preferred_element_type=F32)


def tn(a, b):
    return lax.dot_general(a, b, (((0,), (0,)), ((), ())), preferred_element_type=F32)


def each(low, high, body):
    if high - low <= 32:
        for i in range(low, high):
            body(i)
    else:

        def step(i, carry):
            body(i)
            return carry

        lax.fori_loop(low, high, step, 0)


def select_rows(rows, cols, source):
    row = lax.broadcasted_iota(jnp.int32, (rows, cols), 0)
    col = lax.broadcasted_iota(jnp.int32, (rows, cols), 1)
    return jnp.where(col == source(row), 1.0, 0.0).astype(BF)


def normalize(values):
    mean = jnp.mean(values, axis=-1, keepdims=True)
    centered = values - mean
    var = jnp.mean(centered * centered, axis=-1, keepdims=True)
    inv = lax.rsqrt(var + EPSILON)
    return centered * inv, inv


def norm_backward(grad, gain, normed, inv):
    scaled = grad * gain
    first = jnp.mean(scaled, axis=-1, keepdims=True)
    second = jnp.mean(scaled * normed, axis=-1, keepdims=True)
    return inv * (scaled - first - normed * second)


class Sizes:
    def __init__(self, mesh, tokens, w_qkv, phi, w_in):
        self.DP, self.MP = mesh.shape["dp"], mesh.shape["mp"]
        self.D, self.E = phi.shape
        self.CW = tokens.shape[1]
        self.RB = w_qkv.shape[1]
        self.QW = 3 * self.CW
        self.HL = self.CW // HEAD_DIM
        self.EPD = w_in.shape[0]
        self.F = w_in.shape[2]
        self.IN = 2
        self.NX = self.DP // self.IN
        self.SP = (SEQ + 15) // 16 * 16
        self.ROWS = tokens.shape[0]
        self.KE = 2 * self.EPD
        self.NS = self.DP * self.MP
        self.LC = self.D // 128
        self.Q = self.EPD * self.LC
        self.QP = (self.Q + 15) // 16 * 16
        self.GD = 8 if self.DP % 8 == 0 else self.DP
        self.GS = self.GD * self.MP
        self.own_weights = self.MP == 4 and self.NX == 4 and self.RB % 32 == 0 and self.E + 2 <= self.KE * self.DP


def scratch_of(z):
    dma = pltpu.SemaphoreType.DMA
    v = pltpu.VMEM
    DP, MP, D, CW, RB, QW, SP, NX, IN, KE = z.DP, z.MP, z.D, z.CW, z.RB, z.QW, z.SP, z.NX, z.IN, z.KE
    half = RB // 2
    items = dict(
        tsend=v((MP, SP, CW), BF), tin=v((MP, SP, CW), BF),
        csend=v((MP, SP, CW), BF), cin=v((MP, SP, CW), BF),
        osend=v((MP, SP, CW), BF), oin=v((MP, SP, CW), BF),
        isend=v((MP, SP, CW), BF),
        wf_in=v((z.EPD, D, z.F), F32), wf_out=v((z.EPD, z.F, D), F32),
        wb_in=v((z.EPD, D, z.F), BF), wb_out=v((z.EPD, z.F, D), BF),
        h1=v((SP, D), BF), qkv=v((MP, SP, QW), BF), probs=v((MP, z.HL, SP, SP), F32),
        att=v((MP, SP, CW), BF), datt=v((MP, SP, CW), BF),
        resid=v((SP, D), F32), dresid=v((SP, D), F32), dh1=v((SP, D), F32),
        slot_out=v((2, DP, z.QP, 128), BF), slot_in=v((2, z.NS, z.QP, 128), BF),
        back_out=v((2, z.NS, z.QP, 128), BF), back_in=v((2, z.NS, z.QP, 128), BF),
        pick_in=v((z.Q * z.GS, z.GS * z.QP), BF), pick_back=v((z.GS * z.QP, z.Q * z.GS), BF),
        pick_sum=v((z.LC * z.GD * z.EPD, z.GS * z.QP), BF),
    )
    items.update(
        tokens=v((CW, z.ROWS), BF), cotangent=v((CW, z.ROWS), BF), norm_params=v((4, D), F32), phi=v((z.E, D), F32),
        output=v((CW, z.ROWS), F32), slots=v((z.EPD, z.NS, D), BF), dresults=v((z.EPD, z.NS, D), BF),
        hidden=v((z.EPD, z.NS, z.F), BF), dpre=v((z.EPD, z.NS, z.F), BF),
    )
    sems = dict(
        load=(6,), store=(5,), tok=(2, MP), cot=(2, MP), outs=(2, MP), ings=(2, MP), hbm=(2,),
        slot=(2, 2), back=(2, 2),
    )
    if z.own_weights:
        items.update(
            w_qkv=v((3, RB, CW), F32), w_proj=v((CW, RB), F32),
            wall=v((MP, NX, IN, RB, D), BF),
            gq=v((MP, NX, IN, RB, QW), BF), gp=v((NX, IN, RB, D), BF),
            cq=v((MP, NX, RB, QW), BF), cp=v((NX, RB, D), BF),
            xq=v((MP, NX, RB, QW), BF), xp=v((NX, RB, D), BF),
            aq=v((MP, 4, half, QW), BF), ap=v((4, half, D), BF),
            bq=v((MP, 2, half, QW), BF), bp=v((2, half, D), BF),
            dq=v((MP, 2, half, QW), BF), dp_=v((2, half, D), BF),
            zf=v((RB, D), F32), zs=v((MP, RB, D), BF), zr=v((5, RB, D), BF), fp=v((MP, RB, CW), F32),
            sa=v((DP, KE, D), F32), sb=v((DP, KE, D), F32), sc=v((MP, KE, D), F32), sd=v((DP, KE, D), F32),
            ta=v((2, D), F32), tb=v((DP, 2, D), F32), tc=v((MP, 2, D), F32),
        )
        sems.update(
            wz=(2, 5), wx=(2, MP, 4), wc=(2, MP),
            gc=(2, MP), gx=(2, MP, 6), gz=(2, 5), hc=(2,), hx=(2, 6),
            s1=(2, DP), s2=(2, MP), s3=(2, DP), t1=(2, DP), t2=(2, MP),
        )
    names, shapes = [], []
    for name, shape in items.items():
        names.append(name)
        shapes.append(shape)
    for name, shape in sems.items():
        names.append("m_" + name)
        shapes.append(dma(shape))
    names.append("entered")
    shapes.append(pltpu.SemaphoreType.REGULAR)
    return names, shapes


class Refs:
    pass


def block_kernel(z, in_names, out_names, names, *refs):
    r = Refs()
    for name, ref in zip(in_names + out_names + names, refs):
        setattr(r, name, ref)
    DP, MP, D, CW, RB, QW, SP = z.DP, z.MP, z.D, z.CW, z.RB, z.QW, z.SP
    NX, IN, E, EPD, KE = z.NX, z.IN, z.E, z.EPD, z.KE
    half = RB // 2
    dp, mp = lax.axis_index("dp"), lax.axis_index("mp")
    xy, co = dp // IN, lax.rem(dp, IN)
    xn = xy + 1 - 2 * lax.rem(xy, 2)
    yn = lax.rem(xy + 2, NX)
    dg = lax.rem(xn + 2, NX)
    to_x, to_y, to_core = (xn * IN + co, mp), (yn * IN + co, mp), (xy * IN + 1 - co, mp)
    sends = []

    def remote(src, dst, sem, s_at, r_at, device):
        return pltpu.make_async_remote_copy(
            src_ref=src, dst_ref=dst, send_sem=sem.at[(0,) + s_at], recv_sem=sem.at[(1,) + r_at],
            device_id=device, device_id_type=MESH,
        )

    def send(*copy):
        remote(*copy).start()
        sends.append(lambda: remote(*copy).wait_send())

    def arrive(ref, sem, at):
        remote(ref, ref, sem, at, at, to_mp(1)).wait_recv()

    def mp_at(k):
        if MP != 4:
            return lax.rem(mp + k, MP)
        return 2 * lax.rem(mp // 2 + k // 2, 2) + lax.rem(mp + k, 2)

    def mp_back(k):
        return k if MP == 4 else MP - k

    def dp_at(k):
        return lax.rem(dp + k, DP)

    def to_mp(k):
        return (dp, mp_at(k))

    def to_dp(k):
        return (dp_at(k), mp)

    def to_any(k):
        if isinstance(k, int):
            return (dp_at(k // MP), lax.rem(mp + k % MP, MP))
        return (dp_at(k // MP), lax.rem(mp + lax.rem(k, MP), MP))

    barrier = pltpu.get_barrier_semaphore()
    if z.own_weights:
        for k in range(1, MP):
            pl.semaphore_signal(barrier, inc=1, device_id=to_mp(k), device_id_type=MESH)
        each(1, DP, lambda k: pl.semaphore_signal(barrier, inc=1, device_id=to_dp(k), device_id_type=MESH))
    else:
        each(1, z.NS, lambda k: pl.semaphore_signal(barrier, inc=1, device_id=to_any(k), device_id_type=MESH))

    loads, stores = {}, []
    needed = (["w_qkv", "w_proj"] if z.own_weights else []) + ["tokens", "cotangent", "norm_params", "phi"]
    for i, name in enumerate(needed):
        loads[name] = pltpu.make_async_copy(getattr(r, "hbm_" + name), getattr(r, name), r.m_load.at[i])
        loads[name].start()

    def store(name):
        copy = pltpu.make_async_copy(getattr(r, name), getattr(r, "hbm_" + name), r.m_store.at[len(stores)])
        copy.start()
        stores.append(copy)

    load_in = pltpu.make_async_copy(r.w_in, r.wf_in, r.m_hbm.at[0])
    load_out = pltpu.make_async_copy(r.w_out, r.wf_out, r.m_hbm.at[1])
    load_in.start()
    load_out.start()

    if z.own_weights:
        loads["w_qkv"].wait()
        loads["w_proj"].wait()
        r.wall[mp, xy, co] = jnp.concatenate(
            [r.w_qkv[c].astype(BF) for c in range(3)] + [r.w_proj[...].T.astype(BF)], axis=1
        )
    pl.semaphore_wait(barrier, MP - 1 + DP - 1 if z.own_weights else z.NS - 1)
    if z.own_weights:
        for k in range(1, MP):
            pl.semaphore_signal(r.entered, inc=1, device_id=to_mp(k), device_id_type=MESH)

    def to_images(source, target):
        target[...] = jnp.zeros((MP, SP, CW), BF)
        rows = source[...].T
        for i in range(MP):
            target[i, 0:SEQ, :] = rows[SEQ * i : SEQ * (i + 1)]

    def swap(src, dst, sem):
        for k in range(1, MP):
            send(src.at[mp_at(k)], dst.at[mp], sem, (k,), (mp_back(k),), to_mp(k))
        dst[mp] = src[mp]

    def swap_wait(dst, sem):
        for k in range(1, MP):
            arrive(dst.at[mp_at(k)], sem, (k,))

    def to_column(block, sem):
        for k in range(1, MP):
            send(block, block, sem, (k,), (mp_back(k),), to_mp(k))

    class Plane:
        def __init__(self, block, sem, at):
            self.block, self.sem, self.at = block, sem, at

        def copy(self, ref, way, device):
            send(ref, ref, self.sem, self.at + (way,), self.at + (way,), device)

        def start(self):
            self.copy(self.block(xy, 0, RB), 0, to_x)
            self.copy(self.block(xy, 0, RB), 1, to_y)

        def forward(self):
            arrive(self.block(xn, 0, RB), self.sem, self.at + (0,))
            self.copy(self.block(xn, 0, half), 2, to_y)
            arrive(self.block(yn, 0, RB), self.sem, self.at + (1,))
            self.copy(self.block(yn, half, half), 3, to_x)

        def wait(self):
            arrive(self.block(dg, 0, half), self.sem, self.at + (2,))
            arrive(self.block(dg, half, half), self.sem, self.at + (3,))

    middle = lax.rem((mp + 1) // 2, 2)
    slots_at = [0, 1, 2 + middle, 3 - middle]

    def column_copy(k, way, slot, target):
        block = r.wall.at[mp_at(k), xy, co]
        return remote(block, block, r.m_wz, (way,), (slot,), to_mp(target))

    def column_send(*copy):
        column_copy(*copy).start()
        sends.append(lambda: column_copy(*copy).wait_send())

    def column_pass(*copy):
        pl.when(middle == 1)(lambda: column_copy(*copy).start())
        sends.append(lambda: pl.when(middle == 1)(lambda: column_copy(*copy).wait_send()))

    def weight_plane(s):
        return Plane(lambda pos, low, rows: r.wall.at[mp_at(slots_at[s]), pos, co, pl.ds(low, rows)], r.m_wx, (s,))

    def load_expert(copy, wide, low):
        copy.wait()
        low[...] = wide[...].astype(BF)


    def make_picks():
        GS, Q, QP, LC = z.GS, z.Q, z.QP, z.LC
        r.pick_in[...] = select_rows(Q * GS, GS * QP, lambda row: (row % GS) * QP + row // GS)
        r.pick_back[...] = select_rows(
            GS * QP, Q * GS, lambda row: jnp.where(row % QP < Q, (row % QP) * GS + row // QP, -1)
        )
        shape = (LC * z.GD * EPD, GS * QP)
        row, col = (lax.broadcasted_iota(jnp.int32, shape, i) for i in range(2))
        expert, chunk = row % (z.GD * EPD), row // (z.GD * EPD)
        wanted = (col // (QP * MP) == expert // EPD) & (col % QP == (expert % EPD) * LC + chunk)
        r.pick_sum[...] = jnp.where(wanted, 1.0, 0.0).astype(BF)

    if z.own_weights:
        planes = [weight_plane(s) for s in range(MP)]

        def column_arrived(s, k, way, slot, target):
            arrive(r.wall.at[mp_at(slots_at[s]), xy, co], r.m_wz, (slots_at[s],))
            if k:
                column_pass(k, way, slot, target)
            planes[s].start()

        def plane_arrived(s):
            planes[s].wait()
            block = r.wall.at[mp_at(slots_at[s]), :, co]
            send(block, block, r.m_wc, (s,), (s,), to_core)

        column_send(0, 0, 1, 1)
        column_send(0, 1, 3, 3)
        planes[0].start()
        loads["tokens"].wait()
        to_images(r.tokens, r.tsend)
        load_expert(load_in, r.wf_in, r.wb_in)
        column_arrived(1, 1, 2, 2, 3)
        planes[0].forward()
        loads["cotangent"].wait()
        to_images(r.cotangent, r.csend)
        column_arrived(2, 3, 3, 2, 1)
        planes[1].forward()
        swap(r.tsend, r.tin, r.m_tok)
        plane_arrived(0)
        load_expert(load_out, r.wf_out, r.wb_out)
        make_picks()
        column_arrived(3, 0, 0, 0, 0)
        planes[2].forward()
        plane_arrived(1)
        planes[3].forward()
        swap(r.csend, r.cin, r.m_cot)
        plane_arrived(2)
    else:
        loads["tokens"].wait()
        to_images(r.tokens, r.tsend)
        swap(r.tsend, r.tin, r.m_tok)
        loads["cotangent"].wait()
        to_images(r.cotangent, r.csend)
        swap(r.csend, r.cin, r.m_cot)
        load_expert(load_in, r.wf_in, r.wb_in)
        load_expert(load_out, r.wf_out, r.wb_out)
        make_picks()

    swap_wait(r.tin, r.m_tok)
    loads["norm_params"].wait()
    loads["phi"].wait()
    gain1, shift1 = r.norm_params[0:1, :], r.norm_params[1:2, :]
    gain2, shift2 = r.norm_params[2:3, :], r.norm_params[3:4, :]

    def own_image(ref):
        return jnp.concatenate([ref[i] for i in range(MP)], axis=1)

    normed1, _ = normalize(own_image(r.tin).astype(F32))
    r.h1[...] = (normed1 * gain1 + shift1).astype(BF)

    scale = 1.0 / math.sqrt(HEAD_DIM)
    key_ok = lax.broadcasted_iota(jnp.int32, (1, SP), 1) < SEQ

    def weight(m):
        return r.wall[m].reshape(D, D)[:, :QW] if z.own_weights else r.wall[m]

    def proj_weight(m):
        return r.wall[m].reshape(D, D)[:, QW:] if z.own_weights else r.wpall[m]

    def head_cols(qkv, h):
        return (qkv[:, c * CW + h * HEAD_DIM : c * CW + (h + 1) * HEAD_DIM] for c in range(3))

    def heads_forward(s):
        m = mp_at(slots_at[s])
        if z.own_weights:
            arrive(r.wall.at[m, :, 1 - co], r.m_wc, (s,))
        qkv = nn(r.h1[...], weight(m)).astype(BF)
        r.qkv[m] = qkv
        if z.own_weights and s == MP - 2:
            plane_arrived(s + 1)
        attended = []
        for h in range(z.HL):
            query, key, value = head_cols(qkv, h)
            scores = jnp.where(key_ok, nt(query, key) * scale, NEG)
            top = jnp.max(scores, axis=-1, keepdims=True)
            grown = jnp.exp(scores - top)
            probs = grown / jnp.sum(grown, axis=-1, keepdims=True)
            r.probs[m, h] = probs
            attended.append(nn(probs.astype(BF), value))
        r.att[m] = jnp.concatenate(attended, axis=1).astype(BF)

    for s in range(MP):
        heads_forward(s)

    resid = own_image(r.tin).astype(F32)
    for m in range(MP):
        resid = resid + nt(r.att[m], proj_weight(m))
    r.resid[...] = resid
    normed2, inv2 = normalize(resid)
    h2 = (normed2 * gain2 + shift2).astype(BF)
    phi_low = r.phi[...].astype(BF)
    logits = nt(h2, phi_low)
    token_ok = lax.broadcasted_iota(jnp.int32, (SP, 1), 0) < SEQ
    masked = jnp.where(token_ok, logits, NEG)
    grown = jnp.exp(masked - jnp.max(masked, axis=0, keepdims=True))
    dispatch = grown / jnp.sum(grown, axis=0, keepdims=True)
    grown = jnp.exp(logits - jnp.max(logits, axis=1, keepdims=True))
    combine = grown / jnp.sum(grown, axis=1, keepdims=True)
    dispatch_low, combine_low = dispatch.astype(BF), combine.astype(BF)
    slots = tn(dispatch_low, h2).astype(BF)

    GD, GS, Q, QP, LC = z.GD, z.GS, z.Q, z.QP, z.LC
    groups = DP // GD
    here = dp * MP + mp

    def stack(rows):
        return jnp.concatenate([rows[:, c * 128 : (c + 1) * 128] for c in range(LC)], axis=0)

    def unstack(chunks):
        count = chunks.shape[0] // LC
        return jnp.concatenate([chunks[c * count : (c + 1) * count] for c in range(LC)], axis=1)

    def exchange(source, dst, kind, sem):
        def copy(k):
            device = to_any(k)
            return pltpu.make_async_remote_copy(
                src_ref=source(*device), dst_ref=dst.at[kind, here], send_sem=sem.at[0, kind],
                recv_sem=sem.at[1, kind], device_id=device, device_id_type=MESH,
            )

        each(1, z.NS, lambda k: copy(k).start())
        all_of_them = dst.at[kind, pl.ds(0, z.NS - 1)]
        sends.append(
            lambda: pltpu.make_async_remote_copy(
                src_ref=all_of_them, dst_ref=all_of_them, send_sem=sem.at[0, kind], recv_sem=sem.at[1, kind],
                device_id=to_mp(1), device_id_type=MESH,
            ).wait_send()
        )

    def exchange_wait(dst, kind, sem):
        all_of_them = dst.at[kind, pl.ds(0, z.NS - 1)]
        pltpu.make_async_remote_copy(
            src_ref=all_of_them, dst_ref=all_of_them, send_sem=sem.at[0, kind], recv_sem=sem.at[1, kind],
            device_id=to_mp(1), device_id_type=MESH,
        ).wait_recv()

    def out_row(row):
        d, q = row // QP, row % QP
        return jnp.where(q < Q, (q % LC) * (GD * EPD) + d * EPD + q // LC, -1)

    pick_out = select_rows(GD * QP, LC * GD * EPD, out_row)

    def send_slots(kind, rows):
        for g in range(groups):
            part = nn(pick_out, stack(rows[g * GD * EPD : (g + 1) * GD * EPD]))
            r.slot_out[kind, g * GD : (g + 1) * GD] = part.astype(BF).reshape(GD, QP, 128)
        exchange(lambda d, m: r.slot_out.at[kind, d], r.slot_in, kind, r.m_slot)
        r.slot_in[kind, here] = r.slot_out[kind, dp]

    if z.own_weights:
        pl.semaphore_wait(r.entered, MP - 1)
    send_slots(0, slots)
    swap_wait(r.cin, r.m_cot)
    grad = own_image(r.cin)
    send_slots(1, tn(combine_low, grad).astype(BF))

    def expert_rows(kind):
        exchange_wait(r.slot_in, kind, r.m_slot)
        found = [[] for _ in range(EPD)]
        for g in range(groups):
            got = r.slot_in[kind, g * GS : (g + 1) * GS].reshape(GS * QP, 128)
            chunks = nn(r.pick_in[...], got)
            for e in range(EPD):
                found[e].append(unstack(chunks[e * LC * GS : (e + 1) * LC * GS]).astype(BF))
        return [jnp.concatenate(one, axis=0) for one in found]

    def send_parts(kind, per_expert):
        for g in range(groups):
            rows = [stack(one[g * GS : (g + 1) * GS]).astype(BF) for one in per_expert]
            part = nn(r.pick_back[...], jnp.concatenate(rows, axis=0))
            r.back_out[kind, g * GS : (g + 1) * GS] = part.astype(BF).reshape(GS, QP, 128)
        exchange(lambda d, m: r.back_out.at[kind, d * MP + m], r.back_in, kind, r.m_back)
        r.back_in[kind, here] = r.back_out[kind, here]

    def back_rows(kind):
        exchange_wait(r.back_in, kind, r.m_back)
        found = []
        for g in range(groups):
            got = r.back_in[kind, g * GS : (g + 1) * GS].reshape(GS * QP, 128)
            found.append(unstack(nn(r.pick_sum[...], got)).astype(BF))
        return jnp.concatenate(found, axis=0)

    slopes, results_part = [], []
    for e, slots_e in enumerate(expert_rows(0)):
        pre = nn(slots_e, r.wb_in[e])
        cdf = 0.5 * (1.0 + lax.erf(pre * (1.0 / math.sqrt(2.0))))
        hidden = (pre * cdf).astype(BF)
        results_part.append(nn(hidden, r.wb_out[e]))
        slopes.append(cdf + pre * jnp.exp(-0.5 * pre * pre) * (1.0 / math.sqrt(2.0 * math.pi)))
        r.slots[e], r.hidden[e] = slots_e, hidden
    send_parts(0, results_part)
    dslots_part = []
    for e, dresults_e in enumerate(expert_rows(1)):
        dpre = (nt(dresults_e, r.wb_out[e]) * slopes[e]).astype(BF)
        dslots_part.append(nt(dpre, r.wb_in[e]))
        r.dresults[e], r.dpre[e] = dresults_e, dpre
    send_parts(1, dslots_part)
    for name in ("slots", "hidden", "dresults", "dpre"):
        store(name)
    results = back_rows(0)

    output = r.resid[...] + nn(combine_low, results)
    for m in range(MP):
        r.osend[m] = output[:, m * CW : (m + 1) * CW].astype(BF)
    swap(r.osend, r.oin, r.m_outs)
    dslots = back_rows(1)
    dcombine, ddispatch = nt(grad, results), nt(h2, dslots)
    dlogits = dispatch * (ddispatch - jnp.sum(dispatch * ddispatch, axis=0, keepdims=True))
    dlogits = dlogits + combine * (dcombine - jnp.sum(combine * dcombine, axis=1, keepdims=True))
    dlogits = dlogits.astype(BF)
    dh2 = nn(dispatch_low, dslots) + nn(dlogits, phi_low)
    dresid = grad.astype(F32) + norm_backward(dh2, gain2, normed2, inv2)
    r.dresid[...] = dresid
    dbranch = dresid.astype(BF)
    proj_part = tn(dbranch, own_image(r.att)).astype(BF)

    class Unit:
        def __init__(self, part, got, mine, first, out, second, core_sem, sem, at):
            self.part, self.got, self.mine, self.first = part, got, mine, first
            self.out, self.second, self.core_sem, self.sem, self.at = out, second, core_sem, sem, at

        def start(self):
            send(self.part.at[:, 1 - co], self.got, self.core_sem, self.at, self.at, to_core)

        def copy(self, src, dst, way, device):
            send(src, dst, self.sem, self.at + (way,), self.at + (way,), device)

        def plane(self):
            arrive(self.got, self.core_sem, self.at)
            for x in range(NX):
                self.mine[x] = (self.part[x, co].astype(F32) + self.got[x].astype(F32)).astype(BF)
            low, high = pl.ds(0, half), pl.ds(half, half)
            self.copy(self.mine.at[dg, low], self.first.at[1], 1, to_x)
            self.copy(self.mine.at[dg, high], self.first.at[3], 3, to_y)
            self.copy(self.mine.at[xn, low], self.first.at[0], 0, to_x)
            self.copy(self.mine.at[yn, high], self.first.at[2], 2, to_y)

        def added(self, x, low, index):
            arrive(self.first.at[index], self.sem, self.at + (index,))
            return self.mine[x, low : low + half, :].astype(F32) + self.first[index].astype(F32)

        def forward(self):
            self.out[0] = self.added(yn, 0, 1).astype(BF)
            self.copy(self.out.at[0], self.second.at[0], 4, to_y)
            self.out[1] = self.added(xn, half, 3).astype(BF)
            self.copy(self.out.at[1], self.second.at[1], 5, to_x)

        def total(self):
            pieces = []
            for i in range(2):
                piece = self.added(xy, i * half, 2 * i)
                arrive(self.second.at[i], self.sem, self.at + (4 + i,))
                pieces.append(piece + self.second[i].astype(F32))
            return jnp.concatenate(pieces, axis=0)

    orders = [2 + middle, 3 - middle, 1, 0]

    def qkv_unit(i):
        m = mp_at(orders[i])
        return Unit(r.gq.at[m], r.cq.at[i], r.xq.at[i], r.aq.at[i], r.bq.at[i], r.dq.at[i], r.m_gc, r.m_gx, (i,))

    def column_slot(i):
        return (i + 3 * middle,) if i < 2 else (2,)

    def from_line(index):
        arrive(r.zr.at[index], r.m_gz, (index,))
        return r.zr[index].astype(F32)

    def unit_total(i):
        return jnp.concatenate([units[i].total(), r.fp[mp_at(orders[i])]], axis=1)

    def column(i):
        r.zf[...] = unit_total(i)

        @pl.when(middle == 1)
        def _():
            r.zf[...] += from_line([0, 1, 4][i])

        r.zs[i] = r.zf[...].astype(BF)
        target = 1 if i == 2 else 1 + 2 * middle
        at = column_slot(i)

        def copy():
            return pltpu.make_async_remote_copy(
                src_ref=r.zs.at[i], dst_ref=r.zr.at[at[0]], send_sem=r.m_gz.at[0, i], recv_sem=r.m_gz.at[1, at[0]],
                device_id=to_mp(target), device_id_type=MESH,
            )

        copy().start()
        sends.append(lambda: copy().wait_send())

    def column_own():
        r.zf[...] = unit_total(MP - 1) + from_line(2)

        @pl.when(middle == 1)
        def _():
            r.zf[...] += from_line(3)

        for c in range(3):
            r.qkv_grad[c] = r.zf[:, c * CW : (c + 1) * CW]
        r.proj_grad[...] = r.zf[:, QW:].T

    def proj_total():
        total = proj_unit.total()
        for m in range(MP):
            r.fp[m] = total[:, m * CW : (m + 1) * CW]

    def dp_swap(src, dst, sem):
        def copy(k):
            return remote(src.at[dp_at(k)], dst.at[dp], sem, (k,), (DP - k,), to_dp(k))

        each(1, DP, lambda k: copy(k).start())
        sends.append(lambda: each(1, DP, lambda k: copy(k).wait_send()))
        dst[dp] = src[dp]

    def dp_wait(dst, sem):
        each(1, DP, lambda k: arrive(dst.at[dp_at(k)], sem, (k,)))

    def sum_of(ref, count):
        total = ref[0]
        for i in range(1, count):
            total = total + ref[i]
        return total

    def small_column():
        dp_wait(r.sb, r.m_s1)
        r.sc[mp] = sum_of(r.sb, DP)
        to_column(r.sc.at[mp], r.m_s2)

    def small_back():
        for k in range(1, MP):
            arrive(r.sc.at[mp_at(k)], r.m_s2, (k,))
        r.sd[dp] = sum_of(r.sc, MP)
        for k in range(1, DP):
            send(r.sd.at[dp], r.sd.at[dp], r.m_s3, (k,), (DP - k,), to_dp(k))

    def gains(grad_out, normed):
        return jnp.concatenate(
            [jnp.sum(grad_out * normed, axis=0, keepdims=True), jnp.sum(grad_out, axis=0, keepdims=True)], axis=0
        )

    if z.own_weights:
        units = [qkv_unit(i) for i in range(MP)]
        proj_unit = Unit(r.gp, r.cp, r.xp, r.ap, r.bp, r.dp_, r.m_hc, r.m_hx, ())
        r.gp[...] = proj_part.reshape(NX, IN, RB, D)
        proj_unit.start()
    else:
        r.gp[...] = proj_part
    for m in range(MP):
        r.datt[m] = nn(dbranch, proj_weight(m)).astype(BF)
    rows2 = gains(dh2, normed2)
    if z.own_weights:
        phi_part = tn(dlogits, h2)
        r.sa[...] = jnp.zeros((DP, KE, D), F32)
        for i in range(E // KE):
            r.sa[i] = phi_part[i * KE : (i + 1) * KE]
        r.sa[E // KE, 0:2, :] = rows2
        dp_swap(r.sa, r.sb, r.m_s1)
    else:
        r.phi_grad[...] = tn(dlogits, h2)

    def heads_backward(m):
        qkv, datt = r.qkv[m], r.datt[m]
        pieces = [[], [], []]
        for h in range(z.HL):
            query, key, value = head_cols(qkv, h)
            grad_h = datt[:, h * HEAD_DIM : (h + 1) * HEAD_DIM]
            probs = r.probs[m, h]
            dprobs = nt(grad_h, value)
            dscores = probs * (dprobs - jnp.sum(probs * dprobs, axis=-1, keepdims=True))
            dscores = dscores.astype(BF)
            pieces[0].append(nn(dscores, key) * scale)
            pieces[1].append(tn(dscores, query) * scale)
            pieces[2].append(tn(probs.astype(BF), grad_h))
        dqkv = jnp.concatenate(pieces[0] + pieces[1] + pieces[2], axis=1).astype(BF)
        piece = tn(r.h1[...], dqkv).astype(BF)
        if z.own_weights:
            r.gq[m] = piece.reshape(NX, IN, RB, QW)
        else:
            r.gq[m] = piece
        return dqkv

    between = {}
    if z.own_weights:
        first, second, third, last = units
        between = {0: [proj_unit.plane], 1: [first.plane], 2: [second.plane, proj_unit.forward], 3: [third.plane]}
    for i in range(MP):
        m = mp_at(orders[i] if MP == 4 else i)
        dqkv = heads_backward(m)
        if z.own_weights:
            units[i].start()
        part = nt(dqkv, weight(m))
        if i == 0:
            r.dh1[...] = part
        else:
            r.dh1[...] += part
        for step in between.get(i, []):
            step()

    normed1, inv1 = normalize(own_image(r.tin).astype(F32))
    dh1 = r.dh1[...]
    input_grad = r.dresid[...] + norm_backward(dh1, gain1, normed1, inv1)
    for m in range(MP):
        r.isend[m] = input_grad[:, m * CW : (m + 1) * CW].astype(BF)
    swap(r.isend, r.iin, r.m_ings)
    rows1 = gains(dh1, normed1)
    if z.own_weights:
        r.ta[...] = rows1
        for k in range(1, DP):
            send(r.ta, r.tb.at[dp], r.m_t1, (k,), (DP - k,), to_dp(k))
        r.tb[dp] = rows1

    if z.own_weights:
        first.forward()
        last.plane()
        second.forward()
        third.forward()
        proj_total()
        column(0)
        last.forward()
        small_column()
        column(1)
        small_back()
    if z.own_weights:
        column(2)
        dp_wait(r.tb, r.m_t1)
        r.tc[mp] = sum_of(r.tb, DP)
        to_column(r.tc.at[mp], r.m_t2)
    swap_wait(r.oin, r.m_outs)
    r.output[...] = from_images(r.oin)
    store("output")
    if z.own_weights:
        dp_wait(r.sd, r.m_s3)
        for i in range(E // KE):
            r.phi_grad[i * KE : (i + 1) * KE, :] = r.sd[i]
        column_own()
        for k in range(1, MP):
            arrive(r.tc.at[mp_at(k)], r.m_t2, (k,))
        r.norm_grad[...] = jnp.concatenate([sum_of(r.tc, MP), r.sd[E // KE, 0:2, :]], axis=0)
    else:
        r.norm_grad[...] = jnp.concatenate([rows1, rows2], axis=0)
    swap_wait(r.iin, r.m_ings)

    for wait in sends:
        wait()
    for copy in stores:
        copy.wait()


def from_images(source):
    images = [source[i, 0:SEQ, :].astype(F32) for i in range(source.shape[0])]
    return jnp.concatenate(images, axis=0).T


def finish_kernel(passed, slots, dpre, hidden, dresults, iin, *refs):
    sources, (in_grad, out_grad, input_grad), rest = refs[:passed], refs[passed : passed + 3], refs[passed + 3 :]
    targets, (grads_in, grads_out, grad_t, sem, tile_sem) = rest[:passed], rest[passed:]
    copies = [pltpu.make_async_copy(a, b, sem.at[i]) for i, (a, b) in enumerate(zip(sources, targets))]
    for copy in copies:
        copy.start()
    experts, _, width = slots.shape
    tile = 256 if width % 256 == 0 else width
    count = 0
    for e in range(experts):
        for left, right, held, target in ((slots, dpre, grads_in, in_grad), (hidden, dresults, grads_out, out_grad)):
            for t in range(width // tile):
                here = pl.ds(t * tile, tile)
                held[e, here, :] = tn(left[e, :, t * tile : (t + 1) * tile], right[e])
                copy = pltpu.make_async_copy(held.at[e, here], target.at[e, here], tile_sem.at[count])
                copy.start()
                copies.append(copy)
                count += 1
    grad_t[...] = from_images(iin)
    last = pltpu.make_async_copy(grad_t, input_grad, sem.at[passed])
    last.start()
    for copy in copies + [last]:
        copy.wait()


def per_device(mesh, tokens, norm_params, w_qkv, w_proj, phi, w_in, w_out, cotangent):
    z = Sizes(mesh, tokens, w_qkv, phi, w_in)
    vmem, anyspace = pl.BlockSpec(memory_space=pltpu.VMEM), pl.BlockSpec(memory_space=pl.ANY)
    inputs = dict(
        tokens=tokens.T, norm_params=norm_params, w_qkv=w_qkv, w_proj=w_proj, phi=phi.T, cotangent=cotangent.T
    )
    inputs = {"hbm_" + name: value for name, value in inputs.items()}
    specs = [anyspace] * len(inputs)
    inputs.update(w_in=w_in, w_out=w_out)
    specs += [anyspace] * 2
    images = z.MP * z.DP
    outs = dict(
        hbm_output=((z.CW, z.ROWS), F32), iin=((z.MP, z.SP, z.CW), BF),
        phi_grad=((z.E, z.D), F32), norm_grad=((4, z.D), F32),
        hbm_slots=((z.EPD, images, z.D), BF), hbm_dresults=((z.EPD, images, z.D), BF),
        hbm_hidden=((z.EPD, images, z.F), BF), hbm_dpre=((z.EPD, images, z.F), BF),
    )
    if z.own_weights:
        outs.update(qkv_grad=((3, z.RB, z.CW), F32), proj_grad=((z.CW, z.RB), F32))
    else:
        outs.update(gq=((z.MP, z.D, z.QW), BF), gp=((z.D, z.D), BF))
        wall = lax.all_gather(w_qkv.astype(BF), "dp", axis=1, tiled=True)
        wall = jnp.concatenate([wall[c] for c in range(3)], axis=1)
        wpall = lax.all_gather(w_proj.T.astype(BF), "dp", axis=0, tiled=True)
        inputs.update(wall=lax.all_gather(wall, "mp"), wpall=lax.all_gather(wpall, "mp"))
        specs += [vmem] * 2
    names, scratch = scratch_of(z)
    result = pl.pallas_call(
        functools.partial(block_kernel, z, list(inputs), list(outs), names),
        out_shape=[jax.ShapeDtypeStruct(*one) for one in outs.values()],
        in_specs=specs,
        out_specs=[anyspace if name.startswith("hbm_") else vmem for name in outs],
        scratch_shapes=scratch,
        compiler_params=pltpu.CompilerParams(
            collective_id=0, has_side_effects=True, vmem_limit_bytes=62 * 2**20
        ),
        name="block",
    )(*inputs.values())
    outs = {name.removeprefix("hbm_"): one for name, one in outs.items()}
    got = dict(zip(outs, result))

    passed = ["output", "norm_grad", "phi_grad"] + (["qkv_grad", "proj_grad"] if z.own_weights else [])
    tile = 256 if z.F % 256 == 0 and z.D == z.F else z.F
    tiles = 2 * z.EPD * (z.F // tile)
    results = pl.pallas_call(
        functools.partial(finish_kernel, len(passed)),
        in_specs=[vmem] * (5 + len(passed)),
        out_specs=[anyspace] * (3 + len(passed)),
        out_shape=[
            jax.ShapeDtypeStruct((z.EPD, z.D, z.F), F32),
            jax.ShapeDtypeStruct((z.EPD, z.F, z.D), F32),
            jax.ShapeDtypeStruct((z.CW, z.ROWS), F32),
        ]
        + [jax.ShapeDtypeStruct(*outs[name]) for name in passed],
        scratch_shapes=[
            pltpu.VMEM((z.EPD, z.D, z.F), F32),
            pltpu.VMEM((z.EPD, z.F, z.D), F32),
            pltpu.VMEM((z.CW, z.ROWS), F32),
            pltpu.SemaphoreType.DMA((len(passed) + 1,)),
            pltpu.SemaphoreType.DMA((tiles,)),
        ],
        compiler_params=pltpu.CompilerParams(vmem_limit_bytes=60 * 2**20),
        name="finish",
    )(got["slots"], got["dpre"], got["hidden"], got["dresults"], got["iin"], *(got[name] for name in passed))
    in_grad, out_grad, input_grad = results[:3]
    got.update(zip(passed, results[3:]))
    output, input_grad = got["output"].T, input_grad.T
    phi_grad, norm_grad = got["phi_grad"].T, got["norm_grad"]
    if z.own_weights:
        qkv_grad, proj_grad = got["qkv_grad"], got["proj_grad"]
    else:
        phi_grad, norm_grad = lax.psum((phi_grad, norm_grad), ("dp", "mp"))
        gq = lax.psum_scatter(got["gq"].astype(F32), "mp", scatter_dimension=0, tiled=False)
        gp = lax.psum_scatter(got["gp"].astype(F32), "mp", scatter_dimension=1, tiled=True)
        gq = jnp.stack([gq[:, c * z.CW : (c + 1) * z.CW] for c in range(3)])
        qkv_grad = lax.psum_scatter(gq, "dp", scatter_dimension=1, tiled=True)
        proj_grad = lax.psum_scatter(gp, "dp", scatter_dimension=0, tiled=True).T
    return (
        output, input_grad, qkv_grad, proj_grad, in_grad, out_grad, phi_grad, norm_grad
    )


def solution(mesh):
    return jax.shard_map(
        functools.partial(per_device, mesh),
        mesh=mesh,
        in_specs=(
            P("dp", "mp"), P(), P(None, "dp", "mp"), P("mp", "dp"), P(),
            P("dp", None, "mp"), P("dp", "mp", None), P("dp", "mp"),
        ),
        out_specs=(
            P("dp", "mp"), P("dp", "mp"), P(None, "dp", "mp"), P("mp", "dp"),
            P("dp", None, "mp"), P("dp", "mp", None), P(), P(),
        ),
        check_vma=False,
    )
```

```python
import functools
import math

import jax
import jax.numpy as jnp
from jax import lax
from jax.experimental import pallas as pl
from jax.experimental.pallas import tpu as pltpu
from jax.sharding import PartitionSpec as P

HEAD_DIM = 64
SEQ = 196
EPSILON = 1e-06
MESH = pl.DeviceIdType.MESH
BF = jnp.bfloat16
F32 = jnp.float32
NEG = -1e30


def nn(a, b):
    return lax.dot_general(a, b, (((1,), (0,)), ((), ())), preferred_element_type=F32)


def nt(a, b):
    return lax.dot_general(a, b, (((1,), (1,)), ((), ())), preferred_element_type=F32)


def tn(a, b):
    return lax.dot_general(a, b, (((0,), (0,)), ((), ())), preferred_element_type=F32)


def each(low, high, body):
    if high - low <= 32:
        for i in range(low, high):
            body(i)
    else:

        def step(i, carry):
            body(i)
            return carry

        lax.fori_loop(low, high, step, 0)


def select_rows(rows, cols, source):
    row = lax.broadcasted_iota(jnp.int32, (rows, cols), 0)
    col = lax.broadcasted_iota(jnp.int32, (rows, cols), 1)
    return jnp.where(col == source(row), 1.0, 0.0).astype(BF)


def normalize(values):
    mean = jnp.mean(values, axis=-1, keepdims=True)
    centered = values - mean
    var = jnp.mean(centered * centered, axis=-1, keepdims=True)
    inv = lax.rsqrt(var + EPSILON)
    return centered * inv, inv


def norm_backward(grad, gain, normed, inv):
    scaled = grad * gain
    first = jnp.mean(scaled, axis=-1, keepdims=True)
    second = jnp.mean(scaled * normed, axis=-1, keepdims=True)
    return inv * (scaled - first - normed * second)


class Sizes:
    def __init__(self, mesh, tokens, w_qkv, phi, w_in):
        self.DP, self.MP = mesh.shape["dp"], mesh.shape["mp"]
        self.D, self.E = phi.shape
        self.CW = tokens.shape[1]
        self.RB = w_qkv.shape[1]
        self.QW = 3 * self.CW
        self.HL = self.CW // HEAD_DIM
        self.EPD = w_in.shape[0]
        self.F = w_in.shape[2]
        self.IN = 2
        self.NX = self.DP // self.IN
        self.SP = (SEQ + 15) // 16 * 16
        self.ROWS = tokens.shape[0]
        self.KE = 2 * self.EPD
        self.NS = self.DP * self.MP
        self.LC = self.D // 128
        self.Q = self.EPD * self.LC
        self.QP = (self.Q + 15) // 16 * 16
        self.GD = 8 if self.DP % 8 == 0 else self.DP
        self.GS = self.GD * self.MP
        self.own_weights = self.MP == 4 and self.NX == 4 and self.RB % 32 == 0 and self.E + 2 <= self.KE * self.DP


def scratch_of(z):
    dma = pltpu.SemaphoreType.DMA
    v = pltpu.VMEM
    DP, MP, D, CW, RB, QW, SP, NX, IN, KE = z.DP, z.MP, z.D, z.CW, z.RB, z.QW, z.SP, z.NX, z.IN, z.KE
    half = RB // 2
    items = dict(
        tsend=v((MP, SP, CW), BF), tin=v((MP, SP, CW), BF),
        csend=v((MP, SP, CW), BF), cin=v((MP, SP, CW), BF),
        osend=v((MP, SP, CW), BF), oin=v((MP, SP, CW), BF),
        isend=v((MP, SP, CW), BF),
        wf_in=v((z.EPD, D, z.F), F32), wf_out=v((z.EPD, z.F, D), F32),
        wb_in=v((z.EPD, D, z.F), BF), wb_out=v((z.EPD, z.F, D), BF),
        h1=v((SP, D), BF), qkv=v((MP, SP, QW), BF), probs=v((MP, z.HL, SP, SP), F32),
        att=v((MP, SP, CW), BF), datt=v((MP, SP, CW), BF),
        resid=v((SP, D), F32), dresid=v((SP, D), F32), dh1=v((SP, D), F32),
        slot_out=v((2, DP, z.QP, 128), BF), slot_in=v((2, z.NS, z.QP, 128), BF),
        back_out=v((2, z.NS, z.QP, 128), BF), back_in=v((2, z.NS, z.QP, 128), BF),
        pick_in=v((z.Q * z.GS, z.GS * z.QP), BF), pick_back=v((z.GS * z.QP, z.Q * z.GS), BF),
        pick_sum=v((z.LC * z.GD * z.EPD, z.GS * z.QP), BF),
    )
    items.update(
        tokens=v((CW, z.ROWS), BF), cotangent=v((CW, z.ROWS), BF), norm_params=v((4, D), F32), phi=v((z.E, D), F32),
        output=v((CW, z.ROWS), F32), slots=v((z.EPD, z.NS, D), BF), dresults=v((z.EPD, z.NS, D), BF),
        hidden=v((z.EPD, z.NS, z.F), BF), dpre=v((z.EPD, z.NS, z.F), BF),
    )
    sems = dict(
        load=(6,), store=(5,), tok=(2, MP), cot=(2, MP), outs=(2, MP), ings=(2, MP), hbm=(2,),
        slot=(2, 2), back=(2, 2),
    )
    if z.own_weights:
        items.update(
            w_qkv=v((3, RB, CW), F32), w_proj=v((CW, RB), F32),
            wall=v((MP, NX, IN, RB, D), BF),
            gq=v((MP, NX, IN, RB, QW), BF), gp=v((NX, IN, RB, D), BF),
            cq=v((MP, NX, RB, QW), BF), cp=v((NX, RB, D), BF),
            xq=v((MP, NX, RB, QW), BF), xp=v((NX, RB, D), BF),
            aq=v((MP, 4, half, QW), BF), ap=v((4, half, D), BF),
            bq=v((MP, 2, half, QW), BF), bp=v((2, half, D), BF),
            dq=v((MP, 2, half, QW), BF), dp_=v((2, half, D), BF),
            zf=v((RB, D), F32), zs=v((MP, RB, D), BF), zr=v((5, RB, D), BF), fp=v((MP, RB, CW), F32),
            sa=v((DP, KE, D), F32), sb=v((DP, KE, D), F32), sc=v((MP, KE, D), F32), sd=v((DP, KE, D), F32),
            ta=v((2, D), F32), tb=v((DP, 2, D), F32), tc=v((MP, 2, D), F32),
        )
        sems.update(
            wz=(2, 5), wx=(2, MP, 4), wc=(2, MP),
            gc=(2, MP), gx=(2, MP, 6), gz=(2, 5), hc=(2,), hx=(2, 6),
            s1=(2, DP), s2=(2, MP), s3=(2, DP), t1=(2, DP), t2=(2, MP),
        )
    names, shapes = [], []
    for name, shape in items.items():
        names.append(name)
        shapes.append(shape)
    for name, shape in sems.items():
        names.append("m_" + name)
        shapes.append(dma(shape))
    names.append("entered")
    shapes.append(pltpu.SemaphoreType.REGULAR)
    return names, shapes


class Refs:
    pass


def block_kernel(z, in_names, out_names, names, *refs):
    r = Refs()
    for name, ref in zip(in_names + out_names + names, refs):
        setattr(r, name, ref)
    DP, MP, D, CW, RB, QW, SP = z.DP, z.MP, z.D, z.CW, z.RB, z.QW, z.SP
    NX, IN, E, EPD, KE = z.NX, z.IN, z.E, z.EPD, z.KE
    half = RB // 2
    dp, mp = lax.axis_index("dp"), lax.axis_index("mp")
    xy, co = dp // IN, lax.rem(dp, IN)
    xn = xy + 1 - 2 * lax.rem(xy, 2)
    yn = lax.rem(xy + 2, NX)
    dg = lax.rem(xn + 2, NX)
    to_x, to_y, to_core = (xn * IN + co, mp), (yn * IN + co, mp), (xy * IN + 1 - co, mp)
    sends = []

    def remote(src, dst, sem, s_at, r_at, device):
        return pltpu.make_async_remote_copy(
            src_ref=src, dst_ref=dst, send_sem=sem.at[(0,) + s_at], recv_sem=sem.at[(1,) + r_at],
            device_id=device, device_id_type=MESH,
        )

    def send(*copy):
        remote(*copy).start()
        sends.append(lambda: remote(*copy).wait_send())

    def arrive(ref, sem, at):
        remote(ref, ref, sem, at, at, to_mp(1)).wait_recv()

    def mp_at(k):
        if MP != 4:
            return lax.rem(mp + k, MP)
        return 2 * lax.rem(mp // 2 + k // 2, 2) + lax.rem(mp + k, 2)

    def mp_back(k):
        return k if MP == 4 else MP - k

    def dp_at(k):
        return lax.rem(dp + k, DP)

    def to_mp(k):
        return (dp, mp_at(k))

    def to_dp(k):
        return (dp_at(k), mp)

    def to_any(k):
        if isinstance(k, int):
            return (dp_at(k // MP), lax.rem(mp + k % MP, MP))
        return (dp_at(k // MP), lax.rem(mp + lax.rem(k, MP), MP))

    barrier = pltpu.get_barrier_semaphore()
    if z.own_weights:
        for k in range(1, MP):
            pl.semaphore_signal(barrier, inc=1, device_id=to_mp(k), device_id_type=MESH)
        each(1, DP, lambda k: pl.semaphore_signal(barrier, inc=1, device_id=to_dp(k), device_id_type=MESH))
    else:
        each(1, z.NS, lambda k: pl.semaphore_signal(barrier, inc=1, device_id=to_any(k), device_id_type=MESH))

    loads, stores = {}, []
    needed = (["w_qkv", "w_proj"] if z.own_weights else []) + ["tokens", "cotangent", "norm_params", "phi"]
    for i, name in enumerate(needed):
        loads[name] = pltpu.make_async_copy(getattr(r, "hbm_" + name), getattr(r, name), r.m_load.at[i])
        loads[name].start()

    def store(name):
        copy = pltpu.make_async_copy(getattr(r, name), getattr(r, "hbm_" + name), r.m_store.at[len(stores)])
        copy.start()
        stores.append(copy)

    load_in = pltpu.make_async_copy(r.w_in, r.wf_in, r.m_hbm.at[0])
    load_out = pltpu.make_async_copy(r.w_out, r.wf_out, r.m_hbm.at[1])
    load_in.start()
    load_out.start()

    if z.own_weights:
        loads["w_qkv"].wait()
        loads["w_proj"].wait()
        r.wall[mp, xy, co] = jnp.concatenate(
            [r.w_qkv[c].astype(BF) for c in range(3)] + [r.w_proj[...].T.astype(BF)], axis=1
        )
    pl.semaphore_wait(barrier, MP - 1 + DP - 1 if z.own_weights else z.NS - 1)
    if z.own_weights:
        for k in range(1, MP):
            pl.semaphore_signal(r.entered, inc=1, device_id=to_mp(k), device_id_type=MESH)

    def to_images(source, target):
        target[...] = jnp.zeros((MP, SP, CW), BF)
        rows = source[...].T
        for i in range(MP):
            target[i, 0:SEQ, :] = rows[SEQ * i : SEQ * (i + 1)]

    def swap(src, dst, sem):
        for k in range(1, MP):
            send(src.at[mp_at(k)], dst.at[mp], sem, (k,), (mp_back(k),), to_mp(k))
        dst[mp] = src[mp]

    def swap_wait(dst, sem):
        for k in range(1, MP):
            arrive(dst.at[mp_at(k)], sem, (k,))

    def to_column(block, sem):
        for k in range(1, MP):
            send(block, block, sem, (k,), (mp_back(k),), to_mp(k))

    class Plane:
        def __init__(self, block, sem, at):
            self.block, self.sem, self.at = block, sem, at

        def copy(self, ref, way, device):
            send(ref, ref, self.sem, self.at + (way,), self.at + (way,), device)

        def start(self):
            self.copy(self.block(xy, 0, RB), 0, to_x)
            self.copy(self.block(xy, 0, RB), 1, to_y)

        def forward(self):
            arrive(self.block(xn, 0, RB), self.sem, self.at + (0,))
            self.copy(self.block(xn, 0, half), 2, to_y)
            arrive(self.block(yn, 0, RB), self.sem, self.at + (1,))
            self.copy(self.block(yn, half, half), 3, to_x)

        def wait(self):
            arrive(self.block(dg, 0, half), self.sem, self.at + (2,))
            arrive(self.block(dg, half, half), self.sem, self.at + (3,))

    middle = lax.rem((mp + 1) // 2, 2)
    slots_at = [0, 1, 2 + middle, 3 - middle]

    def column_copy(k, way, slot, target):
        block = r.wall.at[mp_at(k), xy, co]
        return remote(block, block, r.m_wz, (way,), (slot,), to_mp(target))

    def column_send(*copy):
        column_copy(*copy).start()
        sends.append(lambda: column_copy(*copy).wait_send())

    def column_pass(*copy):
        pl.when(middle == 1)(lambda: column_copy(*copy).start())
        sends.append(lambda: pl.when(middle == 1)(lambda: column_copy(*copy).wait_send()))

    def weight_plane(s):
        return Plane(lambda pos, low, rows: r.wall.at[mp_at(slots_at[s]), pos, co, pl.ds(low, rows)], r.m_wx, (s,))

    def load_expert(copy, wide, low):
        copy.wait()
        low[...] = wide[...].astype(BF)


    def make_picks():
        GS, Q, QP, LC = z.GS, z.Q, z.QP, z.LC
        r.pick_in[...] = select_rows(Q * GS, GS * QP, lambda row: (row % GS) * QP + row // GS)
        r.pick_back[...] = select_rows(
            GS * QP, Q * GS, lambda row: jnp.where(row % QP < Q, (row % QP) * GS + row // QP, -1)
        )
        shape = (LC * z.GD * EPD, GS * QP)
        row, col = (lax.broadcasted_iota(jnp.int32, shape, i) for i in range(2))
        expert, chunk = row % (z.GD * EPD), row // (z.GD * EPD)
        wanted = (col // (QP * MP) == expert // EPD) & (col % QP == (expert % EPD) * LC + chunk)
        r.pick_sum[...] = jnp.where(wanted, 1.0, 0.0).astype(BF)

    if z.own_weights:
        planes = [weight_plane(s) for s in range(MP)]

        def column_arrived(s, k, way, slot, target):
            arrive(r.wall.at[mp_at(slots_at[s]), xy, co], r.m_wz, (slots_at[s],))
            if k:
                column_pass(k, way, slot, target)
            planes[s].start()

        def plane_arrived(s):
            planes[s].wait()
            block = r.wall.at[mp_at(slots_at[s]), :, co]
            send(block, block, r.m_wc, (s,), (s,), to_core)

        column_send(0, 0, 1, 1)
        column_send(0, 1, 3, 3)
        planes[0].start()
        loads["tokens"].wait()
        to_images(r.tokens, r.tsend)
        load_expert(load_in, r.wf_in, r.wb_in)
        column_arrived(1, 1, 2, 2, 3)
        planes[0].forward()
        loads["cotangent"].wait()
        to_images(r.cotangent, r.csend)
        column_arrived(2, 3, 3, 2, 1)
        planes[1].forward()
        swap(r.tsend, r.tin, r.m_tok)
        plane_arrived(0)
        load_expert(load_out, r.wf_out, r.wb_out)
        make_picks()
        column_arrived(3, 0, 0, 0, 0)
        planes[2].forward()
        plane_arrived(1)
        planes[3].forward()
        swap(r.csend, r.cin, r.m_cot)
        plane_arrived(2)
    else:
        loads["tokens"].wait()
        to_images(r.tokens, r.tsend)
        swap(r.tsend, r.tin, r.m_tok)
        loads["cotangent"].wait()
        to_images(r.cotangent, r.csend)
        swap(r.csend, r.cin, r.m_cot)
        load_expert(load_in, r.wf_in, r.wb_in)
        load_expert(load_out, r.wf_out, r.wb_out)
        make_picks()

    swap_wait(r.tin, r.m_tok)
    loads["norm_params"].wait()
    loads["phi"].wait()
    gain1, shift1 = r.norm_params[0:1, :], r.norm_params[1:2, :]
    gain2, shift2 = r.norm_params[2:3, :], r.norm_params[3:4, :]

    def own_image(ref):
        return jnp.concatenate([ref[i] for i in range(MP)], axis=1)

    normed1, _ = normalize(own_image(r.tin).astype(F32))
    r.h1[...] = (normed1 * gain1 + shift1).astype(BF)

    scale = 1.0 / math.sqrt(HEAD_DIM)
    key_ok = lax.broadcasted_iota(jnp.int32, (1, SP), 1) < SEQ

    def weight(m):
        return r.wall[m].reshape(D, D)[:, :QW] if z.own_weights else r.wall[m]

    def proj_weight(m):
        return r.wall[m].reshape(D, D)[:, QW:] if z.own_weights else r.wpall[m]

    def head_cols(qkv, h):
        return (qkv[:, c * CW + h * HEAD_DIM : c * CW + (h + 1) * HEAD_DIM] for c in range(3))

    def heads_forward(s):
        m = mp_at(slots_at[s])
        if z.own_weights:
            arrive(r.wall.at[m, :, 1 - co], r.m_wc, (s,))
        qkv = nn(r.h1[...], weight(m)).astype(BF)
        r.qkv[m] = qkv
        if z.own_weights and s == MP - 3:
            plane_arrived(MP - 1)
        attended = []
        for h in range(z.HL):
            query, key, value = head_cols(qkv, h)
            scores = jnp.where(key_ok, nt(query, key) * scale, NEG)
            top = jnp.max(scores, axis=-1, keepdims=True)
            grown = jnp.exp(scores - top)
            probs = grown / jnp.sum(grown, axis=-1, keepdims=True)
            r.probs[m, h] = probs
            attended.append(nn(probs.astype(BF), value))
        r.att[m] = jnp.concatenate(attended, axis=1).astype(BF)

    for s in range(MP):
        heads_forward(s)

    resid = own_image(r.tin).astype(F32)
    for m in range(MP):
        resid = resid + nt(r.att[m], proj_weight(m))
    r.resid[...] = resid
    normed2, inv2 = normalize(resid)
    h2 = (normed2 * gain2 + shift2).astype(BF)
    phi_low = r.phi[...].astype(BF)
    logits = nt(h2, phi_low)
    token_ok = lax.broadcasted_iota(jnp.int32, (SP, 1), 0) < SEQ
    masked = jnp.where(token_ok, logits, NEG)
    grown = jnp.exp(masked - jnp.max(masked, axis=0, keepdims=True))
    dispatch = grown / jnp.sum(grown, axis=0, keepdims=True)
    grown = jnp.exp(logits - jnp.max(logits, axis=1, keepdims=True))
    combine = grown / jnp.sum(grown, axis=1, keepdims=True)
    dispatch_low, combine_low = dispatch.astype(BF), combine.astype(BF)
    slots = tn(dispatch_low, h2).astype(BF)

    GD, GS, Q, QP, LC = z.GD, z.GS, z.Q, z.QP, z.LC
    groups = DP // GD
    here = dp * MP + mp

    def stack(rows):
        return jnp.concatenate([rows[:, c * 128 : (c + 1) * 128] for c in range(LC)], axis=0)

    def unstack(chunks):
        count = chunks.shape[0] // LC
        return jnp.concatenate([chunks[c * count : (c + 1) * count] for c in range(LC)], axis=1)

    def exchange(source, dst, kind, sem):
        def copy(k):
            device = to_any(k)
            return pltpu.make_async_remote_copy(
                src_ref=source(*device), dst_ref=dst.at[kind, here], send_sem=sem.at[0, kind],
                recv_sem=sem.at[1, kind], device_id=device, device_id_type=MESH,
            )

        each(1, z.NS, lambda k: copy(k).start())
        all_of_them = dst.at[kind, pl.ds(0, z.NS - 1)]
        sends.append(
            lambda: pltpu.make_async_remote_copy(
                src_ref=all_of_them, dst_ref=all_of_them, send_sem=sem.at[0, kind], recv_sem=sem.at[1, kind],
                device_id=to_mp(1), device_id_type=MESH,
            ).wait_send()
        )

    def exchange_wait(dst, kind, sem):
        all_of_them = dst.at[kind, pl.ds(0, z.NS - 1)]
        pltpu.make_async_remote_copy(
            src_ref=all_of_them, dst_ref=all_of_them, send_sem=sem.at[0, kind], recv_sem=sem.at[1, kind],
            device_id=to_mp(1), device_id_type=MESH,
        ).wait_recv()

    def out_row(row):
        d, q = row // QP, row % QP
        return jnp.where(q < Q, (q % LC) * (GD * EPD) + d * EPD + q // LC, -1)

    pick_out = select_rows(GD * QP, LC * GD * EPD, out_row)

    def send_slots(kind, rows):
        for g in range(groups):
            part = nn(pick_out, stack(rows[g * GD * EPD : (g + 1) * GD * EPD]))
            r.slot_out[kind, g * GD : (g + 1) * GD] = part.astype(BF).reshape(GD, QP, 128)
        exchange(lambda d, m: r.slot_out.at[kind, d], r.slot_in, kind, r.m_slot)
        r.slot_in[kind, here] = r.slot_out[kind, dp]

    if z.own_weights:
        pl.semaphore_wait(r.entered, MP - 1)
    send_slots(0, slots)
    swap_wait(r.cin, r.m_cot)
    grad = own_image(r.cin)
    send_slots(1, tn(combine_low, grad).astype(BF))

    def expert_rows(kind):
        exchange_wait(r.slot_in, kind, r.m_slot)
        found = [[] for _ in range(EPD)]
        for g in range(groups):
            got = r.slot_in[kind, g * GS : (g + 1) * GS].reshape(GS * QP, 128)
            chunks = nn(r.pick_in[...], got)
            for e in range(EPD):
                found[e].append(unstack(chunks[e * LC * GS : (e + 1) * LC * GS]).astype(BF))
        return [jnp.concatenate(one, axis=0) for one in found]

    def send_parts(kind, per_expert):
        for g in range(groups):
            rows = [stack(one[g * GS : (g + 1) * GS]).astype(BF) for one in per_expert]
            part = nn(r.pick_back[...], jnp.concatenate(rows, axis=0))
            r.back_out[kind, g * GS : (g + 1) * GS] = part.astype(BF).reshape(GS, QP, 128)
        exchange(lambda d, m: r.back_out.at[kind, d * MP + m], r.back_in, kind, r.m_back)
        r.back_in[kind, here] = r.back_out[kind, here]

    def back_rows(kind):
        exchange_wait(r.back_in, kind, r.m_back)
        found = []
        for g in range(groups):
            got = r.back_in[kind, g * GS : (g + 1) * GS].reshape(GS * QP, 128)
            found.append(unstack(nn(r.pick_sum[...], got)).astype(BF))
        return jnp.concatenate(found, axis=0)

    slopes, results_part = [], []
    for e, slots_e in enumerate(expert_rows(0)):
        pre = nn(slots_e, r.wb_in[e])
        cdf = 0.5 * (1.0 + lax.erf(pre * (1.0 / math.sqrt(2.0))))
        hidden = (pre * cdf).astype(BF)
        results_part.append(nn(hidden, r.wb_out[e]))
        slopes.append(cdf + pre * jnp.exp(-0.5 * pre * pre) * (1.0 / math.sqrt(2.0 * math.pi)))
        r.slots[e], r.hidden[e] = slots_e, hidden
    send_parts(0, results_part)
    dslots_part = []
    for e, dresults_e in enumerate(expert_rows(1)):
        dpre = (nt(dresults_e, r.wb_out[e]) * slopes[e]).astype(BF)
        dslots_part.append(nt(dpre, r.wb_in[e]))
        r.dresults[e], r.dpre[e] = dresults_e, dpre
    send_parts(1, dslots_part)
    for name in ("slots", "hidden", "dresults", "dpre"):
        store(name)
    results = back_rows(0)

    output = r.resid[...] + nn(combine_low, results)
    for m in range(MP):
        r.osend[m] = output[:, m * CW : (m + 1) * CW].astype(BF)
    swap(r.osend, r.oin, r.m_outs)
    dslots = back_rows(1)
    dcombine, ddispatch = nt(grad, results), nt(h2, dslots)
    dlogits = dispatch * (ddispatch - jnp.sum(dispatch * ddispatch, axis=0, keepdims=True))
    dlogits = dlogits + combine * (dcombine - jnp.sum(combine * dcombine, axis=1, keepdims=True))
    dlogits = dlogits.astype(BF)
    dh2 = nn(dispatch_low, dslots) + nn(dlogits, phi_low)
    dresid = grad.astype(F32) + norm_backward(dh2, gain2, normed2, inv2)
    r.dresid[...] = dresid
    dbranch = dresid.astype(BF)
    proj_part = tn(dbranch, own_image(r.att)).astype(BF)

    class Unit:
        def __init__(self, part, got, mine, first, out, second, core_sem, sem, at):
            self.part, self.got, self.mine, self.first = part, got, mine, first
            self.out, self.second, self.core_sem, self.sem, self.at = out, second, core_sem, sem, at

        def start(self):
            send(self.part.at[:, 1 - co], self.got, self.core_sem, self.at, self.at, to_core)

        def copy(self, src, dst, way, device):
            send(src, dst, self.sem, self.at + (way,), self.at + (way,), device)

        def plane(self):
            arrive(self.got, self.core_sem, self.at)
            for x in range(NX):
                self.mine[x] = (self.part[x, co].astype(F32) + self.got[x].astype(F32)).astype(BF)
            low, high = pl.ds(0, half), pl.ds(half, half)
            self.copy(self.mine.at[dg, low], self.first.at[1], 1, to_x)
            self.copy(self.mine.at[dg, high], self.first.at[3], 3, to_y)
            self.copy(self.mine.at[xn, low], self.first.at[0], 0, to_x)
            self.copy(self.mine.at[yn, high], self.first.at[2], 2, to_y)

        def added(self, x, low, index):
            arrive(self.first.at[index], self.sem, self.at + (index,))
            return self.mine[x, low : low + half, :].astype(F32) + self.first[index].astype(F32)

        def forward(self):
            self.out[0] = self.added(yn, 0, 1).astype(BF)
            self.copy(self.out.at[0], self.second.at[0], 4, to_y)
            self.out[1] = self.added(xn, half, 3).astype(BF)
            self.copy(self.out.at[1], self.second.at[1], 5, to_x)

        def total(self):
            pieces = []
            for i in range(2):
                piece = self.added(xy, i * half, 2 * i)
                arrive(self.second.at[i], self.sem, self.at + (4 + i,))
                pieces.append(piece + self.second[i].astype(F32))
            return jnp.concatenate(pieces, axis=0)

    orders = [2 + middle, 3 - middle, 1, 0]

    def qkv_unit(i):
        m = mp_at(orders[i])
        return Unit(r.gq.at[m], r.cq.at[i], r.xq.at[i], r.aq.at[i], r.bq.at[i], r.dq.at[i], r.m_gc, r.m_gx, (i,))

    def column_slot(i):
        return (i + 3 * middle,) if i < 2 else (2,)

    def from_line(index):
        arrive(r.zr.at[index], r.m_gz, (index,))
        return r.zr[index].astype(F32)

    def unit_total(i):
        return jnp.concatenate([units[i].total(), r.fp[mp_at(orders[i])]], axis=1)

    def column(i):
        r.zf[...] = unit_total(i)

        @pl.when(middle == 1)
        def _():
            r.zf[...] += from_line([0, 1, 4][i])

        r.zs[i] = r.zf[...].astype(BF)
        target = 1 if i == 2 else 1 + 2 * middle
        at = column_slot(i)

        def copy():
            return pltpu.make_async_remote_copy(
                src_ref=r.zs.at[i], dst_ref=r.zr.at[at[0]], send_sem=r.m_gz.at[0, i], recv_sem=r.m_gz.at[1, at[0]],
                device_id=to_mp(target), device_id_type=MESH,
            )

        copy().start()
        sends.append(lambda: copy().wait_send())

    def column_own():
        r.zf[...] = unit_total(MP - 1) + from_line(2)

        @pl.when(middle == 1)
        def _():
            r.zf[...] += from_line(3)

        for c in range(3):
            r.qkv_grad[c] = r.zf[:, c * CW : (c + 1) * CW]
        r.proj_grad[...] = r.zf[:, QW:].T

    def proj_total():
        total = proj_unit.total()
        for m in range(MP):
            r.fp[m] = total[:, m * CW : (m + 1) * CW]

    def dp_swap(src, dst, sem):
        def copy(k):
            return remote(src.at[dp_at(k)], dst.at[dp], sem, (k,), (DP - k,), to_dp(k))

        each(1, DP, lambda k: copy(k).start())
        sends.append(lambda: each(1, DP, lambda k: copy(k).wait_send()))
        dst[dp] = src[dp]

    def dp_wait(dst, sem):
        each(1, DP, lambda k: arrive(dst.at[dp_at(k)], sem, (k,)))

    def sum_of(ref, count):
        total = ref[0]
        for i in range(1, count):
            total = total + ref[i]
        return total

    def small_column():
        dp_wait(r.sb, r.m_s1)
        r.sc[mp] = sum_of(r.sb, DP)
        to_column(r.sc.at[mp], r.m_s2)

    def small_back():
        for k in range(1, MP):
            arrive(r.sc.at[mp_at(k)], r.m_s2, (k,))
        r.sd[dp] = sum_of(r.sc, MP)
        for k in range(1, DP):
            send(r.sd.at[dp], r.sd.at[dp], r.m_s3, (k,), (DP - k,), to_dp(k))

    def gains(grad_out, normed):
        return jnp.concatenate(
            [jnp.sum(grad_out * normed, axis=0, keepdims=True), jnp.sum(grad_out, axis=0, keepdims=True)], axis=0
        )

    if z.own_weights:
        units = [qkv_unit(i) for i in range(MP)]
        proj_unit = Unit(r.gp, r.cp, r.xp, r.ap, r.bp, r.dp_, r.m_hc, r.m_hx, ())
        r.gp[...] = proj_part.reshape(NX, IN, RB, D)
        proj_unit.start()
    else:
        r.gp[...] = proj_part
    for m in range(MP):
        r.datt[m] = nn(dbranch, proj_weight(m)).astype(BF)
    rows2 = gains(dh2, normed2)
    if z.own_weights:
        phi_part = tn(dlogits, h2)
        r.sa[...] = jnp.zeros((DP, KE, D), F32)
        for i in range(E // KE):
            r.sa[i] = phi_part[i * KE : (i + 1) * KE]
        r.sa[E // KE, 0:2, :] = rows2
        dp_swap(r.sa, r.sb, r.m_s1)
    else:
        r.phi_grad[...] = tn(dlogits, h2)

    def heads_backward(m):
        qkv, datt = r.qkv[m], r.datt[m]
        pieces = [[], [], []]
        for h in range(z.HL):
            query, key, value = head_cols(qkv, h)
            grad_h = datt[:, h * HEAD_DIM : (h + 1) * HEAD_DIM]
            probs = r.probs[m, h]
            dprobs = nt(grad_h, value)
            dscores = probs * (dprobs - jnp.sum(probs * dprobs, axis=-1, keepdims=True))
            dscores = dscores.astype(BF)
            pieces[0].append(nn(dscores, key) * scale)
            pieces[1].append(tn(dscores, query) * scale)
            pieces[2].append(tn(probs.astype(BF), grad_h))
        dqkv = jnp.concatenate(pieces[0] + pieces[1] + pieces[2], axis=1).astype(BF)
        piece = tn(r.h1[...], dqkv).astype(BF)
        if z.own_weights:
            r.gq[m] = piece.reshape(NX, IN, RB, QW)
        else:
            r.gq[m] = piece
        return dqkv

    between = {}
    if z.own_weights:
        first, second, third, last = units
        between = {0: [proj_unit.plane], 1: [first.plane], 2: [second.plane, proj_unit.forward], 3: [third.plane]}
    for i in range(MP):
        m = mp_at(orders[i] if MP == 4 else i)
        dqkv = heads_backward(m)
        if z.own_weights:
            units[i].start()
        part = nt(dqkv, weight(m))
        if i == 0:
            r.dh1[...] = part
        else:
            r.dh1[...] += part
        for step in between.get(i, []):
            step()

    normed1, inv1 = normalize(own_image(r.tin).astype(F32))
    dh1 = r.dh1[...]
    input_grad = r.dresid[...] + norm_backward(dh1, gain1, normed1, inv1)
    for m in range(MP):
        r.isend[m] = input_grad[:, m * CW : (m + 1) * CW].astype(BF)
    swap(r.isend, r.iin, r.m_ings)
    rows1 = gains(dh1, normed1)
    if z.own_weights:
        r.ta[...] = rows1
        for k in range(1, DP):
            send(r.ta, r.tb.at[dp], r.m_t1, (k,), (DP - k,), to_dp(k))
        r.tb[dp] = rows1

    if z.own_weights:
        first.forward()
        last.plane()
        second.forward()
        third.forward()
        proj_total()
        column(0)
        last.forward()
        small_column()
        column(1)
        small_back()
    if z.own_weights:
        column(2)
        dp_wait(r.tb, r.m_t1)
        r.tc[mp] = sum_of(r.tb, DP)
        to_column(r.tc.at[mp], r.m_t2)
    swap_wait(r.oin, r.m_outs)
    r.output[...] = from_images(r.oin)
    store("output")
    if z.own_weights:
        dp_wait(r.sd, r.m_s3)
        for i in range(E // KE):
            r.phi_grad[i * KE : (i + 1) * KE, :] = r.sd[i]
        column_own()
        for k in range(1, MP):
            arrive(r.tc.at[mp_at(k)], r.m_t2, (k,))
        r.norm_grad[...] = jnp.concatenate([sum_of(r.tc, MP), r.sd[E // KE, 0:2, :]], axis=0)
    else:
        r.norm_grad[...] = jnp.concatenate([rows1, rows2], axis=0)
    swap_wait(r.iin, r.m_ings)

    for wait in sends:
        wait()
    for copy in stores:
        copy.wait()


def from_images(source):
    images = [source[i, 0:SEQ, :].astype(F32) for i in range(source.shape[0])]
    return jnp.concatenate(images, axis=0).T


def finish_kernel(passed, slots, dpre, hidden, dresults, iin, *refs):
    sources, (in_grad, out_grad, input_grad), rest = refs[:passed], refs[passed : passed + 3], refs[passed + 3 :]
    targets, (grads_in, grads_out, grad_t, sem, tile_sem) = rest[:passed], rest[passed:]
    copies = [pltpu.make_async_copy(a, b, sem.at[i]) for i, (a, b) in enumerate(zip(sources, targets))]
    for copy in copies:
        copy.start()
    experts, _, width = slots.shape
    tile = 256 if width % 256 == 0 else width
    count = 0
    for e in range(experts):
        for left, right, held, target in ((slots, dpre, grads_in, in_grad), (hidden, dresults, grads_out, out_grad)):
            for t in range(width // tile):
                here = pl.ds(t * tile, tile)
                held[e, here, :] = tn(left[e, :, t * tile : (t + 1) * tile], right[e])
                copy = pltpu.make_async_copy(held.at[e, here], target.at[e, here], tile_sem.at[count])
                copy.start()
                copies.append(copy)
                count += 1
    grad_t[...] = from_images(iin)
    last = pltpu.make_async_copy(grad_t, input_grad, sem.at[passed])
    last.start()
    for copy in copies + [last]:
        copy.wait()


def per_device(mesh, tokens, norm_params, w_qkv, w_proj, phi, w_in, w_out, cotangent):
    z = Sizes(mesh, tokens, w_qkv, phi, w_in)
    vmem, anyspace = pl.BlockSpec(memory_space=pltpu.VMEM), pl.BlockSpec(memory_space=pl.ANY)
    inputs = dict(
        tokens=tokens.T, norm_params=norm_params, w_qkv=w_qkv, w_proj=w_proj, phi=phi.T, cotangent=cotangent.T
    )
    inputs = {"hbm_" + name: value for name, value in inputs.items()}
    specs = [anyspace] * len(inputs)
    inputs.update(w_in=w_in, w_out=w_out)
    specs += [anyspace] * 2
    images = z.MP * z.DP
    outs = dict(
        hbm_output=((z.CW, z.ROWS), F32), iin=((z.MP, z.SP, z.CW), BF),
        phi_grad=((z.E, z.D), F32), norm_grad=((4, z.D), F32),
        hbm_slots=((z.EPD, images, z.D), BF), hbm_dresults=((z.EPD, images, z.D), BF),
        hbm_hidden=((z.EPD, images, z.F), BF), hbm_dpre=((z.EPD, images, z.F), BF),
    )
    if z.own_weights:
        outs.update(qkv_grad=((3, z.RB, z.CW), F32), proj_grad=((z.CW, z.RB), F32))
    else:
        outs.update(gq=((z.MP, z.D, z.QW), BF), gp=((z.D, z.D), BF))
        wall = lax.all_gather(w_qkv.astype(BF), "dp", axis=1, tiled=True)
        wall = jnp.concatenate([wall[c] for c in range(3)], axis=1)
        wpall = lax.all_gather(w_proj.T.astype(BF), "dp", axis=0, tiled=True)
        inputs.update(wall=lax.all_gather(wall, "mp"), wpall=lax.all_gather(wpall, "mp"))
        specs += [vmem] * 2
    names, scratch = scratch_of(z)
    result = pl.pallas_call(
        functools.partial(block_kernel, z, list(inputs), list(outs), names),
        out_shape=[jax.ShapeDtypeStruct(*one) for one in outs.values()],
        in_specs=specs,
        out_specs=[anyspace if name.startswith("hbm_") else vmem for name in outs],
        scratch_shapes=scratch,
        compiler_params=pltpu.CompilerParams(
            collective_id=0, has_side_effects=True, vmem_limit_bytes=62 * 2**20
        ),
        name="block",
    )(*inputs.values())
    outs = {name.removeprefix("hbm_"): one for name, one in outs.items()}
    got = dict(zip(outs, result))

    passed = ["output", "norm_grad", "phi_grad"] + (["qkv_grad", "proj_grad"] if z.own_weights else [])
    tile = 256 if z.F % 256 == 0 and z.D == z.F else z.F
    tiles = 2 * z.EPD * (z.F // tile)
    results = pl.pallas_call(
        functools.partial(finish_kernel, len(passed)),
        in_specs=[vmem] * (5 + len(passed)),
        out_specs=[anyspace] * (3 + len(passed)),
        out_shape=[
            jax.ShapeDtypeStruct((z.EPD, z.D, z.F), F32),
            jax.ShapeDtypeStruct((z.EPD, z.F, z.D), F32),
            jax.ShapeDtypeStruct((z.CW, z.ROWS), F32),
        ]
        + [jax.ShapeDtypeStruct(*outs[name]) for name in passed],
        scratch_shapes=[
            pltpu.VMEM((z.EPD, z.D, z.F), F32),
            pltpu.VMEM((z.EPD, z.F, z.D), F32),
            pltpu.VMEM((z.CW, z.ROWS), F32),
            pltpu.SemaphoreType.DMA((len(passed) + 1,)),
            pltpu.SemaphoreType.DMA((tiles,)),
        ],
        compiler_params=pltpu.CompilerParams(vmem_limit_bytes=60 * 2**20),
        name="finish",
    )(got["slots"], got["dpre"], got["hidden"], got["dresults"], got["iin"], *(got[name] for name in passed))
    in_grad, out_grad, input_grad = results[:3]
    got.update(zip(passed, results[3:]))
    output, input_grad = got["output"].T, input_grad.T
    phi_grad, norm_grad = got["phi_grad"].T, got["norm_grad"]
    if z.own_weights:
        qkv_grad, proj_grad = got["qkv_grad"], got["proj_grad"]
    else:
        phi_grad, norm_grad = lax.psum((phi_grad, norm_grad), ("dp", "mp"))
        gq = lax.psum_scatter(got["gq"].astype(F32), "mp", scatter_dimension=0, tiled=False)
        gp = lax.psum_scatter(got["gp"].astype(F32), "mp", scatter_dimension=1, tiled=True)
        gq = jnp.stack([gq[:, c * z.CW : (c + 1) * z.CW] for c in range(3)])
        qkv_grad = lax.psum_scatter(gq, "dp", scatter_dimension=1, tiled=True)
        proj_grad = lax.psum_scatter(gp, "dp", scatter_dimension=0, tiled=True).T
    return (
        output, input_grad, qkv_grad, proj_grad, in_grad, out_grad, phi_grad, norm_grad
    )


def solution(mesh):
    return jax.shard_map(
        functools.partial(per_device, mesh),
        mesh=mesh,
        in_specs=(
            P("dp", "mp"), P(), P(None, "dp", "mp"), P("mp", "dp"), P(),
            P("dp", None, "mp"), P("dp", "mp", None), P("dp", "mp"),
        ),
        out_specs=(
            P("dp", "mp"), P("dp", "mp"), P(None, "dp", "mp"), P("mp", "dp"),
            P("dp", None, "mp"), P("dp", "mp", None), P(), P(),
        ),
        check_vma=False,
    )
```
